128 devices in a mesh: loop: 8 (over x_hi, z), rep: 8 (over y, x_lo), sec: 2 (over core).
Axes of the slice: x: 4 (x_hi: 2, x_lo: 2; x = x_hi * 2 + x_lo), y: 4, z: 4, core: 2. Of those that a mesh axis runs over, the one named last changes fastest.
Arguments:
- student: bfloat16 [12288, 1024], P(('loop', 'rep'), 'sec'), may hold values from -6 to 6
- teacher: bfloat16 [12288, 4096], P(('loop', 'rep'), 'sec'), may hold values from -6 to 6
Outputs:
- student_grad: float32 [12288, 1024], P(('loop', 'rep'), 'sec')
The draws below stay inside these ranges and needn't reach their ends.
All inputs are finite; a program needn't handle non-finite values.
Results may differ from the reference program's by a relative error of at most 0.022.
Values may be sent and summed in bfloat16 or wider, within the bound.
No kernel may reach another device: no remote copies, remote signals or barrier semaphores. Data moves between devices by JAX's collectives and lax.ppermute only.
A program may use at most 128 MiB of HBM per device.

```python
import math
import jax
import jax.numpy as jnp
from jax import lax

DS = 1024
DT = 4096
BLOCK = 1536
PASSAGES = 12288
N_LOOP = 8


def shard_levels(own_key, shape, pieces, smallest, top_value):
    gain = 1.0
    for dim, shards_of in pieces:
        draws = jax.random.uniform(jax.random.fold_in(jax.random.fold_in(own_key, 6), dim), (shards_of,), jnp.float32, smallest / len(pieces), top_value / len(pieces))
        gain = gain * jnp.repeat(jnp.exp(draws), shape[dim] // shards_of).reshape((-1,) + (1,) * (len(shape) - 1 - dim))
    return gain


def gaussian(rng, extent, spread, reach, cuts=(), held_as=jnp.bfloat16):
    gain = shard_levels(rng, extent, cuts, -0.22, 0.18) if cuts else 1.0
    array = jax.random.normal(rng, extent, jnp.float32) * spread * gain
    return jnp.minimum(jnp.maximum(array, -reach), reach).astype(held_as)


def setup_inputs(seed: int = 0) -> dict:
    splits = jax.random.split(jax.random.key(seed), 3)
    student = gaussian(splits[0], (PASSAGES, DS), 1.0, 6.0, ((0, 64), (1, 2)))
    teacher = gaussian(splits[1], (PASSAGES, DT), 1.0, 6.0, ((0, 64), (1, 2)))
    return {"student": student, "teacher": teacher}


def reference(student, teacher):
    eps = 1e-06
    s32 = student.astype(jnp.float32)
    t32 = teacher.astype(jnp.float32)
    ssq_s = lax.optimization_barrier(jnp.sum(s32 * s32, axis=1)) + eps
    ssq_t = lax.optimization_barrier(jnp.sum(t32 * t32, axis=1)) + eps
    inv_s = lax.rsqrt(ssq_s)
    norm_s = (s32 * inv_s[:, None]).astype(jnp.bfloat16)
    norm_t = (t32 * lax.rsqrt(ssq_t)[:, None]).astype(jnp.bfloat16)
    coef = 32.0 * DS / math.sqrt(PASSAGES)
    blocks_s = norm_s.reshape(N_LOOP, BLOCK, DS)
    blocks_t = norm_t.reshape(N_LOOP, BLOCK, DT)

    def one_block(pair):
        rows_s, rows_t = pair
        first = jnp.dot(rows_s, norm_s.T, preferred_element_type=jnp.float32)
        second = jnp.dot(rows_t, norm_t.T, preferred_element_type=jnp.float32)
        mismatch = (first - second).astype(jnp.bfloat16)
        return coef * jnp.dot(mismatch, norm_s, preferred_element_type=jnp.float32)
    grad_n = lax.map(one_block, (blocks_s, blocks_t)).reshape(PASSAGES, DS)
    norm_f = norm_s.astype(jnp.float32)
    inner = lax.optimization_barrier(jnp.sum(grad_n * norm_f, axis=1))
    return (grad_n - inner[:, None] * norm_f) * inv_s[:, None]
```

```python
import itertools

import jax
import jax.numpy as jnp
from jax import lax
from jax.sharding import PartitionSpec as P

AXES = ("loop", "rep", "sec")
X, Y, Z = 0, 1, 2
SIZE = 4
GATHER = (Y, X)
FIRST = (Z, Y)
SECOND = (X, Z)


def index_of(chip, core):
    x, y, z = chip
    return (((x // 2) * SIZE + z) * 8 + y * 2 + x % 2) * 2 + core


def shifted(array, axis_of_core, by):
    pairs = []
    for chip in itertools.product(range(SIZE), repeat=3):
        for core in range(2):
            target = list(chip)
            axis = axis_of_core[core]
            target[axis] = (target[axis] + by) % SIZE
            pairs.append((index_of(chip, core), index_of(target, core)))
    return lax.ppermute(array, AXES, pairs)


def other_core(array):
    return lax.ppermute(array, "sec", [(0, 1), (1, 0)])


def place_along(axis_of_core):
    loop, rep, core = (lax.axis_index(name) for name in AXES)
    place = ((loop // SIZE) * 2 + rep % 2, rep // 2, loop % SIZE)
    return jnp.where(core == 0, place[axis_of_core[0]], place[axis_of_core[1]])


def block(array, which, size, axis):
    return lax.dynamic_slice_in_dim(array, which * size, size, axis)


def reduce_scattered(array, axis_of_core):
    place = place_along(axis_of_core)
    size = array.shape[0] // SIZE
    total = block(array, place, size, 0)
    for by in (1, 3, 2):
        part = block(array, (place + by) % SIZE, size, 0).astype(jnp.bfloat16)
        total = total + shifted(part, axis_of_core, by).astype(jnp.float32)
    return total


def all_gathered(array, axis_of_core):
    place = place_along(axis_of_core)
    parts = [array] + [shifted(array, axis_of_core, -by) for by in (1, 2, 3)]
    around = jnp.concatenate(parts + parts, axis=0)
    size = array.shape[0]
    return lax.dynamic_slice_in_dim(around, ((SIZE - place) % SIZE) * size, SIZE * size, 0)


def cross(left, right):
    return lax.dot_general(
        left, right, (((0,), (0,)), ((), ())), preferred_element_type=jnp.float32
    )


def body(student, teacher):
    eps = 1e-06
    rows, half = student.shape
    wide = teacher.shape[1]
    width = 2 * half
    groups = lax.axis_size("loop") * lax.axis_size("rep")
    passages = rows * groups
    coef = 32.0 * width / (passages**0.5)
    level = passages / width
    s_own, t_own = student.astype(jnp.float32), teacher.astype(jnp.float32)
    s_far, t_far = (other_core(a).astype(jnp.float32) for a in (student, teacher))

    def inverse(own, far):
        total = jnp.sum(own * own, axis=1) + jnp.sum(far * far, axis=1)
        return lax.rsqrt(total + eps)[:, None]

    inv_s, inv_t = inverse(s_own, s_far), inverse(t_own, t_far)
    norm_s, norm_sf = ((a * inv_s).astype(jnp.bfloat16) for a in (s_own, s_far))
    norm_t, norm_tf = ((a * inv_t).astype(jnp.bfloat16) for a in (t_own, t_far))

    place = place_along(GATHER)
    ss, ts = half // SIZE, wide // SIZE

    def features(by):
        which = (place + by) % SIZE
        pieces = [block(a, which, ss, 1) for a in (norm_s, norm_sf)]
        pieces += [block(a, which, ts, 1) for a in (norm_t, norm_tf)]
        return jnp.concatenate(pieces + [norm_s], axis=1)

    packs = [features(0)] + [shifted(features(by), GATHER, by) for by in (1, 2, 3)]
    pack = jnp.concatenate(packs, axis=0)
    feats = 2 * (ss + ts)
    left, right = pack[:, :feats], pack[:, feats:]
    product = cross(left, right)
    row = lax.broadcasted_iota(jnp.int32, (2 * ss, half), 0)
    col = lax.broadcasted_iota(jnp.int32, (2 * ss, half), 1)
    on_diagonal = (row < ss) & (col == row + place * ss)
    share = level * SIZE / groups
    gram = jnp.concatenate(
        [product[: 2 * ss] - jnp.where(on_diagonal, share, 0.0), -product[2 * ss :]], axis=0
    )
    piece = reduce_scattered(reduce_scattered(gram, FIRST), SECOND).astype(jnp.bfloat16)
    weights = all_gathered(all_gathered(piece, SECOND), FIRST)
    partial = jnp.dot(left, weights, preferred_element_type=jnp.float32)
    norm_f = norm_s.astype(jnp.float32)
    grad_n = partial[:rows] + level * norm_f
    for by in (1, 2, 3):
        sent = partial[by * rows : (by + 1) * rows].astype(jnp.bfloat16)
        grad_n = grad_n + shifted(sent, GATHER, -by).astype(jnp.float32)
    grad_n = coef * grad_n
    inner = jnp.sum(grad_n * norm_f, axis=1)
    inner = inner + other_core(inner)
    return (grad_n - inner[:, None] * norm_f) * inv_s


def solution(mesh):
    placed = (P(("loop", "rep"), "sec"), P(("loop", "rep"), "sec"))
    return jax.shard_map(
        body, mesh=mesh, in_specs=placed, out_specs=P(("loop", "rep"), "sec"), check_vma=False
    )
```

```python
import functools
import itertools

import jax
import jax.numpy as jnp
from jax import lax
from jax.experimental import pallas as pl
from jax.experimental.pallas import tpu as pltpu
from jax.sharding import PartitionSpec as P

AXES = ("loop", "rep", "sec")
X, Y, Z = 0, 1, 2
SIZE = 4
GATHER = (Y, X)
FIRST = (Z, Y)
SECOND = (X, Z)
STRIP = 16
PARAMS = pltpu.CompilerParams(vmem_limit_bytes=40 * 1024 * 1024)
SCALAR = pl.BlockSpec(memory_space=pltpu.SMEM)
WHOLE = pl.BlockSpec(memory_space=pltpu.VMEM)


def index_of(chip, core):
    x, y, z = chip
    return (((x // 2) * SIZE + z) * 8 + y * 2 + x % 2) * 2 + core


def shifted(array, axis_of_core, by):
    pairs = []
    for chip in itertools.product(range(SIZE), repeat=3):
        for core in range(2):
            target = list(chip)
            axis = axis_of_core[core]
            target[axis] = (target[axis] + by) % SIZE
            pairs.append((index_of(chip, core), index_of(target, core)))
    return lax.ppermute(array, AXES, pairs)


def other_core(array):
    return lax.ppermute(array, "sec", [(0, 1), (1, 0)])


def place_along(axis_of_core):
    loop, rep, core = (lax.axis_index(name) for name in AXES)
    place = ((loop // SIZE) * 2 + rep % 2, rep // 2, loop % SIZE)
    return jnp.where(core == 0, place[axis_of_core[0]], place[axis_of_core[1]])


def pack_kernel(places, s_own, s_far, t_own, t_far, pack0, pack1, pack2, pack3, inv_out):
    packs = (pack0, pack1, pack2, pack3)
    rows, half = s_own.shape
    wide = t_own.shape[1]
    ss, ts = half // SIZE, wide // SIZE
    feats = 2 * (ss + ts)

    def inverse(own, far, at):
        a, b = own[at, :].astype(jnp.float32), far[at, :].astype(jnp.float32)
        total = jnp.sum(a * a, axis=1, keepdims=True) + jnp.sum(b * b, axis=1, keepdims=True)
        return lax.rsqrt(total + 1e-06)

    @pl.loop(0, rows // STRIP)
    def _(strip):
        at = pl.ds(pl.multiple_of(strip * STRIP, STRIP), STRIP)
        inv_s, inv_t = inverse(s_own, s_far, at), inverse(t_own, t_far, at)
        inv_out[at, :] = inv_s
        norm = (s_own[at, :].astype(jnp.float32) * inv_s).astype(jnp.bfloat16)
        for by in range(SIZE):
            which = lax.rem(places[0] + by, SIZE)
            pack = packs[by]
            start = 0
            for ref, size, inv in (
                (s_own, ss, inv_s),
                (s_far, ss, inv_s),
                (t_own, ts, inv_t),
                (t_far, ts, inv_t),
            ):
                piece = ref[at, pl.ds(pl.multiple_of(which * size, size), size)]
                pack[at, pl.ds(start, size)] = (piece.astype(jnp.float32) * inv).astype(
                    jnp.bfloat16
                )
                start += size
            pack[at, pl.ds(feats, half)] = norm


def gram_kernel(
    share, places, pack0, pack1, pack2, pack3, own, send1, send2, send3, whole, product
):
    rows = pack0.shape[0]
    half = product.shape[0]
    feats = product.shape[1]
    ss = half // SIZE
    for k, pack in enumerate((pack0, pack1, pack2, pack3)):
        whole[pl.ds(k * rows, rows), :] = pack[...]
    product[...] = lax.dot_general(
        whole[:, pl.ds(feats, half)],
        whole[:, pl.ds(0, feats)],
        (((0,), (0,)), ((), ())),
        preferred_element_type=jnp.float32,
    )
    diagonal = pl.ds(pl.multiple_of(places[0] * ss, ss), ss)
    row = lax.broadcasted_iota(jnp.int32, (ss, ss), 0)
    col = lax.broadcasted_iota(jnp.int32, (ss, ss), 1)
    product[diagonal, pl.ds(0, ss)] -= jnp.where(row == col, share, 0.0)
    for by, out in enumerate((own, send1, send2, send3)):
        which = lax.rem(places[1] + by, SIZE)
        block = pl.ds(pl.multiple_of(which * ss, ss), ss)
        out[:, pl.ds(0, 2 * ss)] = product[block, pl.ds(0, 2 * ss)].astype(out.dtype)
        out[:, pl.ds(2 * ss, feats - 2 * ss)] = -product[
            block, pl.ds(2 * ss, feats - 2 * ss)
        ].astype(out.dtype)


def apply_kernel(
    places, pack0, pack1, pack2, pack3, piece0, piece1, piece2, piece3, own, send1, send2, send3, weights
):
    ss, feats = piece0.shape
    for by, piece in enumerate((piece0, piece1, piece2, piece3)):
        which = lax.rem(places[1] + SIZE - by, SIZE)
        weights[pl.ds(pl.multiple_of(which * ss, ss), ss), :] = piece[...]
    for pack, out in ((pack0, own), (pack1, send1), (pack2, send2), (pack3, send3)):
        out[...] = lax.dot_general(
            pack[:, pl.ds(0, feats)],
            weights[...],
            (((1,), (1,)), ((), ())),
            preferred_element_type=jnp.float32,
        ).astype(out.dtype)


def shapes(*described):
    return [jax.ShapeDtypeStruct(shape, dtype) for shape, dtype in described]


def body(student, teacher):
    rows, half = student.shape
    wide = teacher.shape[1]
    width = 2 * half
    groups = lax.axis_size("loop") * lax.axis_size("rep")
    passages = rows * groups
    coef = 32.0 * width / (passages**0.5)
    level = passages / width
    ss = half // SIZE
    feats = width // SIZE + 2 * wide // SIZE
    bf16, f32 = jnp.bfloat16, jnp.float32
    places = jnp.stack([place_along(GATHER), place_along(FIRST)]).astype(jnp.int32)

    t_far, s_far = other_core(teacher), other_core(student)
    *packs, inv_s = pl.pallas_call(
        pack_kernel,
        out_shape=shapes(*[((rows, feats + half), bf16)] * SIZE, ((rows, 1), f32)),
        in_specs=[SCALAR] + [WHOLE] * 4,
        out_specs=[WHOLE] * 5,
        compiler_params=PARAMS,
        name="pack",
    )(places, student, s_far, teacher, t_far)
    arrived = [packs[0]] + [shifted(packs[by], GATHER, by) for by in (1, 2, 3)]

    own, *sends = pl.pallas_call(
        functools.partial(gram_kernel, level * SIZE / groups),
        out_shape=shapes(((ss, feats), f32), *[((ss, feats), bf16)] * 3),
        in_specs=[SCALAR] + [WHOLE] * 4,
        out_specs=[WHOLE] * 4,
        scratch_shapes=[
            pltpu.VMEM((SIZE * rows, feats + half), bf16),
            pltpu.VMEM((half, feats), f32),
        ],
        compiler_params=PARAMS,
        name="gram",
    )(places, *arrived)
    total = own
    for by in (1, 2, 3):
        total = total + shifted(sends[by - 1], FIRST, by).astype(f32)
    shared = total.astype(bf16)
    for by in (1, 2, 3):
        total = total + shifted(shared, SECOND, by).astype(f32)
    piece = total.astype(bf16)
    pieces = [piece] + [shifted(piece, FIRST, by) for by in (1, 2, 3)]

    grad_n, *parts = pl.pallas_call(
        apply_kernel,
        out_shape=shapes(((rows, half), f32), *[((rows, half), bf16)] * 3),
        in_specs=[SCALAR] + [WHOLE] * 8,
        out_specs=[WHOLE] * 4,
        scratch_shapes=[pltpu.VMEM((half, feats), bf16)],
        compiler_params=PARAMS,
        name="apply",
    )(places, *arrived, *pieces)
    norm_f = packs[0][:, feats:].astype(f32)
    grad_n = grad_n + level * norm_f
    for by in (1, 2, 3):
        grad_n = grad_n + shifted(parts[by - 1], GATHER, -by).astype(f32)
    grad_n = coef * grad_n
    inner = jnp.sum(grad_n * norm_f, axis=1)
    inner = inner + other_core(inner)
    return (grad_n - inner[:, None] * norm_f) * inv_s


def solution(mesh):
    placed = (P(("loop", "rep"), "sec"), P(("loop", "rep"), "sec"))
    return jax.shard_map(
        body, mesh=mesh, in_specs=placed, out_specs=P(("loop", "rep"), "sec"), check_vma=False
    )
```

```python
import functools
import itertools

import jax
import jax.numpy as jnp
from jax import lax
from jax.experimental import pallas as pl
from jax.experimental.pallas import tpu as pltpu
from jax.sharding import PartitionSpec as P

AXES = ("loop", "rep", "sec")
X, Y, Z = 0, 1, 2
SIZE = 4
GATHER = (Y, X)
FIRST = (Z, Y)
SECOND = (X, Z)
STRIP = 32
PARAMS = pltpu.CompilerParams(vmem_limit_bytes=40 * 1024 * 1024)
SCALAR = pl.BlockSpec(memory_space=pltpu.SMEM)
WHOLE = pl.BlockSpec(memory_space=pltpu.VMEM)
BF16, F32 = jnp.bfloat16, jnp.float32


def index_of(chip, core):
    x, y, z = chip
    return (((x // 2) * SIZE + z) * 8 + y * 2 + x % 2) * 2 + core


def shifted(array, axis_of_core, by):
    pairs = []
    for chip in itertools.product(range(SIZE), repeat=3):
        for core in range(2):
            target = list(chip)
            axis = axis_of_core[core]
            target[axis] = (target[axis] + by) % SIZE
            pairs.append((index_of(chip, core), index_of(target, core)))
    return lax.ppermute(array, AXES, pairs)


def other_core(array):
    return lax.ppermute(array, "sec", [(0, 1), (1, 0)])


def place_along(axis_of_core):
    loop, rep, core = (lax.axis_index(name) for name in AXES)
    place = ((loop // SIZE) * 2 + rep % 2, rep // 2, loop % SIZE)
    return jnp.where(core == 0, place[axis_of_core[0]], place[axis_of_core[1]])


def scaled(piece, inv):
    return (piece.astype(F32) * inv).astype(BF16)


def part(places, by, size):
    return pl.ds(pl.multiple_of(lax.rem(places[0] + by, SIZE) * size, size), size)


def pack_own_kernel(places, s_own, s_far, t_own, t_far, *outs):
    half, wide = s_own.shape[1], t_own.shape[1]
    ts = wide // SIZE

    def inverse(own, far):
        a, b = own[...].astype(F32), far[...].astype(F32)
        total = jnp.sum(a * a, axis=1, keepdims=True) + jnp.sum(b * b, axis=1, keepdims=True)
        return lax.rsqrt(total + 1e-06)

    inv_s, inv_t = inverse(s_own, s_far), inverse(t_own, t_far)
    outs[SIZE][...] = inv_s
    outs[SIZE + 1][...] = inv_t
    norm = scaled(s_own[...], inv_s)
    for by in range(SIZE):
        outs[by][:, pl.ds(0, half)] = norm
        outs[by][:, pl.ds(half, ts)] = scaled(t_own[:, part(places, by, ts)], inv_t)


def pack_far_kernel(places, s_far, t_far, inv_s, inv_t, *outs):
    ss, ts = s_far.shape[1] // SIZE, t_far.shape[1] // SIZE
    for by in range(SIZE):
        outs[by][:, pl.ds(0, ss)] = scaled(s_far[:, part(places, by, ss)], inv_s[...])
        outs[by][:, pl.ds(ss, ts)] = scaled(t_far[:, part(places, by, ts)], inv_t[...])


def native_features(places, pack, half):
    ss = half // SIZE
    return pack[:, part(places, 0, ss)], pack[:, pl.ds(half, pack.shape[1] - half)]


def gram_kernel(share, native, places, *refs):
    count = SIZE if native else 2 * SIZE
    norms, packs = refs[:SIZE], refs[count - SIZE : count]
    outs, (left, right, product) = refs[count : count + SIZE], refs[count + SIZE :]
    half, feats = product.shape
    rows, ss = norms[0].shape[0], half // SIZE
    for k in range(SIZE):
        at = pl.ds(k * rows, rows)
        left[at, :] = norms[k][:, pl.ds(0, half)]
        if native:
            right[at, pl.ds(0, ss)], right[at, pl.ds(ss, feats - ss)] = native_features(
                places, packs[k], half
            )
        else:
            right[at, :] = packs[k][...]
    product[...] = lax.dot_general(
        left[...], right[...], (((0,), (0,)), ((), ())), preferred_element_type=F32
    )
    if native:
        row = lax.broadcasted_iota(jnp.int32, (ss, ss), 0)
        col = lax.broadcasted_iota(jnp.int32, (ss, ss), 1)
        product[part(places, 0, ss), pl.ds(0, ss)] -= jnp.where(row == col, share, 0.0)
    for by, out in enumerate(outs):
        which = lax.rem(places[1] + by, SIZE)
        block = pl.ds(pl.multiple_of(which * ss, ss), ss)
        rest = pl.ds(ss, feats - ss)
        out[:, pl.ds(0, ss)] = product[block, pl.ds(0, ss)].astype(out.dtype)
        out[:, rest] = -product[block, rest].astype(out.dtype)


def gather_weights(places, pieces, weights):
    ss = pieces[0].shape[0]
    for by, piece in enumerate(pieces):
        which = lax.rem(places[1] + SIZE - by, SIZE)
        weights[pl.ds(pl.multiple_of(which * ss, ss), ss), :] = piece[...]


def times(left, weights):
    return lax.dot_general(left, weights, (((1,), (1,)), ((), ())), preferred_element_type=F32)


def apply_native_kernel(places, *refs):
    packs, pieces, (out, left, weights) = refs[:SIZE], refs[SIZE : 2 * SIZE], refs[2 * SIZE :]
    half, feats = weights.shape
    rows, ss = packs[0].shape[0], half // SIZE
    gather_weights(places, pieces, weights)
    for k, pack in enumerate(packs):
        at = pl.ds(k * rows, rows)
        left[at, pl.ds(0, ss)], left[at, pl.ds(ss, feats - ss)] = native_features(
            places, pack, half
        )
    out[...] = times(left[...], weights[...])


def apply_far_kernel(first, count, places, *refs):
    packs, pieces, before = refs[:count], refs[count : count + SIZE], refs[count + SIZE]
    outs, weights = refs[count + SIZE + 1 : -1], refs[-1]
    rows = packs[0].shape[0]
    gather_weights(places, pieces, weights)
    for k, (pack, out) in enumerate(zip(packs, outs)):
        sofar = before[pl.ds((first + k) * rows, rows), :]
        out[...] = (times(pack[...], weights[...]) + sofar).astype(out.dtype)


def shapes(*described):
    return [jax.ShapeDtypeStruct(shape, dtype) for shape, dtype in described]


def kernel_call(kernel, name, outs, n_in, scratch=(), flops=0):
    return pl.pallas_call(
        kernel,
        out_shape=outs,
        in_specs=[SCALAR] + [WHOLE] * n_in,
        out_specs=[WHOLE] * len(outs),
        scratch_shapes=list(scratch),
        compiler_params=PARAMS,
        cost_estimate=pl.CostEstimate(flops=flops, bytes_accessed=4 << 20, transcendentals=0),
        name=name,
    )


def strip_call(kernel, name, widths_in, outs):
    rows = outs[0].shape[0]

    def spec(width):
        return pl.BlockSpec((STRIP, width), lambda i: (i, 0))

    return pl.pallas_call(
        kernel,
        out_shape=outs,
        grid=(rows // STRIP,),
        in_specs=[SCALAR] + [spec(w) for w in widths_in],
        out_specs=[spec(o.shape[1]) for o in outs],
        compiler_params=PARAMS,
        cost_estimate=pl.CostEstimate(flops=0, bytes_accessed=4 << 20, transcendentals=0),
        name=name,
    )


def body(student, teacher):
    rows, half = student.shape
    wide = teacher.shape[1]
    width = 2 * half
    groups = lax.axis_size("loop") * lax.axis_size("rep")
    passages = rows * groups
    coef = 32.0 * width / (passages**0.5)
    level = passages / width
    ss, ts = half // SIZE, wide // SIZE
    feats = ss + ts
    flops = 2 * SIZE * rows * half * feats
    places = jnp.stack([place_along(GATHER), place_along(FIRST)]).astype(jnp.int32)

    t_far, s_far = other_core(teacher), other_core(student)
    *near, inv_s, inv_t = strip_call(
        pack_own_kernel,
        "pack_own",
        (half, half, wide, wide),
        shapes(*[((rows, half + ts), BF16)] * SIZE, *[((rows, 1), F32)] * 2),
    )(places, student, s_far, teacher, t_far)
    far = strip_call(
        pack_far_kernel,
        "pack_far",
        (half, wide, 1, 1),
        shapes(*[((rows, feats), BF16)] * SIZE),
    )(places, s_far, t_far, inv_s, inv_t)
    norm_own = near[0][:, :half]
    near = [near[0]] + [shifted(near[by], GATHER, by) for by in (1, 2, 3)]
    far = [far[0]] + [shifted(far[by], GATHER, by) for by in (1, 2, 3)]

    def weights_of(native, packs, name):
        own, *sends = kernel_call(
            functools.partial(gram_kernel, level * SIZE / groups, native),
            name,
            shapes(((ss, feats), F32), *[((ss, feats), BF16)] * 3),
            len(packs),
            [
                pltpu.VMEM((SIZE * rows, half), BF16),
                pltpu.VMEM((SIZE * rows, feats), BF16),
                pltpu.VMEM((half, feats), F32),
            ],
            flops,
        )(places, *packs)
        total = own
        for by in (1, 2, 3):
            total = total + shifted(sends[by - 1], FIRST, by).astype(F32)
        shared = total.astype(BF16)
        for by in (1, 2, 3):
            total = total + shifted(shared, SECOND, by).astype(F32)
        piece = total.astype(BF16)
        return [piece] + [shifted(piece, FIRST, by) for by in (1, 2, 3)]

    near_weights = weights_of(True, near, "gram_native")
    far_weights = weights_of(False, near + far, "gram_far")

    sofar = kernel_call(
        apply_native_kernel,
        "apply_native",
        shapes(((SIZE * rows, half), F32)),
        2 * SIZE,
        [pltpu.VMEM((SIZE * rows, feats), BF16), pltpu.VMEM((half, feats), BF16)],
        flops,
    )(places, *near, *near_weights)[0]
    parts = kernel_call(
        functools.partial(apply_far_kernel, 1, SIZE - 1),
        "apply_sent",
        shapes(*[((rows, half), BF16)] * 3),
        2 * SIZE,
        [pltpu.VMEM((half, feats), BF16)],
        flops * 3 // 4,
    )(places, *far[1:], *far_weights, sofar)
    grad_n = kernel_call(
        functools.partial(apply_far_kernel, 0, 1),
        "apply_kept",
        shapes(((rows, half), F32)),
        SIZE + 2,
        [pltpu.VMEM((half, feats), BF16)],
        flops // 4,
    )(places, far[0], *far_weights, sofar)[0]
    norm_f = norm_own.astype(F32)
    grad_n = grad_n + level * norm_f
    for by in (1, 2, 3):
        grad_n = grad_n + shifted(parts[by - 1], GATHER, -by).astype(F32)
    grad_n = coef * grad_n
    inner = jnp.sum(grad_n * norm_f, axis=1)
    inner = inner + other_core(inner)
    return (grad_n - inner[:, None] * norm_f) * inv_s


def solution(mesh):
    placed = (P(("loop", "rep"), "sec"), P(("loop", "rep"), "sec"))
    return jax.shard_map(
        body, mesh=mesh, in_specs=placed, out_specs=P(("loop", "rep"), "sec"), check_vma=False
    )
```

```python
import functools
import itertools

import jax
import jax.numpy as jnp
from jax import lax
from jax.experimental import pallas as pl
from jax.experimental.pallas import tpu as pltpu
from jax.sharding import PartitionSpec as P

AXES = ("loop", "rep", "sec")
X, Y, Z = 0, 1, 2
SIZE = 4
GATHER = (Y, X)
FIRST = ((Z, Z), (X, Y))
SECOND = ((X, Y), (Z, Z))
ORDER = (2, 1, 3)
STRIP = 32
PARAMS = pltpu.CompilerParams(vmem_limit_bytes=40 * 1024 * 1024)
SCALAR = pl.BlockSpec(memory_space=pltpu.SMEM)
WHOLE = pl.BlockSpec(memory_space=pltpu.VMEM)
BF16, F32 = jnp.bfloat16, jnp.float32


def index_of(chip, core):
    x, y, z = chip
    return (((x // 2) * SIZE + z) * 8 + y * 2 + x % 2) * 2 + core


def shifted(array, axis_of_core, by):
    pairs = []
    for chip in itertools.product(range(SIZE), repeat=3):
        for core in range(2):
            target = list(chip)
            axis = axis_of_core[core]
            target[axis] = (target[axis] + by) % SIZE
            pairs.append((index_of(chip, core), index_of(target, core)))
    return lax.ppermute(array, AXES, pairs)


def other_core(array):
    return lax.ppermute(array, "sec", [(0, 1), (1, 0)])


def place_along(axis_of_core):
    loop, rep, core = (lax.axis_index(name) for name in AXES)
    place = ((loop // SIZE) * 2 + rep % 2, rep // 2, loop % SIZE)
    return jnp.where(core == 0, place[axis_of_core[0]], place[axis_of_core[1]])


def scaled(piece, inv):
    return (piece.astype(F32) * inv).astype(BF16)


def part(places, by, size):
    return pl.ds(pl.multiple_of(lax.rem(places[0] + by, SIZE) * size, size), size)


def squares(ref):
    values = ref[...].astype(F32)
    return jnp.sum(values * values, axis=1, keepdims=True)


def sums_kernel(s_own, t_own, ssq_s, ssq_t):
    ssq_s[...] = squares(s_own)
    ssq_t[...] = squares(t_own)


def pack_own_kernel(places, s_own, s_far, t_own, t_far, ssq_s, ssq_t, *outs):
    half, wide = s_own.shape[1], t_own.shape[1]
    ts = wide // SIZE
    inv_s = lax.rsqrt(ssq_s[...] + squares(s_far) + 1e-06)
    inv_t = lax.rsqrt(ssq_t[...] + squares(t_far) + 1e-06)
    outs[SIZE][...] = inv_s
    outs[SIZE + 1][...] = inv_t
    norm = scaled(s_own[...], inv_s)
    for by in range(SIZE):
        outs[by][:, pl.ds(0, half)] = norm
        outs[by][:, pl.ds(half, ts)] = scaled(t_own[:, part(places, by, ts)], inv_t)


def pack_far_kernel(places, s_far, t_far, inv_s, inv_t, *outs):
    ss, ts = s_far.shape[1] // SIZE, t_far.shape[1] // SIZE
    for by in range(SIZE):
        outs[by][:, pl.ds(0, ss)] = scaled(s_far[:, part(places, by, ss)], inv_s[...])
        outs[by][:, pl.ds(ss, ts)] = scaled(t_far[:, part(places, by, ts)], inv_t[...])


def native_features(places, pack, half):
    ss = half // SIZE
    return pack[:, part(places, 0, ss)], pack[:, pl.ds(half, pack.shape[1] - half)]


def gram_kernel(share, chunk, places, *refs):
    native = chunk == 0
    count = SIZE if native else 2 * SIZE
    norms, packs = refs[:SIZE], refs[count - SIZE : count]
    outs, (left, right, product) = refs[count : count + SIZE], refs[count + SIZE :]
    half, feats = product.shape
    rows, ss = norms[0].shape[0], half // SIZE
    for k in range(SIZE):
        at = pl.ds(k * rows, rows)
        left[at, :] = norms[k][:, pl.ds(0, half)]
        if native:
            right[at, pl.ds(0, ss)], right[at, pl.ds(ss, feats - ss)] = native_features(
                places, packs[k], half
            )
        else:
            right[at, :] = packs[k][...]
    product[...] = lax.dot_general(
        left[...], right[...], (((0,), (0,)), ((), ())), preferred_element_type=F32
    )
    if native:
        row = lax.broadcasted_iota(jnp.int32, (ss, ss), 0)
        col = lax.broadcasted_iota(jnp.int32, (ss, ss), 1)
        product[part(places, 0, ss), pl.ds(0, ss)] -= jnp.where(row == col, share, 0.0)
    for by, out in enumerate(outs):
        which = lax.rem(places[1 + chunk] + by, SIZE)
        block = pl.ds(pl.multiple_of(which * ss, ss), ss)
        rest = pl.ds(ss, feats - ss)
        out[:, pl.ds(0, ss)] = product[block, pl.ds(0, ss)].astype(out.dtype)
        out[:, rest] = -product[block, rest].astype(out.dtype)


def gather_weights(place, pieces, weights):
    ss = pieces[0].shape[0]
    for by, piece in enumerate(pieces):
        which = lax.rem(place + SIZE - by, SIZE)
        weights[pl.ds(pl.multiple_of(which * ss, ss), ss), :] = piece[...]


def times(left, weights):
    return lax.dot_general(left, weights, (((1,), (1,)), ((), ())), preferred_element_type=F32)


def apply_native_kernel(places, *refs):
    packs, pieces, (out, left, weights) = refs[:SIZE], refs[SIZE : 2 * SIZE], refs[2 * SIZE :]
    half, feats = weights.shape
    rows, ss = packs[0].shape[0], half // SIZE
    gather_weights(places[1], pieces, weights)
    for k, pack in enumerate(packs):
        at = pl.ds(k * rows, rows)
        left[at, pl.ds(0, ss)], left[at, pl.ds(ss, feats - ss)] = native_features(
            places, pack, half
        )
    out[...] = times(left[...], weights[...])


def apply_far_kernel(first, count, places, *refs):
    packs, pieces, before = refs[:count], refs[count : count + SIZE], refs[count + SIZE]
    outs, weights = refs[count + SIZE + 1 : -1], refs[-1]
    rows = packs[0].shape[0]
    gather_weights(places[2], pieces, weights)
    for k, (pack, out) in enumerate(zip(packs, outs)):
        sofar = before[pl.ds((first + k) * rows, rows), :]
        out[...] = (times(pack[...], weights[...]) + sofar).astype(out.dtype)


def shapes(*described):
    return [jax.ShapeDtypeStruct(shape, dtype) for shape, dtype in described]


def kernel_call(kernel, name, outs, n_in, scratch=(), flops=0):
    return pl.pallas_call(
        kernel,
        out_shape=outs,
        in_specs=[SCALAR] + [WHOLE] * n_in,
        out_specs=[WHOLE] * len(outs),
        scratch_shapes=list(scratch),
        compiler_params=PARAMS,
        cost_estimate=pl.CostEstimate(flops=flops, bytes_accessed=4 << 20, transcendentals=0),
        name=name,
    )


def strip_call(kernel, name, widths_in, outs):
    rows = outs[0].shape[0]

    def spec(width):
        return pl.BlockSpec((STRIP, width), lambda i: (i, 0))

    return pl.pallas_call(
        kernel,
        out_shape=outs,
        grid=(rows // STRIP,),
        in_specs=[SCALAR] + [spec(w) for w in widths_in],
        out_specs=[spec(o.shape[1]) for o in outs],
        compiler_params=PARAMS,
        cost_estimate=pl.CostEstimate(flops=0, bytes_accessed=4 << 20, transcendentals=0),
        name=name,
    )


def body(student, teacher):
    rows, half = student.shape
    wide = teacher.shape[1]
    width = 2 * half
    groups = lax.axis_size("loop") * lax.axis_size("rep")
    passages = rows * groups
    coef = 32.0 * width / (passages**0.5)
    level = passages / width
    ss, ts = half // SIZE, wide // SIZE
    feats = ss + ts
    flops = 2 * SIZE * rows * half * feats
    places = jnp.stack([place_along(axes) for axes in (GATHER, *FIRST)]).astype(jnp.int32)

    t_far, s_far = other_core(teacher), other_core(student)
    ssq_s, ssq_t = pl.pallas_call(
        sums_kernel,
        out_shape=shapes(*[((rows, 1), F32)] * 2),
        in_specs=[WHOLE] * 2,
        out_specs=[WHOLE] * 2,
        compiler_params=PARAMS,
        cost_estimate=pl.CostEstimate(flops=0, bytes_accessed=1 << 20, transcendentals=0),
        name="sums",
    )(student, teacher)
    *near, inv_s, inv_t = strip_call(
        pack_own_kernel,
        "pack_own",
        (half, half, wide, wide, 1, 1),
        shapes(*[((rows, half + ts), BF16)] * SIZE, *[((rows, 1), F32)] * 2),
    )(places, student, s_far, teacher, t_far, ssq_s, ssq_t)
    far = strip_call(
        pack_far_kernel,
        "pack_far",
        (half, wide, 1, 1),
        shapes(*[((rows, feats), BF16)] * SIZE),
    )(places, s_far, t_far, inv_s, inv_t)
    norm_own = near[0][:, :half]

    def exchanged(own, sent, axis_of_core, sign=1):
        arrived = {by: shifted(sent(by), axis_of_core, sign * by) for by in ORDER}
        return [own] + [arrived[by] for by in (1, 2, 3)]

    def added(total, sent, axis_of_core, sign=1):
        for array in exchanged(None, sent, axis_of_core, sign)[1:]:
            total = total + array.astype(F32)
        return total

    near = exchanged(near[0], near.__getitem__, GATHER)
    far = exchanged(far[0], far.__getitem__, GATHER)

    def weights_of(chunk, packs, name):
        own, *sends = kernel_call(
            functools.partial(gram_kernel, level * SIZE / groups, chunk),
            name,
            shapes(((ss, feats), F32), *[((ss, feats), BF16)] * 3),
            len(packs),
            [
                pltpu.VMEM((SIZE * rows, half), BF16),
                pltpu.VMEM((SIZE * rows, feats), BF16),
                pltpu.VMEM((half, feats), F32),
            ],
            flops,
        )(places, *packs)
        total = added(own, lambda by: sends[by - 1], FIRST[chunk])
        shared = total.astype(BF16)
        piece = added(total, lambda by: shared, SECOND[chunk]).astype(BF16)
        return exchanged(piece, lambda by: piece, FIRST[chunk])

    near_weights = weights_of(0, near, "gram_native")
    far_weights = weights_of(1, near + far, "gram_far")

    sofar = kernel_call(
        apply_native_kernel,
        "apply_native",
        shapes(((SIZE * rows, half), F32)),
        2 * SIZE,
        [pltpu.VMEM((SIZE * rows, feats), BF16), pltpu.VMEM((half, feats), BF16)],
        flops,
    )(places, *near, *near_weights)[0]
    parts = kernel_call(
        functools.partial(apply_far_kernel, 1, SIZE - 1),
        "apply_sent",
        shapes(*[((rows, half), BF16)] * 3),
        2 * SIZE,
        [pltpu.VMEM((half, feats), BF16)],
        flops * 3 // 4,
    )(places, *far[1:], *far_weights, sofar)
    grad_n = kernel_call(
        functools.partial(apply_far_kernel, 0, 1),
        "apply_kept",
        shapes(((rows, half), F32)),
        SIZE + 2,
        [pltpu.VMEM((half, feats), BF16)],
        flops // 4,
    )(places, far[0], *far_weights, sofar)[0]
    norm_f = norm_own.astype(F32)
    grad_n = grad_n + level * norm_f
    grad_n = coef * added(grad_n, lambda by: parts[by - 1], GATHER, -1)
    inner = jnp.sum(grad_n * norm_f, axis=1)
    inner = inner + other_core(inner)
    return (grad_n - inner[:, None] * norm_f) * inv_s


def solution(mesh):
    placed = (P(("loop", "rep"), "sec"), P(("loop", "rep"), "sec"))
    return jax.shard_map(
        body, mesh=mesh, in_specs=placed, out_specs=P(("loop", "rep"), "sec"), check_vma=False
    )
```

```python
import functools
import itertools

import jax
import jax.numpy as jnp
from jax import lax
from jax.experimental import pallas as pl
from jax.experimental.pallas import tpu as pltpu
from jax.sharding import PartitionSpec as P

AXES = ("loop", "rep", "sec")
X, Y, Z = 0, 1, 2
SIZE = 4
GATHER = (Y, X)
REDUCE = (X, Y)
GATHER_FLIP = (1, 3)
REDUCE_FLIP = (3, 1)
BIT_OF_Z = ((0, 1, 1, 0), (0, 0, 1, 1))
GROUP = 8
MESSAGES = ((0, 0), (2, 1), (2, 0), (1, 1), (3, 1), (1, 0), (3, 0), (0, 1))
EARLY = 3
RING_ORDER = (2, 1, 3)
STRIP = 64
LOADS = 4
PARAMS = pltpu.CompilerParams(vmem_limit_bytes=40 * 1024 * 1024)
SCALAR = pl.BlockSpec(memory_space=pltpu.SMEM)
WHOLE = pl.BlockSpec(memory_space=pltpu.VMEM)
BF16, F32 = jnp.bfloat16, jnp.float32


def index_of(chip, core):
    x, y, z = chip
    return (((x // 2) * SIZE + z) * 8 + y * 2 + x % 2) * 2 + core


def moved(array, axis_of_core, by, flip_of_core=(0, 0)):
    pairs = []
    for chip in itertools.product(range(SIZE), repeat=3):
        for core in range(2):
            target = list(chip)
            axis = axis_of_core[core]
            target[axis] = (target[axis] + by) % SIZE
            target[Z] ^= flip_of_core[core]
            pairs.append((index_of(chip, core), index_of(target, core)))
    return lax.ppermute(array, AXES, pairs)


def other_core(array):
    return lax.ppermute(array, "sec", [(0, 1), (1, 0)])


def places_here():
    loop, rep, core = (lax.axis_index(name) for name in AXES)
    place = ((loop // SIZE) * 2 + rep % 2, rep // 2, loop % SIZE)
    bits = []
    for table in BIT_OF_Z:
        bit = sum(jnp.where(place[Z] == z, value, 0) for z, value in enumerate(table))
        bits.append(bit)
    first = core == 0
    return jnp.stack(
        [
            jnp.where(first, place[GATHER[0]], place[GATHER[1]]),
            jnp.where(first, bits[0], bits[1]),
            jnp.where(first, place[REDUCE[0]], place[REDUCE[1]]),
        ]
    ).astype(jnp.int32)


def block(which, size):
    return pl.ds(pl.multiple_of(which * size, size), size)


def squares(values):
    values = values.astype(F32)
    return jnp.sum(values * values, axis=1, keepdims=True)


def load_kernel(s_from, t_from, s_own, t_own, ssq_s, ssq_t, arrived):
    rows = s_own.shape[0]
    step = rows // LOADS
    copies = []
    for i in range(LOADS):
        at = pl.ds(i * step, step)
        pair = [
            pltpu.make_async_copy(s_from.at[at, :], s_own.at[at, :], arrived.at[0, i]),
            pltpu.make_async_copy(t_from.at[at, :], t_own.at[at, :], arrived.at[1, i]),
        ]
        for copy in pair:
            copy.start()
        copies.append(pair)
    for i, pair in enumerate(copies):
        for copy in pair:
            copy.wait()
        at = pl.ds(i * step, step)
        ssq_s[at, :] = squares(s_own[at, :])
        ssq_t[at, :] = squares(t_own[at, :])


def inverse_kernel(s_far, t_far, ssq_s, ssq_t, inv_s, inv_t):
    inv_s[...] = lax.rsqrt(ssq_s[...] + squares(s_far[...]) + 1e-06)
    inv_t[...] = lax.rsqrt(ssq_t[...] + squares(t_far[...]) + 1e-06)


def scaled(piece, inv):
    return (piece.astype(F32) * inv).astype(BF16)


def pack_kernel(messages, places, s_own, s_far, t_own, t_far, first_s, first_t, *outs):
    rows, half = s_own.shape
    ss, ts = half // SIZE, t_own.shape[1] // GROUP
    if len(outs) > len(messages):
        inverse_kernel(s_far, t_far, first_s, first_t, *outs[len(messages) :])
        first_s, first_t = outs[len(messages) :]

    @pl.loop(0, rows // STRIP)
    def _(strip):
        at = pl.ds(pl.multiple_of(strip * STRIP, STRIP), STRIP)
        inv_s, inv_t = first_s[at, :], first_t[at, :]
        norm = scaled(s_own[at, :], inv_s)
        for (by, flip), out in zip(messages, outs):
            ring = lax.rem(places[0] + by, SIZE)
            bit = places[1] if flip == 0 else 1 - places[1]
            out[at, pl.ds(0, half)] = norm
            own, far = (ref[at, block(ring, ss)].astype(F32) for ref in (s_own, s_far))
            out[at, pl.ds(half, ss)] = (jnp.where(bit == 1, far, own) * inv_s).astype(BF16)
            which = block(ring + SIZE * bit, ts)
            out[at, pl.ds(half + ss, ts)] = scaled(t_own[at, which], inv_t)
            out[at, pl.ds(half + ss + ts, ts)] = scaled(t_far[at, which], inv_t)


def stacked(packs, left, right):
    rows, half = packs[0].shape[0], left.shape[1]
    for k, pack in enumerate(packs):
        at = pl.ds(k * rows, rows)
        left[at, :] = pack[:, pl.ds(0, half)]
        right[at, :] = pack[:, pl.ds(half, right.shape[1])]


def cross(left, right):
    return lax.dot_general(
        left[...], right[...], (((0,), (0,)), ((), ())), preferred_element_type=F32
    )


def gram_early_kernel(*refs):
    packs, (product, left, right) = refs[:-3], refs[-3:]
    stacked(packs, left, right)
    product[...] = cross(left, right)


def gram_late_kernel(share, places, *refs):
    packs, (before, *outs), (left, right, product) = refs[: -SIZE - 4], refs[-SIZE - 4 : -3], refs[-3:]
    half, feats = product.shape
    ss = half // SIZE
    stacked(packs, left, right)
    product[...] = before[...] + cross(left, right)
    row = lax.broadcasted_iota(jnp.int32, (ss, ss), 0)
    col = lax.broadcasted_iota(jnp.int32, (ss, ss), 1)
    on_diagonal = (row == col) & (places[1] == 0)
    product[block(places[0], ss), pl.ds(0, ss)] -= jnp.where(on_diagonal, share, 0.0)
    for by, out in enumerate(outs):
        at = block(lax.rem(places[2] + by, SIZE), ss)
        rest = pl.ds(ss, feats - ss)
        out[:, pl.ds(0, ss)] = product[at, pl.ds(0, ss)].astype(out.dtype)
        out[:, rest] = -product[at, rest].astype(out.dtype)


def apply_kernel(count, places, *refs):
    packs, pieces = refs[:count], refs[count : count + SIZE]
    outs, weights = refs[count + SIZE : -1], refs[-1]
    half, feats = weights.shape
    ss = half // SIZE
    for by, piece in enumerate(pieces):
        weights[block(lax.rem(places[2] + SIZE - by, SIZE), ss), :] = piece[...]
    for pack, out in zip(packs, outs):
        out[...] = lax.dot_general(
            pack[:, pl.ds(half, feats)],
            weights[...],
            (((1,), (1,)), ((), ())),
            preferred_element_type=F32,
        ).astype(out.dtype)


def shapes(*described):
    return [jax.ShapeDtypeStruct(shape, dtype) for shape, dtype in described]


def kernel_call(kernel, name, outs, args, scratch=(), flops=0, specs=None):
    return pl.pallas_call(
        kernel,
        out_shape=outs,
        in_specs=specs or [SCALAR] + [WHOLE] * (len(args) - 1),
        out_specs=[WHOLE] * len(outs),
        scratch_shapes=list(scratch),
        compiler_params=PARAMS,
        cost_estimate=pl.CostEstimate(flops=flops, bytes_accessed=4 << 20, transcendentals=0),
        name=name,
    )(*args)


def body(student, teacher):
    rows, half = student.shape
    wide = teacher.shape[1]
    width = 2 * half
    groups = lax.axis_size("loop") * lax.axis_size("rep")
    passages = rows * groups
    coef = 32.0 * width / (passages**0.5)
    level = passages / width
    ss, ts = half // SIZE, wide // GROUP
    feats = ss + 2 * ts
    flops = GROUP * rows * half * feats
    places = places_here()

    t_far, s_far = other_core(teacher), other_core(student)
    s_own, t_own, ssq_s, ssq_t = kernel_call(
        load_kernel,
        "load",
        shapes((student.shape, BF16), (teacher.shape, BF16), *[((rows, 1), F32)] * 2),
        (student, teacher),
        [pltpu.SemaphoreType.DMA((2, LOADS))],
        specs=[pl.BlockSpec(memory_space=pltpu.HBM)] * 2,
    )
    pack = ((rows, half + feats), BF16)
    *sent, inv_s, inv_t = kernel_call(
        functools.partial(pack_kernel, MESSAGES[1:EARLY]),
        "pack_early",
        shapes(*[pack] * (EARLY - 1), *[((rows, 1), F32)] * 2),
        (places, s_own, s_far, t_own, t_far, ssq_s, ssq_t),
    )
    late = MESSAGES[EARLY:] + MESSAGES[:1]
    sent += kernel_call(
        functools.partial(pack_kernel, late),
        "pack_late",
        shapes(*[pack] * len(late)),
        (places, s_own, s_far, t_own, t_far, inv_s, inv_t),
    )
    packs = [sent[-1]] + [
        moved(array, GATHER, by, [flip * f for f in GATHER_FLIP])
        for array, (by, flip) in zip(sent, MESSAGES[1:])
    ]
    norm_f = packs[0][:, :half].astype(F32)

    count = GROUP // 2
    operands = [pltpu.VMEM((count * rows, half), BF16), pltpu.VMEM((count * rows, feats), BF16)]
    product = pl.pallas_call(
        gram_early_kernel,
        out_shape=shapes(((half, feats), F32))[0],
        in_specs=[WHOLE] * count,
        out_specs=WHOLE,
        scratch_shapes=operands,
        compiler_params=PARAMS,
        cost_estimate=pl.CostEstimate(flops=flops, bytes_accessed=4 << 20, transcendentals=0),
        name="gram_early",
    )(*packs[:count])
    own, *sends = kernel_call(
        functools.partial(gram_late_kernel, level * GROUP / groups),
        "gram_late",
        shapes(((ss, feats), F32), *[((ss, feats), BF16)] * 3),
        (places, *packs[count:], product),
        operands + [pltpu.VMEM((half, feats), F32)],
        flops,
    )
    arrived = [moved(sends[by - 1], REDUCE, by) for by in RING_ORDER]
    total = own + sum(array.astype(F32) for array in arrived)
    total = total + moved(total.astype(BF16), REDUCE, 0, REDUCE_FLIP).astype(F32)
    piece = total.astype(BF16)
    arrived = {by: moved(piece, REDUCE, by) for by in RING_ORDER}
    pieces = [piece] + [arrived[by] for by in (1, 2, 3)]

    weights = [pltpu.VMEM((half, feats), BF16)]
    back = kernel_call(
        functools.partial(apply_kernel, EARLY),
        "apply_early",
        shapes(*[((rows, half), BF16)] * EARLY),
        (places, *packs[1 : EARLY + 1], *pieces),
        weights,
        flops * EARLY // GROUP,
    )
    rest = GROUP - 1 - EARLY
    *later, grad_n = kernel_call(
        functools.partial(apply_kernel, rest + 1),
        "apply_late",
        shapes(*[((rows, half), BF16)] * rest, ((rows, half), F32)),
        (places, *packs[EARLY + 1 :], packs[0], *pieces),
        weights,
        flops * (rest + 1) // GROUP,
    )
    grad_n = grad_n + level * norm_f
    for array, (by, flip) in zip(list(back) + later, MESSAGES[1:]):
        grad_n = grad_n + moved(array, GATHER, -by, [flip * f for f in GATHER_FLIP]).astype(F32)
    grad_n = coef * grad_n
    inner = jnp.sum(grad_n * norm_f, axis=1)
    inner = inner + other_core(inner)
    return (grad_n - inner[:, None] * norm_f) * inv_s


def solution(mesh):
    placed = (P(("loop", "rep"), "sec"), P(("loop", "rep"), "sec"))
    return jax.shard_map(
        body, mesh=mesh, in_specs=placed, out_specs=P(("loop", "rep"), "sec"), check_vma=False
    )
```

```python
import functools
import itertools

import jax
import jax.numpy as jnp
from jax import lax
from jax.experimental import pallas as pl
from jax.experimental.pallas import tpu as pltpu
from jax.sharding import PartitionSpec as P

AXES = ("loop", "rep", "sec")
X, Y, Z = 0, 1, 2
SIZE = 4
GATHER = (Y, X)
FIRST = ((X, Z), (Z, Y))
SECOND = ((Z, Y), (X, Z))
ORDER = (2, 1, 3)
STRIP = 32
PARAMS = pltpu.CompilerParams(vmem_limit_bytes=40 * 1024 * 1024)
SCALAR = pl.BlockSpec(memory_space=pltpu.SMEM)
WHOLE = pl.BlockSpec(memory_space=pltpu.VMEM)
BF16, F32 = jnp.bfloat16, jnp.float32


def index_of(chip, core):
    x, y, z = chip
    return (((x // 2) * SIZE + z) * 8 + y * 2 + x % 2) * 2 + core


def shifted(array, axis_of_core, by):
    pairs = []
    for chip in itertools.product(range(SIZE), repeat=3):
        for core in range(2):
            target = list(chip)
            axis = axis_of_core[core]
            target[axis] = (target[axis] + by) % SIZE
            pairs.append((index_of(chip, core), index_of(target, core)))
    return lax.ppermute(array, AXES, pairs)


def other_core(array):
    return lax.ppermute(array, "sec", [(0, 1), (1, 0)])


def place_along(axis_of_core):
    loop, rep, core = (lax.axis_index(name) for name in AXES)
    place = ((loop // SIZE) * 2 + rep % 2, rep // 2, loop % SIZE)
    return jnp.where(core == 0, place[axis_of_core[0]], place[axis_of_core[1]])


def scaled(piece, inv):
    return (piece.astype(F32) * inv).astype(BF16)


def part(places, by, size):
    return pl.ds(pl.multiple_of(lax.rem(places[0] + by, SIZE) * size, size), size)


def squares(values):
    values = values.astype(F32)
    return jnp.sum(values * values, axis=1, keepdims=True)


def strips(rows):
    return [pl.ds(start, STRIP) for start in range(0, rows, STRIP)]


def sums_kernel(s_own, t_own, ssq_s, ssq_t):
    for at in strips(s_own.shape[0]):
        ssq_s[at, :] = squares(s_own[at, :])
        ssq_t[at, :] = squares(t_own[at, :])


def pack_own_kernel(places, s_own, s_far, t_own, t_far, ssq_s, ssq_t, *outs):
    rows, half = s_own.shape
    ts = t_own.shape[1] // SIZE
    inv_s, inv_t = outs[SIZE:]
    for at in strips(rows):
        inv_s[at, :] = lax.rsqrt(ssq_s[at, :] + squares(s_far[at, :]) + 1e-06)
        inv_t[at, :] = lax.rsqrt(ssq_t[at, :] + squares(t_far[at, :]) + 1e-06)
    for at in strips(rows):
        norm = scaled(s_own[at, :], inv_s[at, :])
        for by in range(SIZE):
            outs[by][at, pl.ds(0, half)] = norm
            outs[by][at, pl.ds(half, ts)] = scaled(t_own[at, part(places, by, ts)], inv_t[at, :])


def pack_far_kernel(places, s_far, t_far, inv_s, inv_t, *outs):
    rows = s_far.shape[0]
    ss, ts = s_far.shape[1] // SIZE, t_far.shape[1] // SIZE
    for at in strips(rows):
        for by in range(SIZE):
            outs[by][at, pl.ds(0, ss)] = scaled(s_far[at, part(places, by, ss)], inv_s[at, :])
            outs[by][at, pl.ds(ss, ts)] = scaled(t_far[at, part(places, by, ts)], inv_t[at, :])


def native_features(places, pack, half):
    ss = half // SIZE
    return pack[:, part(places, 0, ss)], pack[:, pl.ds(half, pack.shape[1] - half)]


def gram_kernel(share, chunk, places, *refs):
    native = chunk == 0
    count = SIZE if native else 2 * SIZE
    norms, packs = refs[:SIZE], refs[count - SIZE : count]
    outs, (left, right, product) = refs[count : count + SIZE], refs[count + SIZE :]
    half, feats = product.shape
    rows, ss = norms[0].shape[0], half // SIZE
    for k in range(SIZE):
        at = pl.ds(k * rows, rows)
        left[at, :] = norms[k][:, pl.ds(0, half)]
        if native:
            right[at, pl.ds(0, ss)], right[at, pl.ds(ss, feats - ss)] = native_features(
                places, packs[k], half
            )
        else:
            right[at, :] = packs[k][...]
    product[...] = lax.dot_general(
        left[...], right[...], (((0,), (0,)), ((), ())), preferred_element_type=F32
    )
    if native:
        row = lax.broadcasted_iota(jnp.int32, (ss, ss), 0)
        col = lax.broadcasted_iota(jnp.int32, (ss, ss), 1)
        product[part(places, 0, ss), pl.ds(0, ss)] -= jnp.where(row == col, share, 0.0)
    for by, out in enumerate(outs):
        which = lax.rem(places[1 + chunk] + by, SIZE)
        block = pl.ds(pl.multiple_of(which * ss, ss), ss)
        rest = pl.ds(ss, feats - ss)
        out[:, pl.ds(0, ss)] = product[block, pl.ds(0, ss)].astype(out.dtype)
        out[:, rest] = -product[block, rest].astype(out.dtype)


def gather_weights(place, pieces, weights):
    ss = pieces[0].shape[0]
    for by, piece in enumerate(pieces):
        which = lax.rem(place + SIZE - by, SIZE)
        weights[pl.ds(pl.multiple_of(which * ss, ss), ss), :] = piece[...]


def times(left, weights):
    return lax.dot_general(left, weights, (((1,), (1,)), ((), ())), preferred_element_type=F32)


def apply_native_kernel(places, *refs):
    packs, pieces, (out, left, weights) = refs[:SIZE], refs[SIZE : 2 * SIZE], refs[2 * SIZE :]
    half, feats = weights.shape
    rows, ss = packs[0].shape[0], half // SIZE
    gather_weights(places[1], pieces, weights)
    for k, pack in enumerate(packs):
        at = pl.ds(k * rows, rows)
        left[at, pl.ds(0, ss)], left[at, pl.ds(ss, feats - ss)] = native_features(
            places, pack, half
        )
    out[...] = times(left[...], weights[...])


def apply_far_kernel(first, count, places, *refs):
    packs, pieces, before = refs[:count], refs[count : count + SIZE], refs[count + SIZE]
    outs, weights = refs[count + SIZE + 1 : -1], refs[-1]
    rows = packs[0].shape[0]
    gather_weights(places[2], pieces, weights)
    for k, (pack, out) in enumerate(zip(packs, outs)):
        sofar = before[pl.ds((first + k) * rows, rows), :]
        out[...] = (times(pack[...], weights[...]) + sofar).astype(out.dtype)


def shapes(*described):
    return [jax.ShapeDtypeStruct(shape, dtype) for shape, dtype in described]


def kernel_call(kernel, name, outs, n_in, scratch=(), flops=0):
    return pl.pallas_call(
        kernel,
        out_shape=outs,
        in_specs=[SCALAR] + [WHOLE] * n_in,
        out_specs=[WHOLE] * len(outs),
        scratch_shapes=list(scratch),
        compiler_params=PARAMS,
        cost_estimate=pl.CostEstimate(flops=flops, bytes_accessed=4 << 20, transcendentals=0),
        name=name,
    )


def body(student, teacher):
    rows, half = student.shape
    wide = teacher.shape[1]
    width = 2 * half
    groups = lax.axis_size("loop") * lax.axis_size("rep")
    passages = rows * groups
    coef = 32.0 * width / (passages**0.5)
    level = passages / width
    ss, ts = half // SIZE, wide // SIZE
    feats = ss + ts
    flops = 2 * SIZE * rows * half * feats
    places = jnp.stack([place_along(axes) for axes in (GATHER, *FIRST)]).astype(jnp.int32)

    t_far, s_far = other_core(teacher), other_core(student)
    ssq_s, ssq_t = pl.pallas_call(
        sums_kernel,
        out_shape=shapes(*[((rows, 1), F32)] * 2),
        in_specs=[WHOLE] * 2,
        out_specs=[WHOLE] * 2,
        compiler_params=PARAMS,
        cost_estimate=pl.CostEstimate(flops=0, bytes_accessed=1 << 20, transcendentals=0),
        name="sums",
    )(student, teacher)
    *near, inv_s, inv_t = kernel_call(
        pack_own_kernel,
        "pack_own",
        shapes(*[((rows, half + ts), BF16)] * SIZE, *[((rows, 1), F32)] * 2),
        6,
    )(places, student, s_far, teacher, t_far, ssq_s, ssq_t)
    far = kernel_call(
        pack_far_kernel, "pack_far", shapes(*[((rows, feats), BF16)] * SIZE), 4
    )(places, s_far, t_far, inv_s, inv_t)
    norm_own = near[0][:, :half]

    def exchanged(own, sent, axis_of_core, sign=1):
        arrived = {by: shifted(sent(by), axis_of_core, sign * by) for by in ORDER}
        return [own] + [arrived[by] for by in (1, 2, 3)]

    def added(total, sent, axis_of_core, sign=1):
        for array in exchanged(None, sent, axis_of_core, sign)[1:]:
            total = total + array.astype(F32)
        return total

    near = exchanged(near[0], near.__getitem__, GATHER)
    far = exchanged(far[0], far.__getitem__, GATHER)

    def weights_of(chunk, packs, name):
        own, *sends = kernel_call(
            functools.partial(gram_kernel, level * SIZE / groups, chunk),
            name,
            shapes(((ss, feats), F32), *[((ss, feats), BF16)] * 3),
            len(packs),
            [
                pltpu.VMEM((SIZE * rows, half), BF16),
                pltpu.VMEM((SIZE * rows, feats), BF16),
                pltpu.VMEM((half, feats), F32),
            ],
            flops,
        )(places, *packs)
        total = added(own, lambda by: sends[by - 1], FIRST[chunk])
        shared = total.astype(BF16)
        piece = added(total, lambda by: shared, SECOND[chunk]).astype(BF16)
        return exchanged(piece, lambda by: piece, FIRST[chunk])

    near_weights = weights_of(0, near, "gram_native")
    far_weights = weights_of(1, near + far, "gram_far")

    sofar = kernel_call(
        apply_native_kernel,
        "apply_native",
        shapes(((SIZE * rows, half), F32)),
        2 * SIZE,
        [pltpu.VMEM((SIZE * rows, feats), BF16), pltpu.VMEM((half, feats), BF16)],
        flops,
    )(places, *near, *near_weights)[0]
    parts = kernel_call(
        functools.partial(apply_far_kernel, 1, SIZE - 1),
        "apply_sent",
        shapes(*[((rows, half), BF16)] * 3),
        2 * SIZE,
        [pltpu.VMEM((half, feats), BF16)],
        flops * 3 // 4,
    )(places, *far[1:], *far_weights, sofar)
    grad_n = kernel_call(
        functools.partial(apply_far_kernel, 0, 1),
        "apply_kept",
        shapes(((rows, half), F32)),
        SIZE + 2,
        [pltpu.VMEM((half, feats), BF16)],
        flops // 4,
    )(places, far[0], *far_weights, sofar)[0]
    norm_f = norm_own.astype(F32)
    grad_n = grad_n + level * norm_f
    grad_n = coef * added(grad_n, lambda by: parts[by - 1], GATHER, -1)
    inner = jnp.sum(grad_n * norm_f, axis=1)
    inner = inner + other_core(inner)
    return (grad_n - inner[:, None] * norm_f) * inv_s


def solution(mesh):
    placed = (P(("loop", "rep"), "sec"), P(("loop", "rep"), "sec"))
    return jax.shard_map(
        body, mesh=mesh, in_specs=placed, out_specs=P(("loop", "rep"), "sec"), check_vma=False
    )
```

```python
import functools
import itertools

import jax
import jax.numpy as jnp
from jax import lax
from jax.experimental import pallas as pl
from jax.experimental.pallas import tpu as pltpu
from jax.sharding import PartitionSpec as P

AXES = ("loop", "rep", "sec")
X, Y, Z = 0, 1, 2
SIZE = 4
GATHER = (Y, X)
FIRST = ((X, Z), (Z, Y))
SECOND = ((Z, Y), (X, Z))
ORDER = (2, 1, 3)
PAIRS = ((1, 3), (3, 1))
STRIP = 32
PARAMS = pltpu.CompilerParams(vmem_limit_bytes=40 * 1024 * 1024)
SCALAR = pl.BlockSpec(memory_space=pltpu.SMEM)
WHOLE = pl.BlockSpec(memory_space=pltpu.VMEM)
BF16, F32 = jnp.bfloat16, jnp.float32


def index_of(chip, core):
    x, y, z = chip
    return (((x // 2) * SIZE + z) * 8 + y * 2 + x % 2) * 2 + core


def moved(array, axis_of_core, place_of):
    pairs = []
    for chip in itertools.product(range(SIZE), repeat=3):
        for core in range(2):
            target = list(chip)
            axis = axis_of_core[core]
            target[axis] = place_of(target[axis])
            pairs.append((index_of(chip, core), index_of(target, core)))
    return lax.ppermute(array, AXES, pairs)


def shifted(array, axis_of_core, by):
    return moved(array, axis_of_core, lambda place: (place + by) % SIZE)


def paired(array, axis_of_core, mask):
    return moved(array, axis_of_core, lambda place: place ^ mask)


def other_core(array):
    return lax.ppermute(array, "sec", [(0, 1), (1, 0)])


def place_along(axis_of_core):
    loop, rep, core = (lax.axis_index(name) for name in AXES)
    place = ((loop // SIZE) * 2 + rep % 2, rep // 2, loop % SIZE)
    return jnp.where(core == 0, place[axis_of_core[0]], place[axis_of_core[1]])


def scaled(piece, inv):
    return (piece.astype(F32) * inv).astype(BF16)


def part(places, by, size):
    return pl.ds(pl.multiple_of(lax.rem(places[0] + by, SIZE) * size, size), size)


def squares(values):
    values = values.astype(F32)
    return jnp.sum(values * values, axis=1, keepdims=True)


def strips(rows):
    return [pl.ds(start, STRIP) for start in range(0, rows, STRIP)]


def sums_kernel(s_own, t_own, ssq_s, ssq_t):
    for at in strips(s_own.shape[0]):
        ssq_s[at, :] = squares(s_own[at, :])
        ssq_t[at, :] = squares(t_own[at, :])


def pack_own_kernel(places, s_own, s_far, t_own, t_far, ssq_s, ssq_t, *outs):
    rows, half = s_own.shape
    ts = t_own.shape[1] // SIZE
    inv_s, inv_t = outs[SIZE:]
    for at in strips(rows):
        inv_s[at, :] = lax.rsqrt(ssq_s[at, :] + squares(s_far[at, :]) + 1e-06)
        inv_t[at, :] = lax.rsqrt(ssq_t[at, :] + squares(t_far[at, :]) + 1e-06)
    for at in strips(rows):
        norm = scaled(s_own[at, :], inv_s[at, :])
        for by in range(SIZE):
            outs[by][at, pl.ds(0, half)] = norm
            outs[by][at, pl.ds(half, ts)] = scaled(t_own[at, part(places, by, ts)], inv_t[at, :])


def pack_far_kernel(places, s_far, t_far, inv_s, inv_t, *outs):
    rows = s_far.shape[0]
    ss, ts = s_far.shape[1] // SIZE, t_far.shape[1] // SIZE
    for at in strips(rows):
        for by in range(SIZE):
            outs[by][at, pl.ds(0, ss)] = scaled(s_far[at, part(places, by, ss)], inv_s[at, :])
            outs[by][at, pl.ds(ss, ts)] = scaled(t_far[at, part(places, by, ts)], inv_t[at, :])


def native_features(places, pack, half):
    ss = half // SIZE
    return pack[:, part(places, 0, ss)], pack[:, pl.ds(half, pack.shape[1] - half)]


def gram_kernel(share, chunk, places, *refs):
    native = chunk == 0
    count = SIZE if native else 2 * SIZE
    norms, packs = refs[:SIZE], refs[count - SIZE : count]
    outs, (left, right, product) = refs[count : count + SIZE], refs[count + SIZE :]
    half, feats = product.shape
    rows, ss = norms[0].shape[0], half // SIZE
    for k in range(SIZE):
        at = pl.ds(k * rows, rows)
        left[at, :] = norms[k][:, pl.ds(0, half)]
        if native:
            right[at, pl.ds(0, ss)], right[at, pl.ds(ss, feats - ss)] = native_features(
                places, packs[k], half
            )
        else:
            right[at, :] = packs[k][...]
    product[...] = lax.dot_general(
        left[...], right[...], (((0,), (0,)), ((), ())), preferred_element_type=F32
    )
    if native:
        row = lax.broadcasted_iota(jnp.int32, (ss, ss), 0)
        col = lax.broadcasted_iota(jnp.int32, (ss, ss), 1)
        product[part(places, 0, ss), pl.ds(0, ss)] -= jnp.where(row == col, share, 0.0)
    for by, out in enumerate(outs):
        which = lax.rem(places[1 + chunk] + by, SIZE)
        block = pl.ds(pl.multiple_of(which * ss, ss), ss)
        rest = pl.ds(ss, feats - ss)
        out[:, pl.ds(0, ss)] = product[block, pl.ds(0, ss)].astype(out.dtype)
        out[:, rest] = -product[block, rest].astype(out.dtype)


def gather_weights(place, pieces, weights):
    ss = pieces[0].shape[0]
    for by, piece in enumerate(pieces):
        which = lax.rem(place + SIZE - by, SIZE)
        weights[pl.ds(pl.multiple_of(which * ss, ss), ss), :] = piece[...]


def times(left, weights):
    return lax.dot_general(left, weights, (((1,), (1,)), ((), ())), preferred_element_type=F32)


def apply_native_kernel(places, *refs):
    packs, pieces, (out, left, weights) = refs[:SIZE], refs[SIZE : 2 * SIZE], refs[2 * SIZE :]
    half, feats = weights.shape
    rows, ss = packs[0].shape[0], half // SIZE
    gather_weights(places[1], pieces, weights)
    for k, pack in enumerate(packs):
        at = pl.ds(k * rows, rows)
        left[at, pl.ds(0, ss)], left[at, pl.ds(ss, feats - ss)] = native_features(
            places, pack, half
        )
    out[...] = times(left[...], weights[...])


def apply_far_kernel(first, count, places, *refs):
    packs, pieces, before = refs[:count], refs[count : count + SIZE], refs[count + SIZE]
    outs, weights = refs[count + SIZE + 1 : -1], refs[-1]
    rows = packs[0].shape[0]
    gather_weights(places[2], pieces, weights)
    for k, (pack, out) in enumerate(zip(packs, outs)):
        sofar = before[pl.ds((first + k) * rows, rows), :]
        out[...] = (times(pack[...], weights[...]) + sofar).astype(out.dtype)


def shapes(*described):
    return [jax.ShapeDtypeStruct(shape, dtype) for shape, dtype in described]


def kernel_call(kernel, name, outs, n_in, scratch=(), flops=0):
    return pl.pallas_call(
        kernel,
        out_shape=outs,
        in_specs=[SCALAR] + [WHOLE] * n_in,
        out_specs=[WHOLE] * len(outs),
        scratch_shapes=list(scratch),
        compiler_params=PARAMS,
        cost_estimate=pl.CostEstimate(flops=flops, bytes_accessed=4 << 20, transcendentals=0),
        name=name,
    )


def body(student, teacher):
    rows, half = student.shape
    wide = teacher.shape[1]
    width = 2 * half
    groups = lax.axis_size("loop") * lax.axis_size("rep")
    passages = rows * groups
    coef = 32.0 * width / (passages**0.5)
    level = passages / width
    ss, ts = half // SIZE, wide // SIZE
    feats = ss + ts
    flops = 2 * SIZE * rows * half * feats
    places = jnp.stack([place_along(axes) for axes in (GATHER, *FIRST)]).astype(jnp.int32)

    t_far, s_far = other_core(teacher), other_core(student)
    ssq_s, ssq_t = pl.pallas_call(
        sums_kernel,
        out_shape=shapes(*[((rows, 1), F32)] * 2),
        in_specs=[WHOLE] * 2,
        out_specs=[WHOLE] * 2,
        compiler_params=PARAMS,
        cost_estimate=pl.CostEstimate(flops=0, bytes_accessed=1 << 20, transcendentals=0),
        name="sums",
    )(student, teacher)
    *near, inv_s, inv_t = kernel_call(
        pack_own_kernel,
        "pack_own",
        shapes(*[((rows, half + ts), BF16)] * SIZE, *[((rows, 1), F32)] * 2),
        6,
    )(places, student, s_far, teacher, t_far, ssq_s, ssq_t)
    far = kernel_call(
        pack_far_kernel, "pack_far", shapes(*[((rows, feats), BF16)] * SIZE), 4
    )(places, s_far, t_far, inv_s, inv_t)
    norm_own = near[0][:, :half]

    def exchanged(own, sent, axis_of_core, sign=1):
        arrived = {by: shifted(sent(by), axis_of_core, sign * by) for by in ORDER}
        return [own] + [arrived[by] for by in (1, 2, 3)]

    def added(total, sent, axis_of_core, sign=1):
        for array in exchanged(None, sent, axis_of_core, sign)[1:]:
            total = total + array.astype(F32)
        return total

    near = exchanged(near[0], near.__getitem__, GATHER)
    far = exchanged(far[0], far.__getitem__, GATHER)

    def weights_of(chunk, packs, name):
        own, *sends = kernel_call(
            functools.partial(gram_kernel, level * SIZE / groups, chunk),
            name,
            shapes(((ss, feats), F32), *[((ss, feats), BF16)] * 3),
            len(packs),
            [
                pltpu.VMEM((SIZE * rows, half), BF16),
                pltpu.VMEM((SIZE * rows, feats), BF16),
                pltpu.VMEM((half, feats), F32),
            ],
            flops,
        )(places, *packs)
        total = added(own, lambda by: sends[by - 1], FIRST[chunk])
        for mask in PAIRS[chunk]:
            total = total + paired(total.astype(BF16), SECOND[chunk], mask).astype(F32)
        piece = total.astype(BF16)
        return exchanged(piece, lambda by: piece, FIRST[chunk])

    near_weights = weights_of(0, near, "gram_native")
    far_weights = weights_of(1, near + far, "gram_far")

    sofar = kernel_call(
        apply_native_kernel,
        "apply_native",
        shapes(((SIZE * rows, half), F32)),
        2 * SIZE,
        [pltpu.VMEM((SIZE * rows, feats), BF16), pltpu.VMEM((half, feats), BF16)],
        flops,
    )(places, *near, *near_weights)[0]
    def last_product(by, dtype, name):
        return kernel_call(
            functools.partial(apply_far_kernel, by, 1),
            name,
            shapes(((rows, half), dtype)),
            SIZE + 2,
            [pltpu.VMEM((half, feats), BF16)],
            flops // 4,
        )(places, far[by], *far_weights, sofar)[0]

    parts = {by: last_product(by, BF16, "apply_sent") for by in ORDER}
    grad_n = last_product(0, F32, "apply_kept")
    norm_f = norm_own.astype(F32)
    grad_n = grad_n + level * norm_f
    grad_n = coef * added(grad_n, parts.__getitem__, GATHER, -1)
    inner = jnp.sum(grad_n * norm_f, axis=1)
    inner = inner + other_core(inner)
    return (grad_n - inner[:, None] * norm_f) * inv_s


def solution(mesh):
    placed = (P(("loop", "rep"), "sec"), P(("loop", "rep"), "sec"))
    return jax.shard_map(
        body, mesh=mesh, in_specs=placed, out_specs=P(("loop", "rep"), "sec"), check_vma=False
    )
```

```python
import functools
import itertools

import jax
import jax.numpy as jnp
from jax import lax
from jax.experimental import pallas as pl
from jax.experimental.pallas import tpu as pltpu
from jax.sharding import PartitionSpec as P

AXES = ("loop", "rep", "sec")
X, Y, Z = 0, 1, 2
SIZE = 4
GATHER = (Y, X)
FIRST = ((X, Z), (Z, Y))
SECOND = ((Z, Y), (X, Z))
ORDER = (2, 1, 3)
STRIP = 32
LANES = 128
PARAMS = pltpu.CompilerParams(vmem_limit_bytes=40 * 1024 * 1024)
SCALAR = pl.BlockSpec(memory_space=pltpu.SMEM)
WHOLE = pl.BlockSpec(memory_space=pltpu.VMEM)
BF16, F32 = jnp.bfloat16, jnp.float32


def index_of(chip, core):
    x, y, z = chip
    return (((x // 2) * SIZE + z) * 8 + y * 2 + x % 2) * 2 + core


def shifted(array, axis_of_core, by):
    pairs = []
    for chip in itertools.product(range(SIZE), repeat=3):
        for core in range(2):
            target = list(chip)
            axis = axis_of_core[core]
            target[axis] = (target[axis] + by) % SIZE
            pairs.append((index_of(chip, core), index_of(target, core)))
    return lax.ppermute(array, AXES, pairs)


def other_core(array):
    return lax.ppermute(array, "sec", [(0, 1), (1, 0)])


def place_along(axis_of_core):
    loop, rep, core = (lax.axis_index(name) for name in AXES)
    place = ((loop // SIZE) * 2 + rep % 2, rep // 2, loop % SIZE)
    return jnp.where(core == 0, place[axis_of_core[0]], place[axis_of_core[1]])


def scaled(piece, inv):
    return (piece.astype(F32) * inv).astype(BF16)


def part(places, by, size):
    return pl.ds(pl.multiple_of(lax.rem(places[0] + by, SIZE) * size, size), size)


def squares(values):
    values = values.astype(F32)
    return jnp.sum(values * values, axis=1, keepdims=True)


def strips(rows):
    return [pl.ds(start, STRIP) for start in range(0, rows, STRIP)]


def sums_kernel(s_own, t_own, ssq_s, ssq_t):
    for at in strips(s_own.shape[0]):
        ssq_s[at, :] = squares(s_own[at, :])
        ssq_t[at, :] = squares(t_own[at, :])


def pack_own_kernel(places, s_far, t_own, t_far, ssq_s, ssq_t, *outs):
    rows, wide = t_own.shape
    ts = wide // SIZE
    inv_s, inv_t = outs[SIZE:]
    lane = lax.broadcasted_iota(jnp.int32, (STRIP, LANES), 1)
    for at in strips(rows):
        inv = lax.rsqrt(ssq_s[at, :] + squares(s_far[at, :]) + 1e-06)
        inv_s[at, :] = inv
        inv_t[at, :] = lax.rsqrt(ssq_t[at, :] + squares(t_far[at, :]) + 1e-06)
        terms = jnp.zeros((STRIP, LANES), F32)
        for i in range(3):
            term = inv.astype(BF16).astype(F32)
            terms = jnp.where(lane == i, term, terms)
            inv = inv - term
        for by in range(SIZE):
            outs[by][at, pl.ds(ts, LANES)] = terms.astype(BF16)
    for at in strips(rows):
        for by in range(SIZE):
            outs[by][at, pl.ds(0, ts)] = scaled(t_own[at, part(places, by, ts)], inv_t[at, :])


def pack_far_kernel(places, s_far, t_far, inv_s, inv_t, *outs):
    rows = s_far.shape[0]
    ss, ts = s_far.shape[1] // SIZE, t_far.shape[1] // SIZE
    for at in strips(rows):
        for by in range(SIZE):
            outs[by][at, pl.ds(0, ss)] = scaled(s_far[at, part(places, by, ss)], inv_s[at, :])
            outs[by][at, pl.ds(ss, ts)] = scaled(t_far[at, part(places, by, ts)], inv_t[at, :])


def emit(place, product, outs):
    half, feats = product.shape
    ss = half // SIZE
    rest = pl.ds(ss, feats - ss)
    for by, out in enumerate(outs):
        block = pl.ds(pl.multiple_of(lax.rem(place + by, SIZE) * ss, ss), ss)
        out[:, pl.ds(0, ss)] = product[block, pl.ds(0, ss)].astype(out.dtype)
        out[:, rest] = -product[block, rest].astype(out.dtype)


def cross(left, right):
    return lax.dot_general(
        left[...], right[...], (((0,), (0,)), ((), ())), preferred_element_type=F32
    )


def gram_native_kernel(share, places, *refs):
    students, packs = refs[:SIZE], refs[SIZE : 2 * SIZE]
    outs, (left, right, product) = refs[2 * SIZE : 3 * SIZE], refs[3 * SIZE :]
    half, feats = product.shape
    rows, ss = students[0].shape[0], half // SIZE
    ts = feats - ss
    for k in range(SIZE):
        at = pl.ds(k * rows, rows)
        terms = packs[k][:, pl.ds(ts, LANES)].astype(F32)
        inv = (terms[:, 0:1] + terms[:, 1:2]) + terms[:, 2:3]
        left[at, :] = scaled(students[k][...], inv)
        right[at, pl.ds(0, ss)] = left[at, part(places, 0, ss)]
        right[at, pl.ds(ss, ts)] = packs[k][:, pl.ds(0, ts)]
    product[...] = cross(left, right)
    row = lax.broadcasted_iota(jnp.int32, (ss, ss), 0)
    col = lax.broadcasted_iota(jnp.int32, (ss, ss), 1)
    product[part(places, 0, ss), pl.ds(0, ss)] -= jnp.where(row == col, share, 0.0)
    emit(places[1], product, outs)


def gram_far_kernel(places, left, *refs):
    packs, outs, (right, product) = refs[:SIZE], refs[SIZE : 2 * SIZE], refs[2 * SIZE :]
    rows = packs[0].shape[0]
    for k, pack in enumerate(packs):
        right[pl.ds(k * rows, rows), :] = pack[...]
    product[...] = cross(left, right)
    emit(places[2], product, outs)


def gather_weights(place, pieces, weights):
    ss = pieces[0].shape[0]
    for by, piece in enumerate(pieces):
        which = lax.rem(place + SIZE - by, SIZE)
        weights[pl.ds(pl.multiple_of(which * ss, ss), ss), :] = piece[...]


def times(left, weights):
    return lax.dot_general(left, weights, (((1,), (1,)), ((), ())), preferred_element_type=F32)


def apply_native_kernel(places, left, *refs):
    pieces, (out, weights) = refs[:SIZE], refs[SIZE:]
    gather_weights(places[1], pieces, weights)
    out[...] = times(left[...], weights[...])


def apply_far_kernel(first, count, places, *refs):
    packs, pieces, before = refs[:count], refs[count : count + SIZE], refs[count + SIZE]
    outs, weights = refs[count + SIZE + 1 : -1], refs[-1]
    rows = packs[0].shape[0]
    gather_weights(places[2], pieces, weights)
    for k, (pack, out) in enumerate(zip(packs, outs)):
        sofar = before[pl.ds((first + k) * rows, rows), :]
        out[...] = (times(pack[...], weights[...]) + sofar).astype(out.dtype)


def shapes(*described):
    return [jax.ShapeDtypeStruct(shape, dtype) for shape, dtype in described]


def kernel_call(kernel, name, outs, n_in, scratch=(), flops=0):
    return pl.pallas_call(
        kernel,
        out_shape=outs,
        in_specs=[SCALAR] + [WHOLE] * n_in,
        out_specs=[WHOLE] * len(outs),
        scratch_shapes=list(scratch),
        compiler_params=PARAMS,
        cost_estimate=pl.CostEstimate(flops=flops, bytes_accessed=4 << 20, transcendentals=0),
        name=name,
    )


def body(student, teacher):
    rows, half = student.shape
    wide = teacher.shape[1]
    width = 2 * half
    groups = lax.axis_size("loop") * lax.axis_size("rep")
    passages = rows * groups
    coef = 32.0 * width / (passages**0.5)
    level = passages / width
    ss, ts = half // SIZE, wide // SIZE
    feats = ss + ts
    flops = 2 * SIZE * rows * half * feats
    places = jnp.stack([place_along(axes) for axes in (GATHER, *FIRST)]).astype(jnp.int32)

    t_far, s_far = other_core(teacher), other_core(student)
    ssq_s, ssq_t = pl.pallas_call(
        sums_kernel,
        out_shape=shapes(*[((rows, 1), F32)] * 2),
        in_specs=[WHOLE] * 2,
        out_specs=[WHOLE] * 2,
        compiler_params=PARAMS,
        cost_estimate=pl.CostEstimate(flops=0, bytes_accessed=1 << 20, transcendentals=0),
        name="sums",
    )(student, teacher)
    *near, inv_s, inv_t = kernel_call(
        pack_own_kernel,
        "pack_own",
        shapes(*[((rows, ts + LANES), BF16)] * SIZE, *[((rows, 1), F32)] * 2),
        5,
    )(places, s_far, teacher, t_far, ssq_s, ssq_t)
    far = kernel_call(
        pack_far_kernel, "pack_far", shapes(*[((rows, feats), BF16)] * SIZE), 4
    )(places, s_far, t_far, inv_s, inv_t)

    def exchanged(own, sent, axis_of_core, sign=1):
        arrived = {by: shifted(sent(by), axis_of_core, sign * by) for by in ORDER}
        return [own] + [arrived[by] for by in (1, 2, 3)]

    def added(total, sent, axis_of_core, sign=1):
        for array in exchanged(None, sent, axis_of_core, sign)[1:]:
            total = total + array.astype(F32)
        return total

    students = exchanged(student, lambda by: student, GATHER)
    near = exchanged(near[0], near.__getitem__, GATHER)
    far = exchanged(far[0], far.__getitem__, GATHER)

    blocks = shapes(((ss, feats), F32), *[((ss, feats), BF16)] * 3)
    product = pltpu.VMEM((half, feats), F32)
    stacked = shapes(((SIZE * rows, half), BF16), ((SIZE * rows, feats), BF16))
    *near_blocks, norms, native = kernel_call(
        functools.partial(gram_native_kernel, level * SIZE / groups),
        "gram_native",
        blocks + stacked,
        2 * SIZE,
        [product],
        flops,
    )(places, *students, *near)
    far_blocks = kernel_call(
        gram_far_kernel,
        "gram_far",
        blocks,
        SIZE + 1,
        [pltpu.VMEM((SIZE * rows, feats), BF16), product],
        flops,
    )(places, norms, *far)

    def weights_of(chunk, own, *sends):
        total = added(own, lambda by: sends[by - 1], FIRST[chunk])
        shared = total.astype(BF16)
        piece = added(total, lambda by: shared, SECOND[chunk]).astype(BF16)
        return exchanged(piece, lambda by: piece, FIRST[chunk])

    near_weights = weights_of(0, *near_blocks)
    far_weights = weights_of(1, *far_blocks)

    sofar = kernel_call(
        apply_native_kernel,
        "apply_native",
        shapes(((SIZE * rows, half), F32)),
        SIZE + 1,
        [pltpu.VMEM((half, feats), BF16)],
        flops,
    )(places, native, *near_weights)[0]
    parts = kernel_call(
        functools.partial(apply_far_kernel, 1, SIZE - 1),
        "apply_sent",
        shapes(*[((rows, half), BF16)] * 3),
        2 * SIZE,
        [pltpu.VMEM((half, feats), BF16)],
        flops * 3 // 4,
    )(places, *far[1:], *far_weights, sofar)
    grad_n = kernel_call(
        functools.partial(apply_far_kernel, 0, 1),
        "apply_kept",
        shapes(((rows, half), F32)),
        SIZE + 2,
        [pltpu.VMEM((half, feats), BF16)],
        flops // 4,
    )(places, far[0], *far_weights, sofar)[0]
    norm_f = norms[:rows].astype(F32)
    grad_n = grad_n + level * norm_f
    grad_n = coef * added(grad_n, lambda by: parts[by - 1], GATHER, -1)
    inner = jnp.sum(grad_n * norm_f, axis=1)
    inner = inner + other_core(inner)
    return (grad_n - inner[:, None] * norm_f) * inv_s


def solution(mesh):
    placed = (P(("loop", "rep"), "sec"), P(("loop", "rep"), "sec"))
    return jax.shard_map(
        body, mesh=mesh, in_specs=placed, out_specs=P(("loop", "rep"), "sec"), check_vma=False
    )
```

```python
import functools
import itertools

import jax
import jax.numpy as jnp
from jax import lax
from jax.experimental import pallas as pl
from jax.experimental.pallas import tpu as pltpu
from jax.sharding import PartitionSpec as P

AXES = ("loop", "rep", "sec")
X, Y, Z = 0, 1, 2
SIZE = 4
GATHER = (Y, X)
FIRST = ((X, Z), (Z, Y))
SECOND = ((Z, Y), (X, Z))
ORDER = (2, 1, 3)
STRIP = 32
PARAMS = pltpu.CompilerParams(vmem_limit_bytes=40 * 1024 * 1024)
SCALAR = pl.BlockSpec(memory_space=pltpu.SMEM)
WHOLE = pl.BlockSpec(memory_space=pltpu.VMEM)
BF16, F32 = jnp.bfloat16, jnp.float32


def index_of(chip, core):
    x, y, z = chip
    return (((x // 2) * SIZE + z) * 8 + y * 2 + x % 2) * 2 + core


def shifted(array, axis_of_core, by):
    pairs = []
    for chip in itertools.product(range(SIZE), repeat=3):
        for core in range(2):
            target = list(chip)
            axis = axis_of_core[core]
            target[axis] = (target[axis] + by) % SIZE
            pairs.append((index_of(chip, core), index_of(target, core)))
    return lax.ppermute(array, AXES, pairs)


def other_core(array):
    return lax.ppermute(array, "sec", [(0, 1), (1, 0)])


def place_along(axis_of_core):
    loop, rep, core = (lax.axis_index(name) for name in AXES)
    place = ((loop // SIZE) * 2 + rep % 2, rep // 2, loop % SIZE)
    return jnp.where(core == 0, place[axis_of_core[0]], place[axis_of_core[1]])


def scaled(piece, inv):
    return (piece.astype(F32) * inv).astype(BF16)


def part(places, by, size):
    return pl.ds(pl.multiple_of(lax.rem(places[0] + by, SIZE) * size, size), size)


def squares(values):
    values = values.astype(F32)
    return jnp.sum(values * values, axis=1, keepdims=True)


def strips(rows):
    return [pl.ds(start, STRIP) for start in range(0, rows, STRIP)]


def sums_kernel(s_own, t_own, ssq_s, ssq_t):
    for at in strips(s_own.shape[0]):
        ssq_s[at, :] = squares(s_own[at, :])
        ssq_t[at, :] = squares(t_own[at, :])


def pack_own_kernel(places, s_own, s_far, t_own, t_far, ssq_s, ssq_t, *outs):
    rows, half = s_own.shape
    ts = t_own.shape[1] // SIZE
    inv_s, inv_t = outs[SIZE:]
    for at in strips(rows):
        inv_s[at, :] = lax.rsqrt(ssq_s[at, :] + squares(s_far[at, :]) + 1e-06)
        inv_t[at, :] = lax.rsqrt(ssq_t[at, :] + squares(t_far[at, :]) + 1e-06)
    for at in strips(rows):
        norm = scaled(s_own[at, :], inv_s[at, :])
        for by in range(SIZE):
            outs[by][at, pl.ds(0, half)] = norm
            outs[by][at, pl.ds(half, ts)] = scaled(t_own[at, part(places, by, ts)], inv_t[at, :])


def pack_far_kernel(places, s_far, t_far, inv_s, inv_t, *outs):
    rows = s_far.shape[0]
    ss, ts = s_far.shape[1] // SIZE, t_far.shape[1] // SIZE
    for at in strips(rows):
        for by in range(SIZE):
            outs[by][at, pl.ds(0, ss)] = scaled(s_far[at, part(places, by, ss)], inv_s[at, :])
            outs[by][at, pl.ds(ss, ts)] = scaled(t_far[at, part(places, by, ts)], inv_t[at, :])


def native_features(places, pack, half):
    ss = half // SIZE
    return pack[:, part(places, 0, ss)], pack[:, pl.ds(half, pack.shape[1] - half)]


def stack(places, norms, packs, left, right, native):
    rows = norms[0].shape[0]
    half, feats = left.shape[1], right.shape[1]
    ss = half // SIZE
    for k, (norm, pack) in enumerate(zip(norms, packs)):
        at = pl.ds(k * rows, rows)
        left[at, :] = norm[:, pl.ds(0, half)]
        if native:
            right[at, pl.ds(0, ss)], right[at, pl.ds(ss, feats - ss)] = native_features(
                places, pack, half
            )
        else:
            right[at, :] = pack[...]


def cross(left, right):
    return lax.dot_general(
        left[...], right[...], (((0,), (0,)), ((), ())), preferred_element_type=F32
    )


def emit(place, product, outs):
    half, feats = product.shape
    ss = half // SIZE
    rest = pl.ds(ss, feats - ss)
    for by, out in enumerate(outs):
        block = pl.ds(pl.multiple_of(lax.rem(place + by, SIZE) * ss, ss), ss)
        out[:, pl.ds(0, ss)] = product[block, pl.ds(0, ss)].astype(out.dtype)
        out[:, rest] = -product[block, rest].astype(out.dtype)


def gram_early_kernel(places, *refs):
    packs, (product, left, right) = refs[:-3], refs[-3:]
    stack(places, packs, packs, left, right, True)
    product[...] = cross(left, right)


def gram_native_kernel(share, places, pack, before, *refs):
    outs, (left, right, product) = refs[:SIZE], refs[SIZE:]
    ss = left.shape[1] // SIZE
    stack(places, [pack], [pack], left, right, True)
    product[...] = before[...] + cross(left, right)
    row = lax.broadcasted_iota(jnp.int32, (ss, ss), 0)
    col = lax.broadcasted_iota(jnp.int32, (ss, ss), 1)
    product[part(places, 0, ss), pl.ds(0, ss)] -= jnp.where(row == col, share, 0.0)
    emit(places[1], product, outs)


def gram_far_kernel(places, *refs):
    norms, packs, outs = refs[:SIZE], refs[SIZE : 2 * SIZE], refs[2 * SIZE : 3 * SIZE]
    left, right, product = refs[3 * SIZE :]
    stack(places, norms, packs, left, right, False)
    product[...] = cross(left, right)
    emit(places[2], product, outs)


def gather_weights(place, pieces, weights):
    ss = pieces[0].shape[0]
    for by, piece in enumerate(pieces):
        which = lax.rem(place + SIZE - by, SIZE)
        weights[pl.ds(pl.multiple_of(which * ss, ss), ss), :] = piece[...]


def times(left, weights):
    return lax.dot_general(left, weights, (((1,), (1,)), ((), ())), preferred_element_type=F32)


def apply_native_kernel(places, *refs):
    packs, pieces, (out, left, weights) = refs[:SIZE], refs[SIZE : 2 * SIZE], refs[2 * SIZE :]
    half, feats = weights.shape
    rows, ss = packs[0].shape[0], half // SIZE
    gather_weights(places[1], pieces, weights)
    for k, pack in enumerate(packs):
        at = pl.ds(k * rows, rows)
        left[at, pl.ds(0, ss)], left[at, pl.ds(ss, feats - ss)] = native_features(
            places, pack, half
        )
    out[...] = times(left[...], weights[...])


def apply_early_kernel(places, far1, far2, far3, piece0, piece1, piece2, before, *refs):
    outs, (left, weights) = refs[: SIZE - 1], refs[SIZE - 1 :]
    rows = far1.shape[0]
    last = jnp.zeros(piece0.shape, piece0.dtype)
    gather_weights(places[2], (piece0, piece1, piece2, last), weights)
    for k, pack in enumerate((far1, far2, far3)):
        left[pl.ds(k * rows, rows), :] = pack[...]
    product = times(left[...], weights[...])
    for k, out in enumerate(outs):
        sofar = before[pl.ds((k + 1) * rows, rows), :]
        out[...] = (product[k * rows : (k + 1) * rows] + sofar).astype(out.dtype)


def apply_sent_kernel(places, far1, far2, far3, piece, before, early1, early2, early3, *outs):
    rows, ss = far1.shape[0], piece.shape[0]
    which = lax.rem(places[2] + 1, SIZE)
    block = pl.ds(pl.multiple_of(which * ss, ss), ss)
    for k, (pack, early, out) in enumerate(
        zip((far1, far2, far3), (early1, early2, early3), outs)
    ):
        out[...] = early[...]
        sofar = before[pl.ds((k + 1) * rows, rows), block]
        out[:, block] = (times(pack[...], piece[...]) + sofar).astype(out.dtype)


def apply_kept_kernel(places, pack, *refs):
    pieces, (before, out, weights) = refs[:SIZE], refs[SIZE:]
    gather_weights(places[2], pieces, weights)
    out[...] = times(pack[...], weights[...]) + before[pl.ds(0, pack.shape[0]), :]


def shapes(*described):
    return [jax.ShapeDtypeStruct(shape, dtype) for shape, dtype in described]


def kernel_call(kernel, name, outs, n_in, scratch=(), flops=0):
    return pl.pallas_call(
        kernel,
        out_shape=outs,
        in_specs=[SCALAR] + [WHOLE] * n_in,
        out_specs=[WHOLE] * len(outs),
        scratch_shapes=list(scratch),
        compiler_params=PARAMS,
        cost_estimate=pl.CostEstimate(flops=flops, bytes_accessed=4 << 20, transcendentals=0),
        name=name,
    )


def body(student, teacher):
    rows, half = student.shape
    wide = teacher.shape[1]
    width = 2 * half
    groups = lax.axis_size("loop") * lax.axis_size("rep")
    passages = rows * groups
    coef = 32.0 * width / (passages**0.5)
    level = passages / width
    ss, ts = half // SIZE, wide // SIZE
    feats = ss + ts
    flops = 2 * SIZE * rows * half * feats
    places = jnp.stack([place_along(axes) for axes in (GATHER, *FIRST)]).astype(jnp.int32)

    t_far, s_far = other_core(teacher), other_core(student)
    ssq_s, ssq_t = pl.pallas_call(
        sums_kernel,
        out_shape=shapes(*[((rows, 1), F32)] * 2),
        in_specs=[WHOLE] * 2,
        out_specs=[WHOLE] * 2,
        compiler_params=PARAMS,
        cost_estimate=pl.CostEstimate(flops=0, bytes_accessed=1 << 20, transcendentals=0),
        name="sums",
    )(student, teacher)
    *near, inv_s, inv_t = kernel_call(
        pack_own_kernel,
        "pack_own",
        shapes(*[((rows, half + ts), BF16)] * SIZE, *[((rows, 1), F32)] * 2),
        6,
    )(places, student, s_far, teacher, t_far, ssq_s, ssq_t)
    far = kernel_call(
        pack_far_kernel, "pack_far", shapes(*[((rows, feats), BF16)] * SIZE), 4
    )(places, s_far, t_far, inv_s, inv_t)
    norm_own = near[0][:, :half]

    def exchanged(own, sent, axis_of_core, sign=1):
        arrived = {by: shifted(sent(by), axis_of_core, sign * by) for by in ORDER}
        return [own] + [arrived[by] for by in (1, 2, 3)]

    def added(total, sent, axis_of_core, sign=1):
        for array in exchanged(None, sent, axis_of_core, sign)[1:]:
            total = total + array.astype(F32)
        return total

    near = exchanged(near[0], near.__getitem__, GATHER)
    far = exchanged(far[0], far.__getitem__, GATHER)

    blocks = shapes(((ss, feats), F32), *[((ss, feats), BF16)] * 3)
    product = pltpu.VMEM((half, feats), F32)

    def operands(count):
        return [pltpu.VMEM((count * rows, half), BF16), pltpu.VMEM((count * rows, feats), BF16)]

    early = kernel_call(
        gram_early_kernel, "gram_early", shapes(((half, feats), F32)), 3, operands(3), flops
    )(places, *near[:3])[0]
    near_blocks = kernel_call(
        functools.partial(gram_native_kernel, level * SIZE / groups),
        "gram_native",
        blocks,
        2,
        operands(1) + [product],
        flops // 4,
    )(places, near[3], early)
    far_blocks = kernel_call(
        gram_far_kernel, "gram_far", blocks, 2 * SIZE, operands(SIZE) + [product], flops
    )(places, *near, *far)

    def weights_of(chunk, own, *sends):
        total = added(own, lambda by: sends[by - 1], FIRST[chunk])
        shared = total.astype(BF16)
        piece = added(total, lambda by: shared, SECOND[chunk]).astype(BF16)
        return exchanged(piece, lambda by: piece, FIRST[chunk])

    near_weights = weights_of(0, *near_blocks)
    far_weights = weights_of(1, *far_blocks)

    sofar = kernel_call(
        apply_native_kernel,
        "apply_native",
        shapes(((SIZE * rows, half), F32)),
        2 * SIZE,
        [pltpu.VMEM((SIZE * rows, feats), BF16), pltpu.VMEM((half, feats), BF16)],
        flops,
    )(places, *near, *near_weights)[0]
    messages = shapes(*[((rows, half), BF16)] * 3)
    weights = pltpu.VMEM((half, feats), BF16)
    most = kernel_call(
        apply_early_kernel,
        "apply_early",
        messages,
        7,
        [pltpu.VMEM((3 * rows, feats), BF16), weights],
        flops * 3 // 4,
    )(places, *far[1:], *far_weights[:3], sofar)
    parts = kernel_call(apply_sent_kernel, "apply_sent", messages, 8, (), flops // 4)(
        places, *far[1:], far_weights[3], sofar, *most
    )
    grad_n = kernel_call(
        apply_kept_kernel, "apply_kept", shapes(((rows, half), F32)), SIZE + 2, [weights], flops // 4
    )(places, far[0], *far_weights, sofar)[0]
    norm_f = norm_own.astype(F32)
    grad_n = grad_n + level * norm_f
    grad_n = coef * added(grad_n, lambda by: parts[by - 1], GATHER, -1)
    inner = jnp.sum(grad_n * norm_f, axis=1)
    inner = inner + other_core(inner)
    return (grad_n - inner[:, None] * norm_f) * inv_s


def solution(mesh):
    placed = (P(("loop", "rep"), "sec"), P(("loop", "rep"), "sec"))
    return jax.shard_map(
        body, mesh=mesh, in_specs=placed, out_specs=P(("loop", "rep"), "sec"), check_vma=False
    )
```

```python
import functools
import itertools

import jax
import jax.numpy as jnp
from jax import lax
from jax.experimental import pallas as pl
from jax.experimental.pallas import tpu as pltpu
from jax.sharding import PartitionSpec as P

AXES = ("loop", "rep", "sec")
X, Y, Z = 0, 1, 2
SIZE = 4
GATHER = (Y, X)
FIRST = ((X, Z), (Z, Y))
SECOND = ((Z, Y), (X, Z))
ORDER = (2, 1, 3)
STRIP = 32
PARAMS = pltpu.CompilerParams(vmem_limit_bytes=40 * 1024 * 1024)
SCALAR = pl.BlockSpec(memory_space=pltpu.SMEM)
WHOLE = pl.BlockSpec(memory_space=pltpu.VMEM)
BF16, F32 = jnp.bfloat16, jnp.float32


def index_of(chip, core):
    x, y, z = chip
    return (((x // 2) * SIZE + z) * 8 + y * 2 + x % 2) * 2 + core


def shifted(array, axis_of_core, by):
    pairs = []
    for chip in itertools.product(range(SIZE), repeat=3):
        for core in range(2):
            target = list(chip)
            axis = axis_of_core[core]
            target[axis] = (target[axis] + by) % SIZE
            pairs.append((index_of(chip, core), index_of(target, core)))
    return lax.ppermute(array, AXES, pairs)


def other_core(array):
    return lax.ppermute(array, "sec", [(0, 1), (1, 0)])


def place_along(axis_of_core):
    loop, rep, core = (lax.axis_index(name) for name in AXES)
    place = ((loop // SIZE) * 2 + rep % 2, rep // 2, loop % SIZE)
    return jnp.where(core == 0, place[axis_of_core[0]], place[axis_of_core[1]])


def scaled(piece, inv):
    return (piece.astype(F32) * inv).astype(BF16)


def part(places, by, size):
    return pl.ds(pl.multiple_of(lax.rem(places[0] + by, SIZE) * size, size), size)


def squares(values):
    values = values.astype(F32)
    return jnp.sum(values * values, axis=1, keepdims=True)


def strips(rows):
    return [pl.ds(start, STRIP) for start in range(0, rows, STRIP)]


def sums_kernel(s_own, t_own, ssq_s, ssq_t):
    for at in strips(s_own.shape[0]):
        ssq_s[at, :] = squares(s_own[at, :])
        ssq_t[at, :] = squares(t_own[at, :])


def pack_own_kernel(places, s_own, s_far, t_own, t_far, ssq_s, ssq_t, *outs):
    rows, half = s_own.shape
    ts = t_own.shape[1] // SIZE
    inv_s, inv_t = outs[SIZE:]
    for at in strips(rows):
        inv_s[at, :] = lax.rsqrt(ssq_s[at, :] + squares(s_far[at, :]) + 1e-06)
        inv_t[at, :] = lax.rsqrt(ssq_t[at, :] + squares(t_far[at, :]) + 1e-06)
    for at in strips(rows):
        norm = scaled(s_own[at, :], inv_s[at, :])
        for by in range(SIZE):
            outs[by][at, pl.ds(0, half)] = norm
            outs[by][at, pl.ds(half, ts)] = scaled(t_own[at, part(places, by, ts)], inv_t[at, :])


def pack_far_kernel(places, s_far, t_far, inv_s, inv_t, *outs):
    rows = s_far.shape[0]
    ss, ts = s_far.shape[1] // SIZE, t_far.shape[1] // SIZE
    for at in strips(rows):
        for by in range(SIZE):
            outs[by][at, pl.ds(0, ss)] = scaled(s_far[at, part(places, by, ss)], inv_s[at, :])
            outs[by][at, pl.ds(ss, ts)] = scaled(t_far[at, part(places, by, ts)], inv_t[at, :])


def native_features(places, pack, half):
    ss = half // SIZE
    return pack[:, part(places, 0, ss)], pack[:, pl.ds(half, pack.shape[1] - half)]


def stack(places, chunk, norms, packs, left, right):
    native = chunk == 0
    rows = norms[0].shape[0]
    half, feats = left.shape[1], right.shape[1]
    ss = half // SIZE
    for k, (norm, pack) in enumerate(zip(norms, packs)):
        at = pl.ds(k * rows, rows)
        for by in range(SIZE):
            which = lax.rem(places[1 + chunk] + by, SIZE)
            block = pl.ds(pl.multiple_of(which * ss, ss), ss)
            left[at, pl.ds(by * ss, ss)] = norm[:, block]
        if native:
            right[at, pl.ds(0, ss)], right[at, pl.ds(ss, feats - ss)] = native_features(
                places, pack, half
            )
        else:
            right[at, :] = pack[...]


def cross(left, right):
    return lax.dot_general(
        left[...], right[...], (((0,), (0,)), ((), ())), preferred_element_type=F32
    )


def emit(product, outs):
    half, feats = product.shape
    ss = half // SIZE
    for by, out in enumerate(outs):
        rows = product[by * ss : (by + 1) * ss]
        out[:, pl.ds(0, ss)] = rows[:, :ss].astype(out.dtype)
        out[:, pl.ds(ss, feats - ss)] = -rows[:, ss:].astype(out.dtype)


def gram_early_kernel(share, places, *refs):
    packs, (product, left, right) = refs[:-3], refs[-3:]
    stack(places, 0, packs, packs, left, right)
    product[...] = cross(left, right)
    ss = product.shape[0] // SIZE
    row = lax.broadcasted_iota(jnp.int32, (ss, ss), 0)
    col = lax.broadcasted_iota(jnp.int32, (ss, ss), 1)
    by = lax.rem(places[0] + SIZE - places[1], SIZE)
    block = pl.ds(pl.multiple_of(by * ss, ss), ss)
    product[block, pl.ds(0, ss)] -= jnp.where(row == col, share, 0.0)


def gram_native_kernel(places, pack, before, *refs):
    outs, (left, right) = refs[:SIZE], refs[SIZE:]
    stack(places, 0, [pack], [pack], left, right)
    emit(before[...] + cross(left, right), outs)


def gram_far_kernel(places, *refs):
    norms, packs, outs = refs[:SIZE], refs[SIZE : 2 * SIZE], refs[2 * SIZE : 3 * SIZE]
    left, right = refs[3 * SIZE :]
    stack(places, 1, norms, packs, left, right)
    emit(cross(left, right), outs)


def gather_weights(place, pieces, weights):
    ss = pieces[0].shape[0]
    for by, piece in enumerate(pieces):
        which = lax.rem(place + SIZE - by, SIZE)
        weights[pl.ds(pl.multiple_of(which * ss, ss), ss), :] = piece[...]


def times(left, weights):
    return lax.dot_general(left, weights, (((1,), (1,)), ((), ())), preferred_element_type=F32)


def apply_native_kernel(places, *refs):
    packs, pieces, (out, left, weights) = refs[:SIZE], refs[SIZE : 2 * SIZE], refs[2 * SIZE :]
    half, feats = weights.shape
    rows, ss = packs[0].shape[0], half // SIZE
    gather_weights(places[1], pieces, weights)
    for k, pack in enumerate(packs):
        at = pl.ds(k * rows, rows)
        left[at, pl.ds(0, ss)], left[at, pl.ds(ss, feats - ss)] = native_features(
            places, pack, half
        )
    out[...] = times(left[...], weights[...])


def apply_early_kernel(places, far1, far2, far3, piece0, piece1, piece2, before, *refs):
    outs, (left, weights) = refs[: SIZE - 1], refs[SIZE - 1 :]
    rows = far1.shape[0]
    last = jnp.zeros(piece0.shape, piece0.dtype)
    gather_weights(places[2], (piece0, piece1, piece2, last), weights)
    for k, pack in enumerate((far1, far2, far3)):
        left[pl.ds(k * rows, rows), :] = pack[...]
    product = times(left[...], weights[...])
    for k, out in enumerate(outs):
        sofar = before[pl.ds((k + 1) * rows, rows), :]
        out[...] = (product[k * rows : (k + 1) * rows] + sofar).astype(out.dtype)


def apply_sent_kernel(places, left, piece, before, early1, early2, early3, *outs):
    rows, ss = outs[0].shape[0], piece.shape[0]
    which = lax.rem(places[2] + 1, SIZE)
    block = pl.ds(pl.multiple_of(which * ss, ss), ss)
    product = times(left[...], piece[...])
    for k, out in enumerate(outs):
        sofar = before[pl.ds((k + 1) * rows, rows), block]
        out[:, block] = (product[k * rows : (k + 1) * rows] + sofar).astype(out.dtype)


def apply_kept_kernel(places, pack, *refs):
    pieces, (before, out, weights) = refs[:SIZE], refs[SIZE:]
    gather_weights(places[2], pieces, weights)
    out[...] = times(pack[...], weights[...]) + before[pl.ds(0, pack.shape[0]), :]


def shapes(*described):
    return [jax.ShapeDtypeStruct(shape, dtype) for shape, dtype in described]


def kernel_call(kernel, name, outs, n_in, scratch=(), flops=0, aliases=None):
    return pl.pallas_call(
        kernel,
        out_shape=outs,
        in_specs=[SCALAR] + [WHOLE] * n_in,
        out_specs=[WHOLE] * len(outs),
        scratch_shapes=list(scratch),
        input_output_aliases=aliases or {},
        compiler_params=PARAMS,
        cost_estimate=pl.CostEstimate(flops=flops, bytes_accessed=4 << 20, transcendentals=0),
        name=name,
    )


def body(student, teacher):
    rows, half = student.shape
    wide = teacher.shape[1]
    width = 2 * half
    groups = lax.axis_size("loop") * lax.axis_size("rep")
    passages = rows * groups
    coef = 32.0 * width / (passages**0.5)
    level = passages / width
    ss, ts = half // SIZE, wide // SIZE
    feats = ss + ts
    flops = 2 * SIZE * rows * half * feats
    places = jnp.stack([place_along(axes) for axes in (GATHER, *FIRST)]).astype(jnp.int32)

    t_far, s_far = other_core(teacher), other_core(student)
    ssq_s, ssq_t = pl.pallas_call(
        sums_kernel,
        out_shape=shapes(*[((rows, 1), F32)] * 2),
        in_specs=[WHOLE] * 2,
        out_specs=[WHOLE] * 2,
        compiler_params=PARAMS,
        cost_estimate=pl.CostEstimate(flops=0, bytes_accessed=1 << 20, transcendentals=0),
        name="sums",
    )(student, teacher)
    *near, inv_s, inv_t = kernel_call(
        pack_own_kernel,
        "pack_own",
        shapes(*[((rows, half + ts), BF16)] * SIZE, *[((rows, 1), F32)] * 2),
        6,
    )(places, student, s_far, teacher, t_far, ssq_s, ssq_t)
    far = kernel_call(
        pack_far_kernel, "pack_far", shapes(*[((rows, feats), BF16)] * SIZE), 4
    )(places, s_far, t_far, inv_s, inv_t)
    norm_own = near[0][:, :half]

    def exchanged(own, sent, axis_of_core, sign=1):
        arrived = {by: shifted(sent(by), axis_of_core, sign * by) for by in ORDER}
        return [own] + [arrived[by] for by in (1, 2, 3)]

    def added(total, sent, axis_of_core, sign=1):
        for array in exchanged(None, sent, axis_of_core, sign)[1:]:
            total = total + array.astype(F32)
        return total

    near = exchanged(near[0], near.__getitem__, GATHER)
    far = exchanged(far[0], far.__getitem__, GATHER)

    blocks = shapes(((ss, feats), F32), *[((ss, feats), BF16)] * 3)

    def operands(count):
        return [pltpu.VMEM((count * rows, half), BF16), pltpu.VMEM((count * rows, feats), BF16)]

    early = kernel_call(
        functools.partial(gram_early_kernel, level * SIZE / groups),
        "gram_early",
        shapes(((half, feats), F32)),
        3,
        operands(3),
        flops,
    )(places, *near[:3])[0]
    near_blocks = kernel_call(
        gram_native_kernel, "gram_native", blocks, 2, operands(1), flops // 4
    )(places, near[3], early)
    far_blocks = kernel_call(
        gram_far_kernel, "gram_far", blocks, 2 * SIZE, operands(SIZE), flops
    )(places, *near, *far)

    def weights_of(chunk, own, *sends):
        total = added(own, lambda by: sends[by - 1], FIRST[chunk])
        shared = total.astype(BF16)
        piece = added(total, lambda by: shared, SECOND[chunk]).astype(BF16)
        return exchanged(piece, lambda by: piece, FIRST[chunk])

    near_weights = weights_of(0, *near_blocks)
    far_weights = weights_of(1, *far_blocks)

    sofar = kernel_call(
        apply_native_kernel,
        "apply_native",
        shapes(((SIZE * rows, half), F32)),
        2 * SIZE,
        [pltpu.VMEM((SIZE * rows, feats), BF16), pltpu.VMEM((half, feats), BF16)],
        flops,
    )(places, *near, *near_weights)[0]
    messages = shapes(*[((rows, half), BF16)] * 3)
    weights = pltpu.VMEM((half, feats), BF16)
    *most, stacked = kernel_call(
        apply_early_kernel,
        "apply_early",
        messages + shapes(((3 * rows, feats), BF16)),
        7,
        [weights],
        flops * 3 // 4,
    )(places, *far[1:], *far_weights[:3], sofar)
    parts = kernel_call(
        apply_sent_kernel,
        "apply_sent",
        messages,
        6,
        (),
        flops // 4,
        {4 + k: k for k in range(3)},
    )(places, stacked, far_weights[3], sofar, *most)
    grad_n = kernel_call(
        apply_kept_kernel, "apply_kept", shapes(((rows, half), F32)), SIZE + 2, [weights], flops // 4
    )(places, far[0], *far_weights, sofar)[0]
    norm_f = norm_own.astype(F32)
    grad_n = grad_n + level * norm_f
    grad_n = coef * added(grad_n, lambda by: parts[by - 1], GATHER, -1)
    inner = jnp.sum(grad_n * norm_f, axis=1)
    inner = inner + other_core(inner)
    return (grad_n - inner[:, None] * norm_f) * inv_s


def solution(mesh):
    placed = (P(("loop", "rep"), "sec"), P(("loop", "rep"), "sec"))
    return jax.shard_map(
        body, mesh=mesh, in_specs=placed, out_specs=P(("loop", "rep"), "sec"), check_vma=False
    )
```

```python
import functools
import itertools

import jax
import jax.numpy as jnp
from jax import lax
from jax.experimental import pallas as pl
from jax.experimental.pallas import tpu as pltpu
from jax.sharding import PartitionSpec as P

AXES = ("loop", "rep", "sec")
X, Y, Z = 0, 1, 2
SIZE = 4
GATHER = (Y, X)
FIRST = ((X, Z), (Z, Y))
SECOND = ((Z, Y), (X, Z))
ORDER = (2, 1, 3)
STRIP = 32
PARAMS = pltpu.CompilerParams(vmem_limit_bytes=40 * 1024 * 1024)
WHOLE = pl.BlockSpec(memory_space=pltpu.VMEM)
BF16, F32 = jnp.bfloat16, jnp.float32


def index_of(chip, core):
    x, y, z = chip
    return (((x // 2) * SIZE + z) * 8 + y * 2 + x % 2) * 2 + core


def shifted(array, axis_of_core, by):
    pairs = []
    for chip in itertools.product(range(SIZE), repeat=3):
        for core in range(2):
            target = list(chip)
            axis = axis_of_core[core]
            target[axis] = (target[axis] + by) % SIZE
            pairs.append((index_of(chip, core), index_of(target, core)))
    return lax.ppermute(array, AXES, pairs)


def other_core(array):
    return lax.ppermute(array, "sec", [(0, 1), (1, 0)])


def places_here():
    loop, rep, core = (lax.axis_index(name) for name in AXES)
    chip = (lax.div(loop, SIZE) * 2 + lax.rem(rep, 2), lax.div(rep, 2), lax.rem(loop, SIZE))
    return [jnp.where(core == 0, chip[axes[0]], chip[axes[1]]) for axes in (GATHER, *FIRST)]


def scaled(piece, inv):
    return (piece.astype(F32) * inv).astype(BF16)


def part(places, by, size):
    return pl.ds(pl.multiple_of(lax.rem(places[0] + by, SIZE) * size, size), size)


def squares(values):
    values = values.astype(F32)
    return jnp.sum(values * values, axis=1, keepdims=True)


def strips(rows):
    return [pl.ds(start, STRIP) for start in range(0, rows, STRIP)]


def sums_kernel(s_own, t_own, ssq_s, ssq_t):
    for at in strips(s_own.shape[0]):
        ssq_s[at, :] = squares(s_own[at, :])
        ssq_t[at, :] = squares(t_own[at, :])


def pack_own_kernel(s_own, s_far, t_own, t_far, ssq_s, ssq_t, *outs):
    places = places_here()
    rows, half = s_own.shape
    ts = t_own.shape[1] // SIZE
    inv_s, inv_t = outs[SIZE:]
    for at in strips(rows):
        inv_s[at, :] = lax.rsqrt(ssq_s[at, :] + squares(s_far[at, :]) + 1e-06)
        inv_t[at, :] = lax.rsqrt(ssq_t[at, :] + squares(t_far[at, :]) + 1e-06)
    for at in strips(rows):
        norm = scaled(s_own[at, :], inv_s[at, :])
        for by in range(SIZE):
            outs[by][at, pl.ds(0, half)] = norm
            outs[by][at, pl.ds(half, ts)] = scaled(t_own[at, part(places, by, ts)], inv_t[at, :])


def pack_far_kernel(s_far, t_far, inv_s, inv_t, *outs):
    places = places_here()
    rows = s_far.shape[0]
    ss, ts = s_far.shape[1] // SIZE, t_far.shape[1] // SIZE
    for at in strips(rows):
        for by in range(SIZE):
            outs[by][at, pl.ds(0, ss)] = scaled(s_far[at, part(places, by, ss)], inv_s[at, :])
            outs[by][at, pl.ds(ss, ts)] = scaled(t_far[at, part(places, by, ts)], inv_t[at, :])


def native_features(places, pack, half):
    ss = half // SIZE
    return pack[:, part(places, 0, ss)], pack[:, pl.ds(half, pack.shape[1] - half)]


def stack(places, chunk, norms, packs, left, right):
    native = chunk == 0
    rows = norms[0].shape[0]
    half, feats = left.shape[1], right.shape[1]
    ss = half // SIZE
    for k, (norm, pack) in enumerate(zip(norms, packs)):
        at = pl.ds(k * rows, rows)
        for by in range(SIZE):
            which = lax.rem(places[1 + chunk] + by, SIZE)
            block = pl.ds(pl.multiple_of(which * ss, ss), ss)
            left[at, pl.ds(by * ss, ss)] = norm[:, block]
        if native:
            right[at, pl.ds(0, ss)], right[at, pl.ds(ss, feats - ss)] = native_features(
                places, pack, half
            )
        else:
            right[at, :] = pack[...]


def cross(left, right):
    return lax.dot_general(
        left[...], right[...], (((0,), (0,)), ((), ())), preferred_element_type=F32
    )


def emit(product, outs):
    half, feats = product.shape
    ss = half // SIZE
    for by, out in enumerate(outs):
        rows = product[by * ss : (by + 1) * ss]
        out[:, pl.ds(0, ss)] = rows[:, :ss].astype(out.dtype)
        out[:, pl.ds(ss, feats - ss)] = -rows[:, ss:].astype(out.dtype)


def gram_early_kernel(share, *refs):
    places = places_here()
    packs, (product, left, right) = refs[:-3], refs[-3:]
    stack(places, 0, packs, packs, left, right)
    product[...] = cross(left, right)
    ss = product.shape[0] // SIZE
    row = lax.broadcasted_iota(jnp.int32, (ss, ss), 0)
    col = lax.broadcasted_iota(jnp.int32, (ss, ss), 1)
    by = lax.rem(places[0] + SIZE - places[1], SIZE)
    block = pl.ds(pl.multiple_of(by * ss, ss), ss)
    product[block, pl.ds(0, ss)] -= jnp.where(row == col, share, 0.0)


def gram_native_kernel(pack, before, *refs):
    places = places_here()
    outs, (left, right) = refs[:SIZE], refs[SIZE:]
    stack(places, 0, [pack], [pack], left, right)
    emit(before[...] + cross(left, right), outs)


def gram_far_kernel(*refs):
    places = places_here()
    norms, packs, outs = refs[:SIZE], refs[SIZE : 2 * SIZE], refs[2 * SIZE : 3 * SIZE]
    left, right = refs[3 * SIZE :]
    stack(places, 1, norms, packs, left, right)
    emit(cross(left, right), outs)


def gather_weights(place, pieces, weights):
    ss = pieces[0].shape[0]
    for by, piece in enumerate(pieces):
        which = lax.rem(place + SIZE - by, SIZE)
        weights[pl.ds(pl.multiple_of(which * ss, ss), ss), :] = piece[...]


def times(left, weights):
    return lax.dot_general(left, weights, (((1,), (1,)), ((), ())), preferred_element_type=F32)


def apply_native_kernel(*refs):
    places = places_here()
    packs, pieces, (out, left, weights) = refs[:SIZE], refs[SIZE : 2 * SIZE], refs[2 * SIZE :]
    half, feats = weights.shape
    rows, ss = packs[0].shape[0], half // SIZE
    gather_weights(places[1], pieces, weights)
    for k, pack in enumerate(packs):
        at = pl.ds(k * rows, rows)
        left[at, pl.ds(0, ss)], left[at, pl.ds(ss, feats - ss)] = native_features(
            places, pack, half
        )
    out[...] = times(left[...], weights[...])


def apply_early_kernel(far1, far2, far3, piece0, piece1, piece2, before, *refs):
    places = places_here()
    outs, (left, weights) = refs[: SIZE - 1], refs[SIZE - 1 :]
    rows = far1.shape[0]
    last = jnp.zeros(piece0.shape, piece0.dtype)
    gather_weights(places[2], (piece0, piece1, piece2, last), weights)
    for k, pack in enumerate((far1, far2, far3)):
        left[pl.ds(k * rows, rows), :] = pack[...]
    product = times(left[...], weights[...])
    for k, out in enumerate(outs):
        sofar = before[pl.ds((k + 1) * rows, rows), :]
        out[...] = (product[k * rows : (k + 1) * rows] + sofar).astype(out.dtype)


def apply_sent_kernel(left, piece, before, early1, early2, early3, *outs):
    places = places_here()
    rows, ss = outs[0].shape[0], piece.shape[0]
    which = lax.rem(places[2] + 1, SIZE)
    block = pl.ds(pl.multiple_of(which * ss, ss), ss)
    product = times(left[...], piece[...])
    for k, out in enumerate(outs):
        sofar = before[pl.ds((k + 1) * rows, rows), block]
        out[:, block] = (product[k * rows : (k + 1) * rows] + sofar).astype(out.dtype)


def apply_kept_kernel(pack, *refs):
    places = places_here()
    pieces, (before, out, weights) = refs[:SIZE], refs[SIZE:]
    gather_weights(places[2], pieces, weights)
    out[...] = times(pack[...], weights[...]) + before[pl.ds(0, pack.shape[0]), :]


def shapes(*described):
    return [jax.ShapeDtypeStruct(shape, dtype) for shape, dtype in described]


def kernel_call(kernel, name, outs, n_in, scratch=(), flops=0, aliases=None):
    return pl.pallas_call(
        kernel,
        out_shape=outs,
        in_specs=[WHOLE] * n_in,
        out_specs=[WHOLE] * len(outs),
        scratch_shapes=list(scratch),
        input_output_aliases=aliases or {},
        compiler_params=PARAMS,
        cost_estimate=pl.CostEstimate(flops=flops, bytes_accessed=4 << 20, transcendentals=0),
        name=name,
    )


def body(student, teacher):
    rows, half = student.shape
    wide = teacher.shape[1]
    width = 2 * half
    groups = lax.axis_size("loop") * lax.axis_size("rep")
    passages = rows * groups
    coef = 32.0 * width / (passages**0.5)
    level = passages / width
    ss, ts = half // SIZE, wide // SIZE
    feats = ss + ts
    flops = 2 * SIZE * rows * half * feats

    t_far, s_far = other_core(teacher), other_core(student)
    ssq_s, ssq_t = kernel_call(sums_kernel, "sums", shapes(*[((rows, 1), F32)] * 2), 2)(
        student, teacher
    )
    *near, inv_s, inv_t = kernel_call(
        pack_own_kernel,
        "pack_own",
        shapes(*[((rows, half + ts), BF16)] * SIZE, *[((rows, 1), F32)] * 2),
        6,
    )(student, s_far, teacher, t_far, ssq_s, ssq_t)
    far = kernel_call(
        pack_far_kernel, "pack_far", shapes(*[((rows, feats), BF16)] * SIZE), 4
    )(s_far, t_far, inv_s, inv_t)
    norm_own = near[0][:, :half]

    def exchanged(own, sent, axis_of_core, sign=1):
        arrived = {by: shifted(sent(by), axis_of_core, sign * by) for by in ORDER}
        return [own] + [arrived[by] for by in (1, 2, 3)]

    def added(total, sent, axis_of_core, sign=1):
        for array in exchanged(None, sent, axis_of_core, sign)[1:]:
            total = total + array.astype(F32)
        return total

    near = exchanged(near[0], near.__getitem__, GATHER)
    far = exchanged(far[0], far.__getitem__, GATHER)

    blocks = shapes(((ss, feats), F32), *[((ss, feats), BF16)] * 3)

    def operands(count):
        return [pltpu.VMEM((count * rows, half), BF16), pltpu.VMEM((count * rows, feats), BF16)]

    early = kernel_call(
        functools.partial(gram_early_kernel, level * SIZE / groups),
        "gram_early",
        shapes(((half, feats), F32)),
        3,
        operands(3),
        flops,
    )(*near[:3])[0]
    near_blocks = kernel_call(
        gram_native_kernel, "gram_native", blocks, 2, operands(1), flops // 4
    )(near[3], early)
    far_blocks = kernel_call(
        gram_far_kernel, "gram_far", blocks, 2 * SIZE, operands(SIZE), flops
    )(*near, *far)

    def weights_of(chunk, own, *sends):
        total = added(own, lambda by: sends[by - 1], FIRST[chunk])
        shared = total.astype(BF16)
        piece = added(total, lambda by: shared, SECOND[chunk]).astype(BF16)
        return exchanged(piece, lambda by: piece, FIRST[chunk])

    near_weights = weights_of(0, *near_blocks)
    far_weights = weights_of(1, *far_blocks)

    sofar = kernel_call(
        apply_native_kernel,
        "apply_native",
        shapes(((SIZE * rows, half), F32)),
        2 * SIZE,
        [pltpu.VMEM((SIZE * rows, feats), BF16), pltpu.VMEM((half, feats), BF16)],
        flops,
    )(*near, *near_weights)[0]
    messages = shapes(*[((rows, half), BF16)] * 3)
    weights = pltpu.VMEM((half, feats), BF16)
    *most, stacked = kernel_call(
        apply_early_kernel,
        "apply_early",
        messages + shapes(((3 * rows, feats), BF16)),
        7,
        [weights],
        flops * 3 // 4,
    )(*far[1:], *far_weights[:3], sofar)
    parts = kernel_call(
        apply_sent_kernel,
        "apply_sent",
        messages,
        6,
        (),
        flops // 4,
        {3 + k: k for k in range(3)},
    )(stacked, far_weights[3], sofar, *most)
    grad_n = kernel_call(
        apply_kept_kernel, "apply_kept", shapes(((rows, half), F32)), SIZE + 2, [weights], flops // 4
    )(far[0], *far_weights, sofar)[0]
    norm_f = norm_own.astype(F32)
    grad_n = grad_n + level * norm_f
    grad_n = coef * added(grad_n, lambda by: parts[by - 1], GATHER, -1)
    inner = jnp.sum(grad_n * norm_f, axis=1)
    inner = inner + other_core(inner)
    return (grad_n - inner[:, None] * norm_f) * inv_s


def solution(mesh):
    placed = (P(("loop", "rep"), "sec"), P(("loop", "rep"), "sec"))
    return jax.shard_map(
        body, mesh=mesh, in_specs=placed, out_specs=P(("loop", "rep"), "sec"), check_vma=False
    )
```

```python
import functools
import itertools

import jax
import jax.numpy as jnp
from jax import lax
from jax.experimental import pallas as pl
from jax.experimental.pallas import tpu as pltpu
from jax.sharding import PartitionSpec as P

AXES = ("loop", "rep", "sec")
X, Y, Z = 0, 1, 2
SIZE = 4
GATHER = (Y, X)
FIRST = ((X, Z), (Z, Y))
SECOND = ((Z, Y), (X, Z))
ORDER = (2, 1, 3)
STRIP = 32
PARAMS = pltpu.CompilerParams(vmem_limit_bytes=40 * 1024 * 1024)
WHOLE = pl.BlockSpec(memory_space=pltpu.VMEM)
BF16, F32 = jnp.bfloat16, jnp.float32


def index_of(chip, core):
    x, y, z = chip
    return (((x // 2) * SIZE + z) * 8 + y * 2 + x % 2) * 2 + core


def shifted(array, axis_of_core, by):
    pairs = []
    for chip in itertools.product(range(SIZE), repeat=3):
        for core in range(2):
            target = list(chip)
            axis = axis_of_core[core]
            target[axis] = (target[axis] + by) % SIZE
            pairs.append((index_of(chip, core), index_of(target, core)))
    return lax.ppermute(array, AXES, pairs)


def other_core(array):
    return lax.ppermute(array, "sec", [(0, 1), (1, 0)])


def places_here():
    loop, rep, core = (lax.axis_index(name) for name in AXES)
    chip = (lax.div(loop, SIZE) * 2 + lax.rem(rep, 2), lax.div(rep, 2), lax.rem(loop, SIZE))
    return [jnp.where(core == 0, chip[axes[0]], chip[axes[1]]) for axes in (GATHER, *FIRST)]


def scaled(piece, inv):
    return (piece.astype(F32) * inv).astype(BF16)


def part(places, by, size):
    return pl.ds(pl.multiple_of(lax.rem(places[0] + by, SIZE) * size, size), size)


def squares(values):
    values = values.astype(F32)
    return jnp.sum(values * values, axis=1, keepdims=True)


def strips(rows):
    return [pl.ds(start, STRIP) for start in range(0, rows, STRIP)]


def sums_kernel(s_own, t_own, ssq_s, ssq_t):
    for at in strips(s_own.shape[0]):
        ssq_s[at, :] = squares(s_own[at, :])
        ssq_t[at, :] = squares(t_own[at, :])


def pack_own_kernel(s_own, s_far, t_own, t_far, ssq_s, ssq_t, *outs):
    places = places_here()
    rows, half = s_own.shape
    ts = t_own.shape[1] // SIZE
    inv_s, inv_t = outs[SIZE:]
    for at in strips(rows):
        inv_s[at, :] = lax.rsqrt(ssq_s[at, :] + squares(s_far[at, :]) + 1e-06)
        inv_t[at, :] = lax.rsqrt(ssq_t[at, :] + squares(t_far[at, :]) + 1e-06)
    for at in strips(rows):
        norm = scaled(s_own[at, :], inv_s[at, :])
        for by in range(SIZE):
            outs[by][at, pl.ds(0, half)] = norm
            outs[by][at, pl.ds(half, ts)] = scaled(t_own[at, part(places, by, ts)], inv_t[at, :])


def pack_far_kernel(s_far, t_far, inv_s, inv_t, *outs):
    places = places_here()
    rows = s_far.shape[0]
    ss, ts = s_far.shape[1] // SIZE, t_far.shape[1] // SIZE
    for at in strips(rows):
        for by in range(SIZE):
            outs[by][at, pl.ds(0, ss)] = scaled(s_far[at, part(places, by, ss)], inv_s[at, :])
            outs[by][at, pl.ds(ss, ts)] = scaled(t_far[at, part(places, by, ts)], inv_t[at, :])


def native_features(places, pack, half):
    ss = half // SIZE
    return pack[:, part(places, 0, ss)], pack[:, pl.ds(half, pack.shape[1] - half)]


def stack(places, chunk, norms, packs, left, right):
    native = chunk == 0
    rows = norms[0].shape[0]
    half, feats = left.shape[1], right.shape[1]
    ss = half // SIZE
    for k, (norm, pack) in enumerate(zip(norms, packs)):
        at = pl.ds(k * rows, rows)
        for by in range(SIZE):
            which = lax.rem(places[1 + chunk] + by, SIZE)
            block = pl.ds(pl.multiple_of(which * ss, ss), ss)
            left[at, pl.ds(by * ss, ss)] = norm[:, block]
        if native:
            right[at, pl.ds(0, ss)], right[at, pl.ds(ss, feats - ss)] = native_features(
                places, pack, half
            )
        else:
            right[at, :] = pack[...]


def cross(left, right):
    return lax.dot_general(
        left[...], right[...], (((0,), (0,)), ((), ())), preferred_element_type=F32
    )


def emit(product, outs):
    half, feats = product.shape
    ss = half // SIZE
    for by, out in enumerate(outs):
        rows = product[by * ss : (by + 1) * ss]
        out[:, pl.ds(0, ss)] = rows[:, :ss].astype(out.dtype)
        out[:, pl.ds(ss, feats - ss)] = -rows[:, ss:].astype(out.dtype)


def gram_early_kernel(share, *refs):
    places = places_here()
    packs, (product, left, right) = refs[:-3], refs[-3:]
    stack(places, 0, packs, packs, left, right)
    product[...] = cross(left, right)
    ss = product.shape[0] // SIZE
    row = lax.broadcasted_iota(jnp.int32, (ss, ss), 0)
    col = lax.broadcasted_iota(jnp.int32, (ss, ss), 1)
    by = lax.rem(places[0] + SIZE - places[1], SIZE)
    block = pl.ds(pl.multiple_of(by * ss, ss), ss)
    product[block, pl.ds(0, ss)] -= jnp.where(row == col, share, 0.0)


def gram_native_kernel(pack, before, *refs):
    places = places_here()
    outs, (left, right) = refs[:SIZE], refs[SIZE:]
    stack(places, 0, [pack], [pack], left, right)
    emit(before[...] + cross(left, right), outs)


def gram_far_early_kernel(*refs):
    places = places_here()
    count = len(refs) // 2 - 1
    product, left, right = refs[2 * count :]
    stack(places, 1, refs[:count], refs[count : 2 * count], left, right)
    product[...] = cross(left, right)


def gram_far_kernel(norm, pack, before, *refs):
    places = places_here()
    outs, (left, right) = refs[:SIZE], refs[SIZE:]
    stack(places, 1, [norm], [pack], left, right)
    emit(before[...] + cross(left, right), outs)


def gather_weights(place, pieces, weights):
    ss = pieces[0].shape[0]
    for by, piece in enumerate(pieces):
        which = lax.rem(place + SIZE - by, SIZE)
        weights[pl.ds(pl.multiple_of(which * ss, ss), ss), :] = piece[...]


def times(left, weights):
    return lax.dot_general(left, weights, (((1,), (1,)), ((), ())), preferred_element_type=F32)


def apply_native_kernel(*refs):
    places = places_here()
    packs, pieces, (out, left, weights) = refs[:SIZE], refs[SIZE : 2 * SIZE], refs[2 * SIZE :]
    half, feats = weights.shape
    rows, ss = packs[0].shape[0], half // SIZE
    gather_weights(places[1], pieces, weights)
    for k, pack in enumerate(packs):
        at = pl.ds(k * rows, rows)
        left[at, pl.ds(0, ss)], left[at, pl.ds(ss, feats - ss)] = native_features(
            places, pack, half
        )
    out[...] = times(left[...], weights[...])


def apply_early_kernel(far1, far2, far3, piece0, piece1, piece2, before, *refs):
    places = places_here()
    outs, (left, weights) = refs[: SIZE - 1], refs[SIZE - 1 :]
    rows = far1.shape[0]
    last = jnp.zeros(piece0.shape, piece0.dtype)
    gather_weights(places[2], (piece0, piece1, piece2, last), weights)
    for k, pack in enumerate((far1, far2, far3)):
        left[pl.ds(k * rows, rows), :] = pack[...]
    product = times(left[...], weights[...])
    for k, out in enumerate(outs):
        sofar = before[pl.ds((k + 1) * rows, rows), :]
        out[...] = (product[k * rows : (k + 1) * rows] + sofar).astype(out.dtype)


def apply_sent_kernel(left, piece, before, early1, early2, early3, *outs):
    places = places_here()
    rows, ss = outs[0].shape[0], piece.shape[0]
    which = lax.rem(places[2] + 1, SIZE)
    block = pl.ds(pl.multiple_of(which * ss, ss), ss)
    product = times(left[...], piece[...])
    for k, out in enumerate(outs):
        sofar = before[pl.ds((k + 1) * rows, rows), block]
        out[:, block] = (product[k * rows : (k + 1) * rows] + sofar).astype(out.dtype)


def apply_kept_kernel(pack, *refs):
    places = places_here()
    pieces, (before, out, weights) = refs[:SIZE], refs[SIZE:]
    gather_weights(places[2], pieces, weights)
    out[...] = times(pack[...], weights[...]) + before[pl.ds(0, pack.shape[0]), :]


def shapes(*described):
    return [jax.ShapeDtypeStruct(shape, dtype) for shape, dtype in described]


def kernel_call(kernel, name, outs, n_in, scratch=(), flops=0, aliases=None):
    return pl.pallas_call(
        kernel,
        out_shape=outs,
        in_specs=[WHOLE] * n_in,
        out_specs=[WHOLE] * len(outs),
        scratch_shapes=list(scratch),
        input_output_aliases=aliases or {},
        compiler_params=PARAMS,
        cost_estimate=pl.CostEstimate(flops=flops, bytes_accessed=4 << 20, transcendentals=0),
        name=name,
    )


def body(student, teacher):
    rows, half = student.shape
    wide = teacher.shape[1]
    width = 2 * half
    groups = lax.axis_size("loop") * lax.axis_size("rep")
    passages = rows * groups
    coef = 32.0 * width / (passages**0.5)
    level = passages / width
    ss, ts = half // SIZE, wide // SIZE
    feats = ss + ts
    flops = 2 * SIZE * rows * half * feats

    t_far, s_far = other_core(teacher), other_core(student)
    ssq_s, ssq_t = kernel_call(sums_kernel, "sums", shapes(*[((rows, 1), F32)] * 2), 2)(
        student, teacher
    )
    *near, inv_s, inv_t = kernel_call(
        pack_own_kernel,
        "pack_own",
        shapes(*[((rows, half + ts), BF16)] * SIZE, *[((rows, 1), F32)] * 2),
        6,
    )(student, s_far, teacher, t_far, ssq_s, ssq_t)
    norm_own = near[0][:, :half]

    def exchanged(own, sent, axis_of_core, sign=1):
        arrived = {by: shifted(sent(by), axis_of_core, sign * by) for by in ORDER}
        return [own] + [arrived[by] for by in (1, 2, 3)]

    def added(total, sent, axis_of_core, sign=1):
        for array in exchanged(None, sent, axis_of_core, sign)[1:]:
            total = total + array.astype(F32)
        return total

    near = exchanged(near[0], near.__getitem__, GATHER)
    near[1], t_far = lax.optimization_barrier((near[1], t_far))
    far = kernel_call(
        pack_far_kernel, "pack_far", shapes(*[((rows, feats), BF16)] * SIZE), 4
    )(s_far, t_far, inv_s, inv_t)
    far = exchanged(far[0], far.__getitem__, GATHER)

    blocks = shapes(((ss, feats), F32), *[((ss, feats), BF16)] * 3)

    def operands(count):
        return [pltpu.VMEM((count * rows, half), BF16), pltpu.VMEM((count * rows, feats), BF16)]

    early = kernel_call(
        functools.partial(gram_early_kernel, level * SIZE / groups),
        "gram_early",
        shapes(((half, feats), F32)),
        3,
        operands(3),
        flops,
    )(*near[:3])[0]
    near_blocks = kernel_call(
        gram_native_kernel, "gram_native", blocks, 2, operands(1), flops // 4
    )(near[3], early)
    early = kernel_call(
        gram_far_early_kernel, "gram_far_early", shapes(((half, feats), F32)), 6, operands(3), flops
    )(*near[:3], *far[:3])[0]
    far_blocks = kernel_call(
        gram_far_kernel, "gram_far", blocks, 3, operands(1), flops // 4
    )(near[3], far[3], early)

    def weights_of(chunk, own, *sends):
        total = added(own, lambda by: sends[by - 1], FIRST[chunk])
        shared = total.astype(BF16)
        piece = added(total, lambda by: shared, SECOND[chunk]).astype(BF16)
        return exchanged(piece, lambda by: piece, FIRST[chunk])

    near_weights = weights_of(0, *near_blocks)
    far_weights = weights_of(1, *far_blocks)

    sofar = kernel_call(
        apply_native_kernel,
        "apply_native",
        shapes(((SIZE * rows, half), F32)),
        2 * SIZE,
        [pltpu.VMEM((SIZE * rows, feats), BF16), pltpu.VMEM((half, feats), BF16)],
        flops,
    )(*near, *near_weights)[0]
    messages = shapes(*[((rows, half), BF16)] * 3)
    weights = pltpu.VMEM((half, feats), BF16)
    *most, stacked = kernel_call(
        apply_early_kernel,
        "apply_early",
        messages + shapes(((3 * rows, feats), BF16)),
        7,
        [weights],
        flops * 3 // 4,
    )(*far[1:], *far_weights[:3], sofar)
    parts = kernel_call(
        apply_sent_kernel,
        "apply_sent",
        messages,
        6,
        (),
        flops // 4,
        {3 + k: k for k in range(3)},
    )(stacked, far_weights[3], sofar, *most)
    grad_n = kernel_call(
        apply_kept_kernel, "apply_kept", shapes(((rows, half), F32)), SIZE + 2, [weights], flops // 4
    )(far[0], *far_weights, sofar)[0]
    norm_f = norm_own.astype(F32)
    grad_n = grad_n + level * norm_f
    grad_n = coef * added(grad_n, lambda by: parts[by - 1], GATHER, -1)
    inner = jnp.sum(grad_n * norm_f, axis=1)
    inner = inner + other_core(inner)
    return (grad_n - inner[:, None] * norm_f) * inv_s


def solution(mesh):
    placed = (P(("loop", "rep"), "sec"), P(("loop", "rep"), "sec"))
    return jax.shard_map(
        body, mesh=mesh, in_specs=placed, out_specs=P(("loop", "rep"), "sec"), check_vma=False
    )
```

```python
import functools
import itertools

import jax
import jax.numpy as jnp
from jax import lax
from jax.experimental import pallas as pl
from jax.experimental.pallas import tpu as pltpu
from jax.sharding import PartitionSpec as P

AXES = ("loop", "rep", "sec")
X, Y, Z = 0, 1, 2
SIZE = 4
GATHER = (Y, X)
FIRST = ((X, Z), (Z, Y))
SECOND = ((Z, Y), (X, Z))
ORDER = (1, 3, 2)
STRIP = 32
PARAMS = pltpu.CompilerParams(vmem_limit_bytes=40 * 1024 * 1024)
WHOLE = pl.BlockSpec(memory_space=pltpu.VMEM)
BF16, F32 = jnp.bfloat16, jnp.float32


def index_of(chip, core):
    x, y, z = chip
    return (((x // 2) * SIZE + z) * 8 + y * 2 + x % 2) * 2 + core


def shifted(array, axis_of_core, by):
    pairs = []
    for chip in itertools.product(range(SIZE), repeat=3):
        for core in range(2):
            target = list(chip)
            axis = axis_of_core[core]
            target[axis] = (target[axis] + by) % SIZE
            pairs.append((index_of(chip, core), index_of(target, core)))
    return lax.ppermute(array, AXES, pairs)


def other_core(array):
    return lax.ppermute(array, "sec", [(0, 1), (1, 0)])


def places_here():
    loop, rep, core = (lax.axis_index(name) for name in AXES)
    chip = (lax.div(loop, SIZE) * 2 + lax.rem(rep, 2), lax.div(rep, 2), lax.rem(loop, SIZE))
    return [jnp.where(core == 0, chip[axes[0]], chip[axes[1]]) for axes in (GATHER, *FIRST)]


def scaled(piece, inv):
    return (piece.astype(F32) * inv).astype(BF16)


def part(places, by, size):
    return pl.ds(pl.multiple_of(lax.rem(places[0] + by, SIZE) * size, size), size)


def squares(values):
    values = values.astype(F32)
    return jnp.sum(values * values, axis=1, keepdims=True)


def strips(rows):
    return [pl.ds(start, STRIP) for start in range(0, rows, STRIP)]


def sums_kernel(s_own, t_own, ssq_s, ssq_t):
    for at in strips(s_own.shape[0]):
        ssq_s[at, :] = squares(s_own[at, :])
        ssq_t[at, :] = squares(t_own[at, :])


def pack_own_kernel(s_own, s_far, t_own, t_far, ssq_s, ssq_t, *outs):
    places = places_here()
    rows, half = s_own.shape
    ts = t_own.shape[1] // SIZE
    inv_s, inv_t = outs[SIZE:]
    for at in strips(rows):
        inv_s[at, :] = lax.rsqrt(ssq_s[at, :] + squares(s_far[at, :]) + 1e-06)
        inv_t[at, :] = lax.rsqrt(ssq_t[at, :] + squares(t_far[at, :]) + 1e-06)
    for at in strips(rows):
        norm = scaled(s_own[at, :], inv_s[at, :])
        for by in range(SIZE):
            outs[by][at, pl.ds(0, half)] = norm
            outs[by][at, pl.ds(half, ts)] = scaled(t_own[at, part(places, by, ts)], inv_t[at, :])


def pack_far_kernel(s_far, t_far, inv_s, inv_t, *outs):
    places = places_here()
    rows = s_far.shape[0]
    ss, ts = s_far.shape[1] // SIZE, t_far.shape[1] // SIZE
    for at in strips(rows):
        for by in range(SIZE):
            outs[by][at, pl.ds(0, ss)] = scaled(s_far[at, part(places, by, ss)], inv_s[at, :])
            outs[by][at, pl.ds(ss, ts)] = scaled(t_far[at, part(places, by, ts)], inv_t[at, :])


def native_features(places, pack, half):
    ss = half // SIZE
    return pack[:, part(places, 0, ss)], pack[:, pl.ds(half, pack.shape[1] - half)]


def stack(places, chunk, norms, packs, left, right):
    native = chunk == 0
    rows = norms[0].shape[0]
    half, feats = left.shape[1], right.shape[1]
    ss = half // SIZE
    for k, (norm, pack) in enumerate(zip(norms, packs)):
        at = pl.ds(k * rows, rows)
        for by in range(SIZE):
            which = lax.rem(places[1 + chunk] + by, SIZE)
            block = pl.ds(pl.multiple_of(which * ss, ss), ss)
            left[at, pl.ds(by * ss, ss)] = norm[:, block]
        if native:
            right[at, pl.ds(0, ss)], right[at, pl.ds(ss, feats - ss)] = native_features(
                places, pack, half
            )
        else:
            right[at, :] = pack[...]


def cross(left, right):
    return lax.dot_general(
        left[...], right[...], (((0,), (0,)), ((), ())), preferred_element_type=F32
    )


def emit(product, outs):
    half, feats = product.shape
    ss = half // SIZE
    for by, out in enumerate(outs):
        rows = product[by * ss : (by + 1) * ss]
        out[:, pl.ds(0, ss)] = rows[:, :ss].astype(out.dtype)
        out[:, pl.ds(ss, feats - ss)] = -rows[:, ss:].astype(out.dtype)


def gram_early_kernel(share, *refs):
    places = places_here()
    packs, (product, left, right) = refs[:-3], refs[-3:]
    stack(places, 0, packs, packs, left, right)
    product[...] = cross(left, right)
    ss = product.shape[0] // SIZE
    row = lax.broadcasted_iota(jnp.int32, (ss, ss), 0)
    col = lax.broadcasted_iota(jnp.int32, (ss, ss), 1)
    by = lax.rem(places[0] + SIZE - places[1], SIZE)
    block = pl.ds(pl.multiple_of(by * ss, ss), ss)
    product[block, pl.ds(0, ss)] -= jnp.where(row == col, share, 0.0)


def gram_native_kernel(pack, before, *refs):
    places = places_here()
    outs, (left, right) = refs[:SIZE], refs[SIZE:]
    stack(places, 0, [pack], [pack], left, right)
    emit(before[...] + cross(left, right), outs)


def gram_far_early_kernel(*refs):
    places = places_here()
    count = len(refs) // 2 - 1
    product, left, right = refs[2 * count :]
    stack(places, 1, refs[:count], refs[count : 2 * count], left, right)
    product[...] = cross(left, right)


def gram_far_kernel(norm, pack, before, *refs):
    places = places_here()
    outs, (left, right) = refs[:SIZE], refs[SIZE:]
    stack(places, 1, [norm], [pack], left, right)
    emit(before[...] + cross(left, right), outs)


def gather_weights(place, pieces, weights):
    ss = pieces[0].shape[0]
    for by, piece in enumerate(pieces):
        which = lax.rem(place + SIZE - by, SIZE)
        weights[pl.ds(pl.multiple_of(which * ss, ss), ss), :] = piece[...]


def times(left, weights):
    return lax.dot_general(left, weights, (((1,), (1,)), ((), ())), preferred_element_type=F32)


def apply_native_kernel(*refs):
    places = places_here()
    packs, pieces, (out, left, weights) = refs[:SIZE], refs[SIZE : 2 * SIZE], refs[2 * SIZE :]
    half, feats = weights.shape
    rows, ss = packs[0].shape[0], half // SIZE
    gather_weights(places[1], pieces, weights)
    for k, pack in enumerate(packs):
        at = pl.ds(k * rows, rows)
        left[at, pl.ds(0, ss)], left[at, pl.ds(ss, feats - ss)] = native_features(
            places, pack, half
        )
    out[...] = times(left[...], weights[...])


def apply_early_kernel(far1, far2, far3, piece0, piece1, piece2, before, *refs):
    places = places_here()
    outs, (left, weights) = refs[: SIZE - 1], refs[SIZE - 1 :]
    rows = far1.shape[0]
    last = jnp.zeros(piece0.shape, piece0.dtype)
    gather_weights(places[2], (piece0, piece1, piece2, last), weights)
    for k, pack in enumerate((far1, far2, far3)):
        left[pl.ds(k * rows, rows), :] = pack[...]
    product = times(left[...], weights[...])
    for k, out in enumerate(outs):
        sofar = before[pl.ds((k + 1) * rows, rows), :]
        out[...] = (product[k * rows : (k + 1) * rows] + sofar).astype(out.dtype)


def apply_sent_kernel(left, piece, before, early1, early2, early3, *outs):
    places = places_here()
    rows, ss = outs[0].shape[0], piece.shape[0]
    which = lax.rem(places[2] + 1, SIZE)
    block = pl.ds(pl.multiple_of(which * ss, ss), ss)
    product = times(left[...], piece[...])
    for k, out in enumerate(outs):
        sofar = before[pl.ds((k + 1) * rows, rows), block]
        out[:, block] = (product[k * rows : (k + 1) * rows] + sofar).astype(out.dtype)


def apply_kept_kernel(pack, *refs):
    places = places_here()
    pieces, (before, out, weights) = refs[:SIZE], refs[SIZE:]
    gather_weights(places[2], pieces, weights)
    out[...] = times(pack[...], weights[...]) + before[pl.ds(0, pack.shape[0]), :]


def shapes(*described):
    return [jax.ShapeDtypeStruct(shape, dtype) for shape, dtype in described]


def kernel_call(kernel, name, outs, n_in, scratch=(), flops=0, aliases=None):
    return pl.pallas_call(
        kernel,
        out_shape=outs,
        in_specs=[WHOLE] * n_in,
        out_specs=[WHOLE] * len(outs),
        scratch_shapes=list(scratch),
        input_output_aliases=aliases or {},
        compiler_params=PARAMS,
        cost_estimate=pl.CostEstimate(flops=flops, bytes_accessed=4 << 20, transcendentals=0),
        name=name,
    )


def body(student, teacher):
    rows, half = student.shape
    wide = teacher.shape[1]
    width = 2 * half
    groups = lax.axis_size("loop") * lax.axis_size("rep")
    passages = rows * groups
    coef = 32.0 * width / (passages**0.5)
    level = passages / width
    ss, ts = half // SIZE, wide // SIZE
    feats = ss + ts
    flops = 2 * SIZE * rows * half * feats

    t_far, s_far = other_core(teacher), other_core(student)
    ssq_s, ssq_t = kernel_call(sums_kernel, "sums", shapes(*[((rows, 1), F32)] * 2), 2)(
        student, teacher
    )
    *near, inv_s, inv_t = kernel_call(
        pack_own_kernel,
        "pack_own",
        shapes(*[((rows, half + ts), BF16)] * SIZE, *[((rows, 1), F32)] * 2),
        6,
    )(student, s_far, teacher, t_far, ssq_s, ssq_t)
    norm_own = near[0][:, :half]

    def exchanged(own, sent, axis_of_core, sign=1):
        arrived = {by: shifted(sent(by), axis_of_core, sign * by) for by in ORDER}
        return [own] + [arrived[by] for by in (1, 2, 3)]

    def added(total, sent, axis_of_core, sign=1):
        for array in exchanged(None, sent, axis_of_core, sign)[1:]:
            total = total + array.astype(F32)
        return total

    near = exchanged(near[0], near.__getitem__, GATHER)
    far = kernel_call(
        pack_far_kernel, "pack_far", shapes(*[((rows, feats), BF16)] * SIZE), 4
    )(s_far, t_far, inv_s, inv_t)
    far = exchanged(far[0], far.__getitem__, GATHER)

    blocks = shapes(((ss, feats), F32), *[((ss, feats), BF16)] * 3)

    def operands(count):
        return [pltpu.VMEM((count * rows, half), BF16), pltpu.VMEM((count * rows, feats), BF16)]

    first, last = (0, 1, 3), 2
    early = kernel_call(
        functools.partial(gram_early_kernel, level * SIZE / groups),
        "gram_early",
        shapes(((half, feats), F32)),
        3,
        operands(3),
        flops,
    )(*[near[by] for by in first])[0]
    near_blocks = kernel_call(
        gram_native_kernel, "gram_native", blocks, 2, operands(1), flops // 4
    )(near[last], early)
    early = kernel_call(
        gram_far_early_kernel, "gram_far_early", shapes(((half, feats), F32)), 6, operands(3), flops
    )(*[near[by] for by in first], *[far[by] for by in first])[0]
    far_blocks = kernel_call(
        gram_far_kernel, "gram_far", blocks, 3, operands(1), flops // 4
    )(near[last], far[last], early)

    def weights_of(chunk, own, *sends):
        total = added(own, lambda by: sends[by - 1], FIRST[chunk])
        shared = total.astype(BF16)
        piece = added(total, lambda by: shared, SECOND[chunk]).astype(BF16)
        return exchanged(piece, lambda by: piece, FIRST[chunk])

    near_weights = weights_of(0, *near_blocks)
    far_weights = weights_of(1, *far_blocks)

    sofar = kernel_call(
        apply_native_kernel,
        "apply_native",
        shapes(((SIZE * rows, half), F32)),
        2 * SIZE,
        [pltpu.VMEM((SIZE * rows, feats), BF16), pltpu.VMEM((half, feats), BF16)],
        flops,
    )(*near, *near_weights)[0]
    messages = shapes(*[((rows, half), BF16)] * 3)
    weights = pltpu.VMEM((half, feats), BF16)
    *most, stacked = kernel_call(
        apply_early_kernel,
        "apply_early",
        messages + shapes(((3 * rows, feats), BF16)),
        7,
        [weights],
        flops * 3 // 4,
    )(*far[1:], *far_weights[:3], sofar)
    parts = kernel_call(
        apply_sent_kernel,
        "apply_sent",
        messages,
        6,
        (),
        flops // 4,
        {3 + k: k for k in range(3)},
    )(stacked, far_weights[3], sofar, *most)
    grad_n = kernel_call(
        apply_kept_kernel, "apply_kept", shapes(((rows, half), F32)), SIZE + 2, [weights], flops // 4
    )(far[0], *far_weights, sofar)[0]
    norm_f = norm_own.astype(F32)
    grad_n = grad_n + level * norm_f
    grad_n = coef * added(grad_n, lambda by: parts[by - 1], GATHER, -1)
    inner = jnp.sum(grad_n * norm_f, axis=1)
    inner = inner + other_core(inner)
    return (grad_n - inner[:, None] * norm_f) * inv_s


def solution(mesh):
    placed = (P(("loop", "rep"), "sec"), P(("loop", "rep"), "sec"))
    return jax.shard_map(
        body, mesh=mesh, in_specs=placed, out_specs=P(("loop", "rep"), "sec"), check_vma=False
    )
```

```python
import functools
import itertools

import jax
import jax.numpy as jnp
from jax import lax
from jax.experimental import pallas as pl
from jax.experimental.pallas import tpu as pltpu
from jax.sharding import PartitionSpec as P

AXES = ("loop", "rep", "sec")
X, Y, Z = 0, 1, 2
SIZE = 4
GATHER = (Y, X)
FIRST = ((X, Z), (Z, Z))
SECOND = ((Z, Y), (X, Y))
ORDER = (2, 1, 3)
SUM = (1, 3, 2)
LAST = 3
STRIP = 32
PARAMS = pltpu.CompilerParams(vmem_limit_bytes=40 * 1024 * 1024)
WHOLE = pl.BlockSpec(memory_space=pltpu.VMEM)
BF16, F32 = jnp.bfloat16, jnp.float32


def index_of(chip, core):
    x, y, z = chip
    return (((x // 2) * SIZE + z) * 8 + y * 2 + x % 2) * 2 + core


def shifted(array, axis_of_core, by):
    pairs = []
    for chip in itertools.product(range(SIZE), repeat=3):
        for core in range(2):
            target = list(chip)
            axis = axis_of_core[core]
            target[axis] = (target[axis] + by) % SIZE
            pairs.append((index_of(chip, core), index_of(target, core)))
    return lax.ppermute(array, AXES, pairs)


def other_core(array):
    return lax.ppermute(array, "sec", [(0, 1), (1, 0)])


def places_here():
    loop, rep, core = (lax.axis_index(name) for name in AXES)
    chip = (lax.div(loop, SIZE) * 2 + lax.rem(rep, 2), lax.div(rep, 2), lax.rem(loop, SIZE))
    return [jnp.where(core == 0, chip[axes[0]], chip[axes[1]]) for axes in (GATHER, *FIRST)]


def scaled(piece, inv):
    return (piece.astype(F32) * inv).astype(BF16)


def part(places, by, size):
    return pl.ds(pl.multiple_of(lax.rem(places[0] + by, SIZE) * size, size), size)


def squares(values):
    values = values.astype(F32)
    return jnp.sum(values * values, axis=1, keepdims=True)


def strips(rows):
    return [pl.ds(start, STRIP) for start in range(0, rows, STRIP)]


def sums_kernel(s_own, t_own, ssq_s, ssq_t):
    for at in strips(s_own.shape[0]):
        ssq_s[at, :] = squares(s_own[at, :])
        ssq_t[at, :] = squares(t_own[at, :])


def pack_own_kernel(s_own, s_far, t_own, t_far, ssq_s, ssq_t, *outs):
    places = places_here()
    rows, half = s_own.shape
    ts = t_own.shape[1] // SIZE
    inv_s, inv_t = outs[SIZE:]
    for at in strips(rows):
        inv_s[at, :] = lax.rsqrt(ssq_s[at, :] + squares(s_far[at, :]) + 1e-06)
        inv_t[at, :] = lax.rsqrt(ssq_t[at, :] + squares(t_far[at, :]) + 1e-06)
    for at in strips(rows):
        norm = scaled(s_own[at, :], inv_s[at, :])
        for by in range(SIZE):
            outs[by][at, pl.ds(0, half)] = norm
            outs[by][at, pl.ds(half, ts)] = scaled(t_own[at, part(places, by, ts)], inv_t[at, :])


def pack_far_kernel(s_far, t_far, inv_s, inv_t, *outs):
    places = places_here()
    rows = s_far.shape[0]
    ss, ts = s_far.shape[1] // SIZE, t_far.shape[1] // SIZE
    for at in strips(rows):
        for by in range(SIZE):
            outs[by][at, pl.ds(0, ss)] = scaled(s_far[at, part(places, by, ss)], inv_s[at, :])
            outs[by][at, pl.ds(ss, ts)] = scaled(t_far[at, part(places, by, ts)], inv_t[at, :])


def native_features(places, pack, half):
    ss = half // SIZE
    return pack[:, part(places, 0, ss)], pack[:, pl.ds(half, pack.shape[1] - half)]


def stack(places, chunk, norms, packs, left, right):
    native = chunk == 0
    rows = norms[0].shape[0]
    half, feats = left.shape[1], right.shape[1]
    ss = half // SIZE
    for k, (norm, pack) in enumerate(zip(norms, packs)):
        at = pl.ds(k * rows, rows)
        for by in range(SIZE):
            which = lax.rem(places[1 + chunk] + by, SIZE)
            block = pl.ds(pl.multiple_of(which * ss, ss), ss)
            left[at, pl.ds(by * ss, ss)] = norm[:, block]
        if native:
            right[at, pl.ds(0, ss)], right[at, pl.ds(ss, feats - ss)] = native_features(
                places, pack, half
            )
        else:
            right[at, :] = pack[...]


def cross(left, right):
    return lax.dot_general(
        left[...], right[...], (((0,), (0,)), ((), ())), preferred_element_type=F32
    )


def emit(product, outs):
    half, feats = product.shape
    ss = half // SIZE
    for by, out in enumerate(outs):
        rows = product[by * ss : (by + 1) * ss]
        out[:, pl.ds(0, ss)] = rows[:, :ss].astype(out.dtype)
        out[:, pl.ds(ss, feats - ss)] = -rows[:, ss:].astype(out.dtype)


def gram_early_kernel(share, *refs):
    places = places_here()
    packs, (product, left, right) = refs[:-3], refs[-3:]
    stack(places, 0, packs, packs, left, right)
    product[...] = cross(left, right)
    ss = product.shape[0] // SIZE
    row = lax.broadcasted_iota(jnp.int32, (ss, ss), 0)
    col = lax.broadcasted_iota(jnp.int32, (ss, ss), 1)
    by = lax.rem(places[0] + SIZE - places[1], SIZE)
    block = pl.ds(pl.multiple_of(by * ss, ss), ss)
    product[block, pl.ds(0, ss)] -= jnp.where(row == col, share, 0.0)


def gram_native_kernel(pack, before, *refs):
    places = places_here()
    outs, (left, right) = refs[:SIZE], refs[SIZE:]
    stack(places, 0, [pack], [pack], left, right)
    emit(before[...] + cross(left, right), outs)


def gram_far_early_kernel(*refs):
    places = places_here()
    count = len(refs) // 2 - 1
    product, left, right = refs[2 * count :]
    stack(places, 1, refs[:count], refs[count : 2 * count], left, right)
    product[...] = cross(left, right)


def gram_far_kernel(norm, pack, before, *refs):
    places = places_here()
    outs, (left, right) = refs[:SIZE], refs[SIZE:]
    stack(places, 1, [norm], [pack], left, right)
    emit(before[...] + cross(left, right), outs)


def gather_weights(place, pieces, weights):
    ss = pieces[0].shape[0]
    for by, piece in enumerate(pieces):
        which = lax.rem(place + SIZE - by, SIZE)
        weights[pl.ds(pl.multiple_of(which * ss, ss), ss), :] = piece[...]


def times(left, weights):
    return lax.dot_general(left, weights, (((1,), (1,)), ((), ())), preferred_element_type=F32)


def apply_native_kernel(*refs):
    places = places_here()
    packs, pieces, (out, left, weights) = refs[:SIZE], refs[SIZE : 2 * SIZE], refs[2 * SIZE :]
    half, feats = weights.shape
    rows, ss = packs[0].shape[0], half // SIZE
    gather_weights(places[1], pieces, weights)
    for k, pack in enumerate(packs):
        at = pl.ds(k * rows, rows)
        left[at, pl.ds(0, ss)], left[at, pl.ds(ss, feats - ss)] = native_features(
            places, pack, half
        )
    out[...] = times(left[...], weights[...])


def apply_early_kernel(far1, far2, far3, piece0, piece1, piece2, before, *refs):
    places = places_here()
    outs, (left, weights) = refs[: SIZE - 1], refs[SIZE - 1 :]
    rows = far1.shape[0]
    pieces = [piece0, piece1, piece2]
    pieces.insert(LAST, jnp.zeros(piece0.shape, piece0.dtype))
    gather_weights(places[2], pieces, weights)
    for k, pack in enumerate((far1, far2, far3)):
        left[pl.ds(k * rows, rows), :] = pack[...]
    product = times(left[...], weights[...])
    for k, out in enumerate(outs):
        sofar = before[pl.ds((k + 1) * rows, rows), :]
        out[...] = (product[k * rows : (k + 1) * rows] + sofar).astype(out.dtype)


def apply_sent_kernel(left, piece, before, early1, early2, early3, *outs):
    places = places_here()
    rows, ss = outs[0].shape[0], piece.shape[0]
    which = lax.rem(places[2] + SIZE - LAST, SIZE)
    block = pl.ds(pl.multiple_of(which * ss, ss), ss)
    product = times(left[...], piece[...])
    for k, out in enumerate(outs):
        sofar = before[pl.ds((k + 1) * rows, rows), block]
        out[:, block] = (product[k * rows : (k + 1) * rows] + sofar).astype(out.dtype)


def apply_kept_kernel(pack, *refs):
    places = places_here()
    pieces, (before, out, weights) = refs[:SIZE], refs[SIZE:]
    gather_weights(places[2], pieces, weights)
    out[...] = times(pack[...], weights[...]) + before[pl.ds(0, pack.shape[0]), :]


def shapes(*described):
    return [jax.ShapeDtypeStruct(shape, dtype) for shape, dtype in described]


def kernel_call(kernel, name, outs, n_in, scratch=(), flops=0, aliases=None):
    return pl.pallas_call(
        kernel,
        out_shape=outs,
        in_specs=[WHOLE] * n_in,
        out_specs=[WHOLE] * len(outs),
        scratch_shapes=list(scratch),
        input_output_aliases=aliases or {},
        compiler_params=PARAMS,
        cost_estimate=pl.CostEstimate(flops=flops, bytes_accessed=4 << 20, transcendentals=0),
        name=name,
    )


def body(student, teacher):
    rows, half = student.shape
    wide = teacher.shape[1]
    width = 2 * half
    groups = lax.axis_size("loop") * lax.axis_size("rep")
    passages = rows * groups
    coef = 32.0 * width / (passages**0.5)
    level = passages / width
    ss, ts = half // SIZE, wide // SIZE
    feats = ss + ts
    flops = 2 * SIZE * rows * half * feats

    t_far, s_far = other_core(teacher), other_core(student)
    ssq_s, ssq_t = kernel_call(sums_kernel, "sums", shapes(*[((rows, 1), F32)] * 2), 2)(
        student, teacher
    )
    *near, inv_s, inv_t = kernel_call(
        pack_own_kernel,
        "pack_own",
        shapes(*[((rows, half + ts), BF16)] * SIZE, *[((rows, 1), F32)] * 2),
        6,
    )(student, s_far, teacher, t_far, ssq_s, ssq_t)
    norm_own = near[0][:, :half]

    def exchanged(own, sent, axis_of_core, sign=1):
        arrived = {by: shifted(sent(by), axis_of_core, sign * by) for by in ORDER}
        return [own] + [arrived[by] for by in (1, 2, 3)]

    def added(total, sent, axis_of_core, sign=1):
        arrived = exchanged(None, sent, axis_of_core, sign)
        for by in SUM:
            total = total + arrived[by].astype(F32)
        return total

    near = exchanged(near[0], near.__getitem__, GATHER)
    far = kernel_call(
        pack_far_kernel, "pack_far", shapes(*[((rows, feats), BF16)] * SIZE), 4
    )(s_far, t_far, inv_s, inv_t)
    far = exchanged(far[0], far.__getitem__, GATHER)

    blocks = shapes(((ss, feats), F32), *[((ss, feats), BF16)] * 3)

    def operands(count):
        return [pltpu.VMEM((count * rows, half), BF16), pltpu.VMEM((count * rows, feats), BF16)]

    first = [by for by in range(SIZE) if by != LAST]
    early = kernel_call(
        functools.partial(gram_early_kernel, level * SIZE / groups),
        "gram_early",
        shapes(((half, feats), F32)),
        3,
        operands(3),
        flops,
    )(*[near[by] for by in first])[0]
    near_blocks = kernel_call(
        gram_native_kernel, "gram_native", blocks, 2, operands(1), flops // 4
    )(near[LAST], early)
    early = kernel_call(
        gram_far_early_kernel, "gram_far_early", shapes(((half, feats), F32)), 6, operands(3), flops
    )(*[near[by] for by in first], *[far[by] for by in first])[0]
    far_blocks = kernel_call(
        gram_far_kernel, "gram_far", blocks, 3, operands(1), flops // 4
    )(near[LAST], far[LAST], early)

    def weights_of(chunk, own, *sends):
        total = added(own, lambda by: sends[by - 1], FIRST[chunk])
        shared = total.astype(BF16)
        piece = added(total, lambda by: shared, SECOND[chunk]).astype(BF16)
        return exchanged(piece, lambda by: piece, FIRST[chunk])

    near_weights = weights_of(0, *near_blocks)
    far_weights = weights_of(1, *far_blocks)

    sofar = kernel_call(
        apply_native_kernel,
        "apply_native",
        shapes(((SIZE * rows, half), F32)),
        2 * SIZE,
        [pltpu.VMEM((SIZE * rows, feats), BF16), pltpu.VMEM((half, feats), BF16)],
        flops,
    )(*near, *near_weights)[0]
    messages = shapes(*[((rows, half), BF16)] * 3)
    weights = pltpu.VMEM((half, feats), BF16)
    *most, stacked = kernel_call(
        apply_early_kernel,
        "apply_early",
        messages + shapes(((3 * rows, feats), BF16)),
        7,
        [weights],
        flops * 3 // 4,
    )(*far[1:], *[far_weights[by] for by in range(SIZE) if by != LAST], sofar)
    parts = kernel_call(
        apply_sent_kernel,
        "apply_sent",
        messages,
        6,
        (),
        flops // 4,
        {3 + k: k for k in range(3)},
    )(stacked, far_weights[LAST], sofar, *most)
    grad_n = kernel_call(
        apply_kept_kernel, "apply_kept", shapes(((rows, half), F32)), SIZE + 2, [weights], flops // 4
    )(far[0], *far_weights, sofar)[0]
    norm_f = norm_own.astype(F32)
    grad_n = grad_n + level * norm_f
    grad_n = coef * added(grad_n, lambda by: parts[by - 1], GATHER, -1)
    inner = jnp.sum(grad_n * norm_f, axis=1)
    inner = inner + other_core(inner)
    return (grad_n - inner[:, None] * norm_f) * inv_s


def solution(mesh):
    placed = (P(("loop", "rep"), "sec"), P(("loop", "rep"), "sec"))
    return jax.shard_map(
        body, mesh=mesh, in_specs=placed, out_specs=P(("loop", "rep"), "sec"), check_vma=False
    )
```

```python
import functools
import itertools

import jax
import jax.numpy as jnp
from jax import lax
from jax.experimental import pallas as pl
from jax.experimental.pallas import tpu as pltpu
from jax.sharding import PartitionSpec as P

AXES = ("loop", "rep", "sec")
X, Y, Z = 0, 1, 2
SIZE = 4
GATHER = (Y, X)
FIRST = ((X, Z), (Z, Z))
SECOND = ((Z, Y), (X, Y))
ORDER = (2, 1, 3)
SUM = (1, 3, 2)
BACK = (1, 2, 3)
LAST = 3
STRIP = 32
PARAMS = pltpu.CompilerParams(vmem_limit_bytes=40 * 1024 * 1024)
WHOLE = pl.BlockSpec(memory_space=pltpu.VMEM)
BF16, F32 = jnp.bfloat16, jnp.float32


def index_of(chip, core):
    x, y, z = chip
    return (((x // 2) * SIZE + z) * 8 + y * 2 + x % 2) * 2 + core


def shifted(array, axis_of_core, by):
    pairs = []
    for chip in itertools.product(range(SIZE), repeat=3):
        for core in range(2):
            target = list(chip)
            axis = axis_of_core[core]
            target[axis] = (target[axis] + by) % SIZE
            pairs.append((index_of(chip, core), index_of(target, core)))
    return lax.ppermute(array, AXES, pairs)


def other_core(array):
    return lax.ppermute(array, "sec", [(0, 1), (1, 0)])


def places_here():
    loop, rep, core = (lax.axis_index(name) for name in AXES)
    chip = (lax.div(loop, SIZE) * 2 + lax.rem(rep, 2), lax.div(rep, 2), lax.rem(loop, SIZE))
    return [jnp.where(core == 0, chip[axes[0]], chip[axes[1]]) for axes in (GATHER, *FIRST)]


def scaled(piece, inv):
    return (piece.astype(F32) * inv).astype(BF16)


def part(places, by, size):
    return pl.ds(pl.multiple_of(lax.rem(places[0] + by, SIZE) * size, size), size)


def squares(values):
    values = values.astype(F32)
    return jnp.sum(values * values, axis=1, keepdims=True)


def strips(rows):
    return [pl.ds(start, STRIP) for start in range(0, rows, STRIP)]


def sums_kernel(s_own, t_own, ssq_s, ssq_t):
    for at in strips(s_own.shape[0]):
        ssq_s[at, :] = squares(s_own[at, :])
        ssq_t[at, :] = squares(t_own[at, :])


def pack_own_kernel(s_own, s_far, t_own, t_far, ssq_s, ssq_t, *outs):
    places = places_here()
    rows, half = s_own.shape
    ts = t_own.shape[1] // SIZE
    inv_s, inv_t = outs[SIZE:]
    for at in strips(rows):
        inv_s[at, :] = lax.rsqrt(ssq_s[at, :] + squares(s_far[at, :]) + 1e-06)
        inv_t[at, :] = lax.rsqrt(ssq_t[at, :] + squares(t_far[at, :]) + 1e-06)
    for at in strips(rows):
        norm = scaled(s_own[at, :], inv_s[at, :])
        for by in range(SIZE):
            outs[by][at, pl.ds(0, half)] = norm
            outs[by][at, pl.ds(half, ts)] = scaled(t_own[at, part(places, by, ts)], inv_t[at, :])


def pack_far_kernel(s_far, t_far, inv_s, inv_t, *outs):
    places = places_here()
    rows = s_far.shape[0]
    ss, ts = s_far.shape[1] // SIZE, t_far.shape[1] // SIZE
    for at in strips(rows):
        for by in range(SIZE):
            outs[by][at, pl.ds(0, ss)] = scaled(s_far[at, part(places, by, ss)], inv_s[at, :])
            outs[by][at, pl.ds(ss, ts)] = scaled(t_far[at, part(places, by, ts)], inv_t[at, :])


def native_features(places, pack, half):
    ss = half // SIZE
    return pack[:, part(places, 0, ss)], pack[:, pl.ds(half, pack.shape[1] - half)]


def stack(places, chunk, norms, packs, left, right):
    native = chunk == 0
    rows = norms[0].shape[0]
    half, feats = left.shape[1], right.shape[1]
    ss = half // SIZE
    for k, (norm, pack) in enumerate(zip(norms, packs)):
        at = pl.ds(k * rows, rows)
        for by in range(SIZE):
            which = lax.rem(places[1 + chunk] + by, SIZE)
            block = pl.ds(pl.multiple_of(which * ss, ss), ss)
            left[at, pl.ds(by * ss, ss)] = norm[:, block]
        if native:
            right[at, pl.ds(0, ss)], right[at, pl.ds(ss, feats - ss)] = native_features(
                places, pack, half
            )
        else:
            right[at, :] = pack[...]


def cross(left, right):
    return lax.dot_general(
        left[...], right[...], (((0,), (0,)), ((), ())), preferred_element_type=F32
    )


def emit(product, outs):
    half, feats = product.shape
    ss = half // SIZE
    for by, out in enumerate(outs):
        rows = product[by * ss : (by + 1) * ss]
        out[:, pl.ds(0, ss)] = rows[:, :ss].astype(out.dtype)
        out[:, pl.ds(ss, feats - ss)] = -rows[:, ss:].astype(out.dtype)


def gram_early_kernel(share, *refs):
    places = places_here()
    packs, (product, left, right) = refs[:-3], refs[-3:]
    stack(places, 0, packs, packs, left, right)
    product[...] = cross(left, right)
    ss = product.shape[0] // SIZE
    row = lax.broadcasted_iota(jnp.int32, (ss, ss), 0)
    col = lax.broadcasted_iota(jnp.int32, (ss, ss), 1)
    by = lax.rem(places[0] + SIZE - places[1], SIZE)
    block = pl.ds(pl.multiple_of(by * ss, ss), ss)
    product[block, pl.ds(0, ss)] -= jnp.where(row == col, share, 0.0)


def gram_native_kernel(pack, before, *refs):
    places = places_here()
    outs, (left, right) = refs[:SIZE], refs[SIZE:]
    stack(places, 0, [pack], [pack], left, right)
    emit(before[...] + cross(left, right), outs)


def gram_far_early_kernel(*refs):
    places = places_here()
    count = len(refs) // 2 - 1
    product, left, right = refs[2 * count :]
    stack(places, 1, refs[:count], refs[count : 2 * count], left, right)
    product[...] = cross(left, right)


def gram_far_kernel(norm, pack, before, *refs):
    places = places_here()
    outs, (left, right) = refs[:SIZE], refs[SIZE:]
    stack(places, 1, [norm], [pack], left, right)
    emit(before[...] + cross(left, right), outs)


def gather_weights(place, pieces, weights):
    ss = pieces[0].shape[0]
    for by, piece in enumerate(pieces):
        which = lax.rem(place + SIZE - by, SIZE)
        weights[pl.ds(pl.multiple_of(which * ss, ss), ss), :] = piece[...]


def times(left, weights):
    return lax.dot_general(left, weights, (((1,), (1,)), ((), ())), preferred_element_type=F32)


def apply_native_kernel(*refs):
    places = places_here()
    packs, pieces, (out, left, weights) = refs[:SIZE], refs[SIZE : 2 * SIZE], refs[2 * SIZE :]
    half, feats = weights.shape
    rows, ss = packs[0].shape[0], half // SIZE
    gather_weights(places[1], pieces, weights)
    for k, pack in enumerate(packs):
        at = pl.ds(k * rows, rows)
        left[at, pl.ds(0, ss)], left[at, pl.ds(ss, feats - ss)] = native_features(
            places, pack, half
        )
    out[...] = times(left[...], weights[...])


def apply_early_kernel(far1, far2, far3, piece0, piece1, piece2, before, *refs):
    places = places_here()
    outs, (left, weights) = refs[: SIZE - 1], refs[SIZE - 1 :]
    rows = far1.shape[0]
    pieces = [piece0, piece1, piece2]
    pieces.insert(LAST, jnp.zeros(piece0.shape, piece0.dtype))
    gather_weights(places[2], pieces, weights)
    for k, pack in enumerate((far1, far2, far3)):
        left[pl.ds(k * rows, rows), :] = pack[...]
    product = times(left[...], weights[...])
    for k, out in enumerate(outs):
        sofar = before[pl.ds((k + 1) * rows, rows), :]
        out[...] = (product[k * rows : (k + 1) * rows] + sofar).astype(out.dtype)


def apply_sent_kernel(left, piece, before, early1, early2, early3, *outs):
    places = places_here()
    rows, ss = outs[0].shape[0], piece.shape[0]
    which = lax.rem(places[2] + SIZE - LAST, SIZE)
    block = pl.ds(pl.multiple_of(which * ss, ss), ss)
    product = times(left[...], piece[...])
    for k, out in enumerate(outs):
        sofar = before[pl.ds((k + 1) * rows, rows), block]
        out[:, block] = (product[k * rows : (k + 1) * rows] + sofar).astype(out.dtype)


def apply_kept_kernel(pack, *refs):
    places = places_here()
    pieces, (before, out, weights) = refs[:SIZE], refs[SIZE:]
    gather_weights(places[2], pieces, weights)
    out[...] = times(pack[...], weights[...]) + before[pl.ds(0, pack.shape[0]), :]


def shapes(*described):
    return [jax.ShapeDtypeStruct(shape, dtype) for shape, dtype in described]


def kernel_call(kernel, name, outs, n_in, scratch=(), flops=0, aliases=None):
    return pl.pallas_call(
        kernel,
        out_shape=outs,
        in_specs=[WHOLE] * n_in,
        out_specs=[WHOLE] * len(outs),
        scratch_shapes=list(scratch),
        input_output_aliases=aliases or {},
        compiler_params=PARAMS,
        cost_estimate=pl.CostEstimate(flops=flops, bytes_accessed=4 << 20, transcendentals=0),
        name=name,
    )


def body(student, teacher):
    rows, half = student.shape
    wide = teacher.shape[1]
    width = 2 * half
    groups = lax.axis_size("loop") * lax.axis_size("rep")
    passages = rows * groups
    coef = 32.0 * width / (passages**0.5)
    level = passages / width
    ss, ts = half // SIZE, wide // SIZE
    feats = ss + ts
    flops = 2 * SIZE * rows * half * feats

    t_far, s_far = other_core(teacher), other_core(student)
    ssq_s, ssq_t = kernel_call(sums_kernel, "sums", shapes(*[((rows, 1), F32)] * 2), 2)(
        student, teacher
    )
    *near, inv_s, inv_t = kernel_call(
        pack_own_kernel,
        "pack_own",
        shapes(*[((rows, half + ts), BF16)] * SIZE, *[((rows, 1), F32)] * 2),
        6,
    )(student, s_far, teacher, t_far, ssq_s, ssq_t)
    norm_own = near[0][:, :half]

    def exchanged(own, sent, axis_of_core, sign=1):
        arrived = {by: shifted(sent(by), axis_of_core, sign * by) for by in ORDER}
        return [own] + [arrived[by] for by in (1, 2, 3)]

    def added(total, sent, axis_of_core, sign=1, order=SUM):
        arrived = exchanged(None, sent, axis_of_core, sign)
        for by in order:
            total = total + arrived[by].astype(F32)
        return total

    near = exchanged(near[0], near.__getitem__, GATHER)
    far = kernel_call(
        pack_far_kernel, "pack_far", shapes(*[((rows, feats), BF16)] * SIZE), 4
    )(s_far, t_far, inv_s, inv_t)
    far = exchanged(far[0], far.__getitem__, GATHER)

    blocks = shapes(((ss, feats), F32), *[((ss, feats), BF16)] * 3)

    def operands(count):
        return [pltpu.VMEM((count * rows, half), BF16), pltpu.VMEM((count * rows, feats), BF16)]

    first = [by for by in range(SIZE) if by != LAST]
    early = kernel_call(
        functools.partial(gram_early_kernel, level * SIZE / groups),
        "gram_early",
        shapes(((half, feats), F32)),
        3,
        operands(3),
        flops,
    )(*[near[by] for by in first])[0]
    near_blocks = kernel_call(
        gram_native_kernel, "gram_native", blocks, 2, operands(1), flops // 4
    )(near[LAST], early)
    early = kernel_call(
        gram_far_early_kernel, "gram_far_early", shapes(((half, feats), F32)), 6, operands(3), flops
    )(*[near[by] for by in first], *[far[by] for by in first])[0]
    far_blocks = kernel_call(
        gram_far_kernel, "gram_far", blocks, 3, operands(1), flops // 4
    )(near[LAST], far[LAST], early)

    def weights_of(chunk, own, *sends):
        total = added(own, lambda by: sends[by - 1], FIRST[chunk])
        shared = total.astype(BF16)
        piece = added(total, lambda by: shared, SECOND[chunk]).astype(BF16)
        return exchanged(piece, lambda by: piece, FIRST[chunk])

    near_weights = weights_of(0, *near_blocks)
    far_weights = weights_of(1, *far_blocks)

    sofar = kernel_call(
        apply_native_kernel,
        "apply_native",
        shapes(((SIZE * rows, half), F32)),
        2 * SIZE,
        [pltpu.VMEM((SIZE * rows, feats), BF16), pltpu.VMEM((half, feats), BF16)],
        flops,
    )(*near, *near_weights)[0]
    messages = shapes(*[((rows, half), BF16)] * 3)
    weights = pltpu.VMEM((half, feats), BF16)
    *most, stacked = kernel_call(
        apply_early_kernel,
        "apply_early",
        messages + shapes(((3 * rows, feats), BF16)),
        7,
        [weights],
        flops * 3 // 4,
    )(*far[1:], *[far_weights[by] for by in range(SIZE) if by != LAST], sofar)
    parts = kernel_call(
        apply_sent_kernel,
        "apply_sent",
        messages,
        6,
        (),
        flops // 4,
        {3 + k: k for k in range(3)},
    )(stacked, far_weights[LAST], sofar, *most)
    grad_n = kernel_call(
        apply_kept_kernel, "apply_kept", shapes(((rows, half), F32)), SIZE + 2, [weights], flops // 4
    )(far[0], *far_weights, sofar)[0]
    norm_f = norm_own.astype(F32)
    grad_n = grad_n + level * norm_f
    grad_n = coef * added(grad_n, lambda by: parts[by - 1], GATHER, -1, BACK)
    inner = jnp.sum(grad_n * norm_f, axis=1)
    inner = inner + other_core(inner)
    return (grad_n - inner[:, None] * norm_f) * inv_s


def solution(mesh):
    placed = (P(("loop", "rep"), "sec"), P(("loop", "rep"), "sec"))
    return jax.shard_map(
        body, mesh=mesh, in_specs=placed, out_specs=P(("loop", "rep"), "sec"), check_vma=False
    )
```

```python
import functools
import itertools

import jax
import jax.numpy as jnp
from jax import lax
from jax.experimental import pallas as pl
from jax.experimental.pallas import tpu as pltpu
from jax.sharding import PartitionSpec as P

AXES = ("loop", "rep", "sec")
X, Y, Z = 0, 1, 2
SIZE = 4
GATHER = (Y, X)
FIRST = ((X, Z), (Z, Z))
SECOND = ((Z, Y), (X, Y))
ORDER = (2, 1, 3)
SUM = (1, 3, 2)
BACK = (1, 2, 3)
LAST = 3
STRIP = 32
PARAMS = pltpu.CompilerParams(vmem_limit_bytes=40 * 1024 * 1024)
WHOLE = pl.BlockSpec(memory_space=pltpu.VMEM)
BF16, F32 = jnp.bfloat16, jnp.float32


def index_of(chip, core):
    x, y, z = chip
    return (((x // 2) * SIZE + z) * 8 + y * 2 + x % 2) * 2 + core


def shifted(array, axis_of_core, by):
    pairs = []
    for chip in itertools.product(range(SIZE), repeat=3):
        for core in range(2):
            target = list(chip)
            axis = axis_of_core[core]
            target[axis] = (target[axis] + by) % SIZE
            pairs.append((index_of(chip, core), index_of(target, core)))
    return lax.ppermute(array, AXES, pairs)


def other_core(array):
    return lax.ppermute(array, "sec", [(0, 1), (1, 0)])


def places_here():
    loop, rep, core = (lax.axis_index(name) for name in AXES)
    chip = (lax.div(loop, SIZE) * 2 + lax.rem(rep, 2), lax.div(rep, 2), lax.rem(loop, SIZE))
    return [jnp.where(core == 0, chip[axes[0]], chip[axes[1]]) for axes in (GATHER, *FIRST)]


def scaled(piece, inv):
    return (piece.astype(F32) * inv).astype(BF16)


def part(places, by, size):
    return pl.ds(pl.multiple_of(lax.rem(places[0] + by, SIZE) * size, size), size)


def squares(values):
    values = values.astype(F32)
    return jnp.sum(values * values, axis=1, keepdims=True)


def strips(rows):
    return [pl.ds(start, STRIP) for start in range(0, rows, STRIP)]


def sums_kernel(s_own, t_own, ssq_s, ssq_t):
    for at in strips(s_own.shape[0]):
        ssq_s[at, :] = squares(s_own[at, :])
        ssq_t[at, :] = squares(t_own[at, :])


def pack_own_kernel(s_own, s_far, t_own, t_far, ssq_s, ssq_t, *outs):
    places = places_here()
    rows, half = s_own.shape
    ts = t_own.shape[1] // SIZE
    inv_s, inv_t = outs[SIZE:]
    for at in strips(rows):
        inv_s[at, :] = lax.rsqrt(ssq_s[at, :] + squares(s_far[at, :]) + 1e-06)
        inv_t[at, :] = lax.rsqrt(ssq_t[at, :] + squares(t_far[at, :]) + 1e-06)
    for at in strips(rows):
        norm = scaled(s_own[at, :], inv_s[at, :])
        for by in range(SIZE):
            outs[by][at, pl.ds(0, half)] = norm
            outs[by][at, pl.ds(half, ts)] = scaled(t_own[at, part(places, by, ts)], inv_t[at, :])


def pack_far_kernel(s_far, t_far, inv_s, inv_t, *outs):
    places = places_here()
    rows = s_far.shape[0]
    ss, ts = s_far.shape[1] // SIZE, t_far.shape[1] // SIZE
    for at in strips(rows):
        for by in range(SIZE):
            outs[by][at, pl.ds(0, ss)] = scaled(s_far[at, part(places, by, ss)], inv_s[at, :])
            outs[by][at, pl.ds(ss, ts)] = scaled(t_far[at, part(places, by, ts)], inv_t[at, :])


def native_features(places, pack, half):
    ss = half // SIZE
    return pack[:, part(places, 0, ss)], pack[:, pl.ds(half, pack.shape[1] - half)]


def stack(places, chunk, norms, packs, left, right):
    native = chunk == 0
    rows = norms[0].shape[0]
    half, feats = left.shape[1], right.shape[1]
    ss = half // SIZE
    for k, (norm, pack) in enumerate(zip(norms, packs)):
        at = pl.ds(k * rows, rows)
        for by in range(SIZE):
            which = lax.rem(places[1 + chunk] + by, SIZE)
            block = pl.ds(pl.multiple_of(which * ss, ss), ss)
            left[at, pl.ds(by * ss, ss)] = norm[:, block]
        if native:
            right[at, pl.ds(0, ss)], right[at, pl.ds(ss, feats - ss)] = native_features(
                places, pack, half
            )
        else:
            right[at, :] = pack[...]


def cross(left, right):
    return lax.dot_general(
        left[...], right[...], (((0,), (0,)), ((), ())), preferred_element_type=F32
    )


def emit(product, outs):
    half, feats = product.shape
    ss = half // SIZE
    for by, out in enumerate(outs):
        rows = product[by * ss : (by + 1) * ss]
        out[:, pl.ds(0, ss)] = rows[:, :ss].astype(out.dtype)
        out[:, pl.ds(ss, feats - ss)] = -rows[:, ss:].astype(out.dtype)


def gram_early_kernel(share, *refs):
    places = places_here()
    packs, (product, left, right) = refs[:-3], refs[-3:]
    stack(places, 0, packs, packs, left, right)
    product[...] = cross(left, right)
    ss = product.shape[0] // SIZE
    row = lax.broadcasted_iota(jnp.int32, (ss, ss), 0)
    col = lax.broadcasted_iota(jnp.int32, (ss, ss), 1)
    by = lax.rem(places[0] + SIZE - places[1], SIZE)
    block = pl.ds(pl.multiple_of(by * ss, ss), ss)
    product[block, pl.ds(0, ss)] -= jnp.where(row == col, share, 0.0)


def gram_native_kernel(pack, before, *refs):
    places = places_here()
    outs, (left, right) = refs[:SIZE], refs[SIZE:]
    stack(places, 0, [pack], [pack], left, right)
    emit(before[...] + cross(left, right), outs)


def gram_far_early_kernel(*refs):
    places = places_here()
    count = len(refs) // 2 - 1
    product, left, right = refs[2 * count :]
    stack(places, 1, refs[:count], refs[count : 2 * count], left, right)
    product[...] = cross(left, right)


def gram_far_kernel(norm, pack, before, *refs):
    places = places_here()
    outs, (left, right) = refs[:SIZE], refs[SIZE:]
    stack(places, 1, [norm], [pack], left, right)
    emit(before[...] + cross(left, right), outs)


def gather_weights(place, pieces, weights):
    ss = pieces[0].shape[0]
    for by, piece in enumerate(pieces):
        which = lax.rem(place + SIZE - by, SIZE)
        weights[pl.ds(pl.multiple_of(which * ss, ss), ss), :] = piece[...]


def times(left, weights):
    return lax.dot_general(left, weights, (((1,), (1,)), ((), ())), preferred_element_type=F32)


def apply_native_kernel(*refs):
    places = places_here()
    packs, pieces, (out, left, weights) = refs[:SIZE], refs[SIZE : 2 * SIZE], refs[2 * SIZE :]
    half, feats = weights.shape
    rows, ss = packs[0].shape[0], half // SIZE
    gather_weights(places[1], pieces, weights)
    for k, pack in enumerate(packs):
        at = pl.ds(k * rows, rows)
        left[at, pl.ds(0, ss)], left[at, pl.ds(ss, feats - ss)] = native_features(
            places, pack, half
        )
    out[...] = times(left[...], weights[...])


def apply_early_kernel(far1, far2, far3, piece0, piece1, piece2, before, *refs):
    places = places_here()
    outs, (left, weights) = refs[: SIZE - 1], refs[SIZE - 1 :]
    rows = far1.shape[0]
    pieces = [piece0, piece1, piece2]
    pieces.insert(LAST, jnp.zeros(piece0.shape, piece0.dtype))
    gather_weights(places[2], pieces, weights)
    for k, pack in enumerate((far1, far2, far3)):
        left[pl.ds(k * rows, rows), :] = pack[...]
    product = times(left[...], weights[...])
    for k, out in enumerate(outs):
        sofar = before[pl.ds((k + 1) * rows, rows), :]
        out[...] = (product[k * rows : (k + 1) * rows] + sofar).astype(out.dtype)


def apply_sent_kernel(left, piece, before, early1, early2, early3, *outs):
    places = places_here()
    rows, ss = outs[0].shape[0], piece.shape[0]
    which = lax.rem(places[2] + SIZE - LAST, SIZE)
    block = pl.ds(pl.multiple_of(which * ss, ss), ss)
    product = times(left[...], piece[...])
    for k, (early, out) in enumerate(zip((early1, early2, early3), outs)):
        out[...] = early[...]
        sofar = before[pl.ds((k + 1) * rows, rows), block]
        out[:, block] = (product[k * rows : (k + 1) * rows] + sofar).astype(out.dtype)


def apply_kept_kernel(pack, *refs):
    places = places_here()
    pieces, (before, out, weights) = refs[:SIZE], refs[SIZE:]
    gather_weights(places[2], pieces, weights)
    out[...] = times(pack[...], weights[...]) + before[pl.ds(0, pack.shape[0]), :]


def shapes(*described):
    return [jax.ShapeDtypeStruct(shape, dtype) for shape, dtype in described]


def kernel_call(kernel, name, outs, n_in, scratch=(), flops=0):
    return pl.pallas_call(
        kernel,
        out_shape=outs,
        in_specs=[WHOLE] * n_in,
        out_specs=[WHOLE] * len(outs),
        scratch_shapes=list(scratch),
        compiler_params=PARAMS,
        cost_estimate=pl.CostEstimate(flops=flops, bytes_accessed=4 << 20, transcendentals=0),
        name=name,
    )


def body(student, teacher):
    rows, half = student.shape
    wide = teacher.shape[1]
    width = 2 * half
    groups = lax.axis_size("loop") * lax.axis_size("rep")
    passages = rows * groups
    coef = 32.0 * width / (passages**0.5)
    level = passages / width
    ss, ts = half // SIZE, wide // SIZE
    feats = ss + ts
    flops = 2 * SIZE * rows * half * feats

    t_far, s_far = other_core(teacher), other_core(student)
    ssq_s, ssq_t = kernel_call(sums_kernel, "sums", shapes(*[((rows, 1), F32)] * 2), 2)(
        student, teacher
    )
    *near, inv_s, inv_t = kernel_call(
        pack_own_kernel,
        "pack_own",
        shapes(*[((rows, half + ts), BF16)] * SIZE, *[((rows, 1), F32)] * 2),
        6,
    )(student, s_far, teacher, t_far, ssq_s, ssq_t)
    norm_own = near[0][:, :half]

    def exchanged(own, sent, axis_of_core, sign=1):
        arrived = {by: shifted(sent(by), axis_of_core, sign * by) for by in ORDER}
        return [own] + [arrived[by] for by in (1, 2, 3)]

    def added(total, sent, axis_of_core, sign=1, order=SUM):
        arrived = exchanged(None, sent, axis_of_core, sign)
        for by in order:
            total = total + arrived[by].astype(F32)
        return total

    near = exchanged(near[0], near.__getitem__, GATHER)
    far = kernel_call(
        pack_far_kernel, "pack_far", shapes(*[((rows, feats), BF16)] * SIZE), 4
    )(s_far, t_far, inv_s, inv_t)
    far = exchanged(far[0], far.__getitem__, GATHER)

    blocks = shapes(((ss, feats), F32), *[((ss, feats), BF16)] * 3)

    def operands(count):
        return [pltpu.VMEM((count * rows, half), BF16), pltpu.VMEM((count * rows, feats), BF16)]

    first = [by for by in range(SIZE) if by != LAST]
    early = kernel_call(
        functools.partial(gram_early_kernel, level * SIZE / groups),
        "gram_early",
        shapes(((half, feats), F32)),
        3,
        operands(3),
        flops,
    )(*[near[by] for by in first])[0]
    near_blocks = kernel_call(
        gram_native_kernel, "gram_native", blocks, 2, operands(1), flops // 4
    )(near[LAST], early)
    early = kernel_call(
        gram_far_early_kernel, "gram_far_early", shapes(((half, feats), F32)), 6, operands(3), flops
    )(*[near[by] for by in first], *[far[by] for by in first])[0]
    far_blocks = kernel_call(
        gram_far_kernel, "gram_far", blocks, 3, operands(1), flops // 4
    )(near[LAST], far[LAST], early)

    def weights_of(chunk, own, *sends):
        total = added(own, lambda by: sends[by - 1], FIRST[chunk])
        shared = total.astype(BF16)
        piece = added(total, lambda by: shared, SECOND[chunk]).astype(BF16)
        return exchanged(piece, lambda by: piece, FIRST[chunk])

    near_weights = weights_of(0, *near_blocks)
    far_weights = weights_of(1, *far_blocks)

    sofar = kernel_call(
        apply_native_kernel,
        "apply_native",
        shapes(((SIZE * rows, half), F32)),
        2 * SIZE,
        [pltpu.VMEM((SIZE * rows, feats), BF16), pltpu.VMEM((half, feats), BF16)],
        flops,
    )(*near, *near_weights)[0]
    messages = shapes(*[((rows, half), BF16)] * 3)
    weights = pltpu.VMEM((half, feats), BF16)
    *most, stacked = kernel_call(
        apply_early_kernel,
        "apply_early",
        messages + shapes(((3 * rows, feats), BF16)),
        7,
        [weights],
        flops * 3 // 4,
    )(*far[1:], *[far_weights[by] for by in range(SIZE) if by != LAST], sofar)
    parts = kernel_call(
        apply_sent_kernel,
        "apply_sent",
        messages,
        6,
        (),
        flops // 4,
    )(stacked, far_weights[LAST], sofar, *most)
    grad_n = kernel_call(
        apply_kept_kernel, "apply_kept", shapes(((rows, half), F32)), SIZE + 2, [weights], flops // 4
    )(far[0], *far_weights, sofar)[0]
    norm_f = norm_own.astype(F32)
    grad_n = grad_n + level * norm_f
    grad_n = coef * added(grad_n, lambda by: parts[by - 1], GATHER, -1, BACK)
    inner = jnp.sum(grad_n * norm_f, axis=1)
    inner = inner + other_core(inner)
    return (grad_n - inner[:, None] * norm_f) * inv_s


def solution(mesh):
    placed = (P(("loop", "rep"), "sec"), P(("loop", "rep"), "sec"))
    return jax.shard_map(
        body, mesh=mesh, in_specs=placed, out_specs=P(("loop", "rep"), "sec"), check_vma=False
    )
```

```python
import functools
import itertools

import jax
import jax.numpy as jnp
from jax import lax
from jax.experimental import pallas as pl
from jax.experimental.pallas import tpu as pltpu
from jax.sharding import PartitionSpec as P

AXES = ("loop", "rep", "sec")
X, Y, Z = 0, 1, 2
SIZE = 4
GATHER = (Y, X)
FIRST = ((X, Z), (Z, Z))
SECOND = ((Z, Y), (X, Y))
ORDER = (2, 1, 3)
SUM = (1, 3, 2)
BACK = (1, 2, 3)
LAST = 3
STRIP = 32
PARAMS = pltpu.CompilerParams(vmem_limit_bytes=40 * 1024 * 1024)
WHOLE = pl.BlockSpec(memory_space=pltpu.VMEM)
BF16, F32 = jnp.bfloat16, jnp.float32


def index_of(chip, core):
    x, y, z = chip
    return (((x // 2) * SIZE + z) * 8 + y * 2 + x % 2) * 2 + core


def shifted(array, axis_of_core, by):
    pairs = []
    for chip in itertools.product(range(SIZE), repeat=3):
        for core in range(2):
            target = list(chip)
            axis = axis_of_core[core]
            target[axis] = (target[axis] + by) % SIZE
            pairs.append((index_of(chip, core), index_of(target, core)))
    return lax.ppermute(array, AXES, pairs)


def other_core(array):
    return lax.ppermute(array, "sec", [(0, 1), (1, 0)])


def places_here():
    loop, rep, core = (lax.axis_index(name) for name in AXES)
    chip = (lax.div(loop, SIZE) * 2 + lax.rem(rep, 2), lax.div(rep, 2), lax.rem(loop, SIZE))
    return [jnp.where(core == 0, chip[axes[0]], chip[axes[1]]) for axes in (GATHER, *FIRST)]


def scaled(piece, inv):
    return (piece.astype(F32) * inv).astype(BF16)


def part(places, by, size):
    return pl.ds(pl.multiple_of(lax.rem(places[0] + by, SIZE) * size, size), size)


def squares(values):
    values = values.astype(F32)
    return jnp.sum(values * values, axis=1, keepdims=True)


def strips(rows):
    return [pl.ds(start, STRIP) for start in range(0, rows, STRIP)]


def sums_kernel(s_own, t_own, ssq_s, ssq_t):
    for at in strips(s_own.shape[0]):
        ssq_s[at, :] = squares(s_own[at, :])
        ssq_t[at, :] = squares(t_own[at, :])


def pack_own_kernel(s_own, s_far, t_own, t_far, ssq_s, ssq_t, *outs):
    places = places_here()
    rows, half = s_own.shape
    ts = t_own.shape[1] // SIZE
    inv_s, inv_t = outs[SIZE:]
    for at in strips(rows):
        inv_s[at, :] = lax.rsqrt(ssq_s[at, :] + squares(s_far[at, :]) + 1e-06)
        inv_t[at, :] = lax.rsqrt(ssq_t[at, :] + squares(t_far[at, :]) + 1e-06)
    for at in strips(rows):
        norm = scaled(s_own[at, :], inv_s[at, :])
        for by in range(SIZE):
            outs[by][at, pl.ds(0, half)] = norm
            outs[by][at, pl.ds(half, ts)] = scaled(t_own[at, part(places, by, ts)], inv_t[at, :])


def pack_far_kernel(s_far, t_far, inv_s, inv_t, *outs):
    places = places_here()
    rows = s_far.shape[0]
    ss, ts = s_far.shape[1] // SIZE, t_far.shape[1] // SIZE
    for at in strips(rows):
        for by in range(SIZE):
            outs[by][at, pl.ds(0, ss)] = scaled(s_far[at, part(places, by, ss)], inv_s[at, :])
            outs[by][at, pl.ds(ss, ts)] = scaled(t_far[at, part(places, by, ts)], inv_t[at, :])


def native_features(places, pack, half):
    ss = half // SIZE
    return pack[:, part(places, 0, ss)], pack[:, pl.ds(half, pack.shape[1] - half)]


def stack(places, chunk, norms, packs, left, right):
    native = chunk == 0
    rows = norms[0].shape[0]
    half, feats = left.shape[1], right.shape[1]
    ss = half // SIZE
    for k, (norm, pack) in enumerate(zip(norms, packs)):
        at = pl.ds(k * rows, rows)
        for by in range(SIZE):
            which = lax.rem(places[1 + chunk] + by, SIZE)
            block = pl.ds(pl.multiple_of(which * ss, ss), ss)
            left[at, pl.ds(by * ss, ss)] = norm[:, block]
        if native:
            right[at, pl.ds(0, ss)], right[at, pl.ds(ss, feats - ss)] = native_features(
                places, pack, half
            )
        else:
            right[at, :] = pack[...]


def cross(left, right):
    return lax.dot_general(
        left[...], right[...], (((0,), (0,)), ((), ())), preferred_element_type=F32
    )


def emit(product, outs):
    half, feats = product.shape
    ss = half // SIZE
    for by, out in enumerate(outs):
        rows = product[by * ss : (by + 1) * ss]
        out[:, pl.ds(0, ss)] = rows[:, :ss].astype(out.dtype)
        out[:, pl.ds(ss, feats - ss)] = -rows[:, ss:].astype(out.dtype)


def gram_early_kernel(share, *refs):
    places = places_here()
    packs, (product, left, right) = refs[:-3], refs[-3:]
    stack(places, 0, packs, packs, left, right)
    product[...] = cross(left, right)
    ss = product.shape[0] // SIZE
    row = lax.broadcasted_iota(jnp.int32, (ss, ss), 0)
    col = lax.broadcasted_iota(jnp.int32, (ss, ss), 1)
    by = lax.rem(places[0] + SIZE - places[1], SIZE)
    block = pl.ds(pl.multiple_of(by * ss, ss), ss)
    product[block, pl.ds(0, ss)] -= jnp.where(row == col, share, 0.0)


def gram_native_kernel(pack, before, *refs):
    places = places_here()
    outs, (left, right) = refs[:SIZE], refs[SIZE:]
    stack(places, 0, [pack], [pack], left, right)
    emit(before[...] + cross(left, right), outs)


def gram_far_early_kernel(*refs):
    places = places_here()
    count = len(refs) // 2 - 1
    product, left, right = refs[2 * count :]
    stack(places, 1, refs[:count], refs[count : 2 * count], left, right)
    product[...] = cross(left, right)


def gram_far_kernel(norm, pack, before, *refs):
    places = places_here()
    outs, (left, right) = refs[:SIZE], refs[SIZE:]
    stack(places, 1, [norm], [pack], left, right)
    emit(before[...] + cross(left, right), outs)


def gather_weights(place, pieces, weights):
    ss = pieces[0].shape[0]
    for by, piece in enumerate(pieces):
        which = lax.rem(place + SIZE - by, SIZE)
        weights[pl.ds(pl.multiple_of(which * ss, ss), ss), :] = piece[...]


def times(left, weights):
    return lax.dot_general(left, weights, (((1,), (1,)), ((), ())), preferred_element_type=F32)


def apply_native_kernel(*refs):
    places = places_here()
    packs, pieces, (out, left, weights) = refs[:SIZE], refs[SIZE : 2 * SIZE], refs[2 * SIZE :]
    half, feats = weights.shape
    rows, ss = packs[0].shape[0], half // SIZE
    gather_weights(places[1], pieces, weights)
    for k, pack in enumerate(packs):
        at = pl.ds(k * rows, rows)
        left[at, pl.ds(0, ss)], left[at, pl.ds(ss, feats - ss)] = native_features(
            places, pack, half
        )
    out[...] = times(left[...], weights[...])


def apply_early_kernel(far1, far2, far3, piece0, piece1, piece2, before, *refs):
    places = places_here()
    outs, (left, weights) = refs[: SIZE - 1], refs[SIZE - 1 :]
    rows = far1.shape[0]
    pieces = [piece0, piece1, piece2]
    pieces.insert(LAST, jnp.zeros(piece0.shape, piece0.dtype))
    gather_weights(places[2], pieces, weights)
    for k, pack in enumerate((far1, far2, far3)):
        left[pl.ds(k * rows, rows), :] = pack[...]
    product = times(left[...], weights[...])
    for k, out in enumerate(outs):
        sofar = before[pl.ds((k + 1) * rows, rows), :]
        out[...] = (product[k * rows : (k + 1) * rows] + sofar).astype(out.dtype)


def apply_sent_kernel(left, piece, before, early1, early2, early3, *outs):
    places = places_here()
    rows, ss = outs[0].shape[0], piece.shape[0]
    which = lax.rem(places[2] + SIZE - LAST, SIZE)
    block = pl.ds(pl.multiple_of(which * ss, ss), ss)
    product = times(left[...], piece[...])
    for k, (early, out) in enumerate(zip((early1, early2, early3), outs)):
        out[...] = early[...]
        sofar = before[pl.ds((k + 1) * rows, rows), block]
        out[:, block] = (product[k * rows : (k + 1) * rows] + sofar).astype(out.dtype)


def apply_kept_kernel(level, pack, norm, *refs):
    places = places_here()
    pieces, (before, out, weights) = refs[:SIZE], refs[SIZE:]
    gather_weights(places[2], pieces, weights)
    kept = before[pl.ds(0, pack.shape[0]), :] + level * norm[:, pl.ds(0, out.shape[1])].astype(F32)
    out[...] = times(pack[...], weights[...]) + kept


def shapes(*described):
    return [jax.ShapeDtypeStruct(shape, dtype) for shape, dtype in described]


def kernel_call(kernel, name, outs, n_in, scratch=(), flops=0):
    return pl.pallas_call(
        kernel,
        out_shape=outs,
        in_specs=[WHOLE] * n_in,
        out_specs=[WHOLE] * len(outs),
        scratch_shapes=list(scratch),
        compiler_params=PARAMS,
        cost_estimate=pl.CostEstimate(flops=flops, bytes_accessed=4 << 20, transcendentals=0),
        name=name,
    )


def body(student, teacher):
    rows, half = student.shape
    wide = teacher.shape[1]
    width = 2 * half
    groups = lax.axis_size("loop") * lax.axis_size("rep")
    passages = rows * groups
    coef = 32.0 * width / (passages**0.5)
    level = passages / width
    ss, ts = half // SIZE, wide // SIZE
    feats = ss + ts
    flops = 2 * SIZE * rows * half * feats

    t_far, s_far = other_core(teacher), other_core(student)
    ssq_s, ssq_t = kernel_call(sums_kernel, "sums", shapes(*[((rows, 1), F32)] * 2), 2)(
        student, teacher
    )
    *near, inv_s, inv_t = kernel_call(
        pack_own_kernel,
        "pack_own",
        shapes(*[((rows, half + ts), BF16)] * SIZE, *[((rows, 1), F32)] * 2),
        6,
    )(student, s_far, teacher, t_far, ssq_s, ssq_t)
    norm_own = near[0][:, :half]

    def exchanged(own, sent, axis_of_core, sign=1):
        arrived = {by: shifted(sent(by), axis_of_core, sign * by) for by in ORDER}
        return [own] + [arrived[by] for by in (1, 2, 3)]

    def added(total, sent, axis_of_core, sign=1, order=SUM):
        arrived = exchanged(None, sent, axis_of_core, sign)
        for by in order:
            total = total + arrived[by].astype(F32)
        return total

    near = exchanged(near[0], near.__getitem__, GATHER)
    far = kernel_call(
        pack_far_kernel, "pack_far", shapes(*[((rows, feats), BF16)] * SIZE), 4
    )(s_far, t_far, inv_s, inv_t)
    far = exchanged(far[0], far.__getitem__, GATHER)

    blocks = shapes(((ss, feats), F32), *[((ss, feats), BF16)] * 3)

    def operands(count):
        return [pltpu.VMEM((count * rows, half), BF16), pltpu.VMEM((count * rows, feats), BF16)]

    first = [by for by in range(SIZE) if by != LAST]
    early = kernel_call(
        functools.partial(gram_early_kernel, level * SIZE / groups),
        "gram_early",
        shapes(((half, feats), F32)),
        3,
        operands(3),
        flops,
    )(*[near[by] for by in first])[0]
    near_blocks = kernel_call(
        gram_native_kernel, "gram_native", blocks, 2, operands(1), flops // 4
    )(near[LAST], early)
    early = kernel_call(
        gram_far_early_kernel, "gram_far_early", shapes(((half, feats), F32)), 6, operands(3), flops
    )(*[near[by] for by in first], *[far[by] for by in first])[0]
    far_blocks = kernel_call(
        gram_far_kernel, "gram_far", blocks, 3, operands(1), flops // 4
    )(near[LAST], far[LAST], early)

    def weights_of(chunk, own, *sends):
        total = added(own, lambda by: sends[by - 1], FIRST[chunk])
        shared = total.astype(BF16)
        piece = added(total, lambda by: shared, SECOND[chunk]).astype(BF16)
        return exchanged(piece, lambda by: piece, FIRST[chunk])

    near_weights = weights_of(0, *near_blocks)
    far_weights = weights_of(1, *far_blocks)

    sofar = kernel_call(
        apply_native_kernel,
        "apply_native",
        shapes(((SIZE * rows, half), F32)),
        2 * SIZE,
        [pltpu.VMEM((SIZE * rows, feats), BF16), pltpu.VMEM((half, feats), BF16)],
        flops,
    )(*near, *near_weights)[0]
    messages = shapes(*[((rows, half), BF16)] * 3)
    weights = pltpu.VMEM((half, feats), BF16)
    *most, stacked = kernel_call(
        apply_early_kernel,
        "apply_early",
        messages + shapes(((3 * rows, feats), BF16)),
        7,
        [weights],
        flops * 3 // 4,
    )(*far[1:], *[far_weights[by] for by in range(SIZE) if by != LAST], sofar)
    parts = kernel_call(
        apply_sent_kernel,
        "apply_sent",
        messages,
        6,
        (),
        flops // 4,
    )(stacked, far_weights[LAST], sofar, *most)
    grad_n = kernel_call(
        functools.partial(apply_kept_kernel, level),
        "apply_kept",
        shapes(((rows, half), F32)),
        SIZE + 3,
        [weights],
        flops // 4,
    )(far[0], near[0], *far_weights, sofar)[0]
    norm_f = norm_own.astype(F32)
    grad_n = coef * added(grad_n, lambda by: parts[by - 1], GATHER, -1, BACK)
    inner = jnp.sum(grad_n * norm_f, axis=1)
    inner = inner + other_core(inner)
    return (grad_n - inner[:, None] * norm_f) * inv_s


def solution(mesh):
    placed = (P(("loop", "rep"), "sec"), P(("loop", "rep"), "sec"))
    return jax.shard_map(
        body, mesh=mesh, in_specs=placed, out_specs=P(("loop", "rep"), "sec"), check_vma=False
    )
```
